32 devices in a mesh: windows: 2 (over x), tiles: 16 (over z, y, core).
Axes of the slice: x: 2, y: 2, z: 4, core: 2. Of those that a mesh axis runs over, the one named last changes fastest.
Arguments:
- data: bfloat16 [16, 2, 2048, 128], P('windows', None, 'tiles'), parts along dimension 0, may hold values from -6 to 6
- wavelet: float32 [8, 2], replicated, may hold values from -4 to 4
- panel_block: int32 [1], replicated, may hold values from 0 to 15
- tiles: bfloat16 [512, 2, 128, 128], P(('windows', 'tiles')), parts along dimension 0, may hold values from -0.25 to 0.25
- cover_rows: int32 [512], P(('windows', 'tiles')), parts along dimension 0, may hold values from 0 to 15, as said below
- cover_freqs: int32 [512], P(('windows', 'tiles')), parts along dimension 0, may hold values from 0 to 7
Outputs:
- residual: float32 [16, 2, 2048, 128], P('windows', None, 'tiles'), parts along dimension 0
- gradient: bfloat16 [512, 2, 128, 128], P(('windows', 'tiles')), parts along dimension 0
The draws below stay inside these ranges and needn't reach their ends.
There are 2 independent parts, one for each index of `windows`. The reference program is written for one: setup_inputs(seed, part) draws one part's arguments, and reference() takes and returns one part's arrays. A program takes and returns all parts, laid end to end along the dimension named above; an argument that names none is the same for every part. Nothing has to cross between parts.
Inputs may be any that keep to these rules, and one draw needn't show every extreme that they name: `cover_rows`: among the 16 entries of one column block no row block appears more than 2 times, exactly 12 distinct row blocks appear, one row block appears 2 times in every column block, and together with cover_freqs the entries of one column block name distinct (row block, frequency) pairs.
All inputs are finite; a program needn't handle non-finite values.
Results may differ from the reference program's by a relative error of at most 0.0053.
Values may be sent and summed in bfloat16 or wider, within the bound.
No kernel may reach another device: no remote copies, remote signals or barrier semaphores. Data moves between devices by JAX's collectives and lax.ppermute only.
A program may use at most 128 MiB of HBM per device.

```python
import jax
import jax.numpy as jnp
from jax import lax

BLOCK = 128
PS = 128
FREQ = 8
SLOTS = 16
NR = 2048
TILES_ALL = 256
N_TILES = 16


def coverage_lists(key):
    hottest = jax.random.randint(jax.random.fold_in(key, 11), (), 0, N_TILES)
    column_keys = jax.random.split(jax.random.fold_in(key, 12), N_TILES)
    used = 3 * N_TILES // 4
    twice = N_TILES // 4

    def one_column(column_key):
        key_rank, key_start, key_second, key_order = jax.random.split(column_key, 4)
        blocks = jnp.arange(N_TILES, dtype=jnp.int32)
        ranking = jax.random.permutation(key_rank, N_TILES).astype(jnp.int32)
        ranking = jnp.where(blocks == N_TILES - 1, -1, ranking)
        ranking = jnp.where(blocks == hottest, -2, ranking)
        ordering = jnp.argsort(ranking, stable=True).astype(jnp.int32)
        rows = jnp.concatenate([ordering[:used], ordering[:twice]])
        offset = jax.random.randint(key_start, (), 0, FREQ)
        first_freqs = (offset + jnp.arange(used, dtype=jnp.int32)) % FREQ
        shifts = jax.random.randint(key_second, (twice,), 0, FREQ - 1)
        second_freqs = (first_freqs[:twice] + 1 + shifts) % FREQ
        freqs = jnp.concatenate([first_freqs, second_freqs])
        shuffle = jax.random.permutation(key_order, N_TILES)
        return (rows[shuffle], freqs[shuffle])
    rows, freqs = jax.vmap(one_column)(column_keys)
    return (rows.reshape(-1).astype(jnp.int32), freqs.reshape(-1).astype(jnp.int32))


def draw_cover_rows(key, part):
    return coverage_lists(key)[0]


def draw_cover_freqs(key, part):
    return coverage_lists(key)[1]


def block_levels(stream_key, extent, cuts, smallest, largest):
    factor_of, own = 1.0, jax.random.fold_in(stream_key, 6)
    for axis_at, blocks in cuts:
        steps = jnp.exp(jax.random.uniform(jax.random.fold_in(own, axis_at), (blocks,), jnp.float32, smallest / len(cuts), largest / len(cuts)))
        factor_of = factor_of * jnp.repeat(steps, extent[axis_at] // blocks).reshape([-1 if axis == axis_at else 1 for axis in range(len(extent))])
    return factor_of


def normal_values(key, dims, spread, limit, cuts=(), kind=jnp.bfloat16):
    result = spread * jax.random.normal(key, dims, jnp.float32)
    if cuts:
        result = result * block_levels(key, dims, cuts, -0.22, 0.18)
    return jnp.clip(result, -limit, limit).astype(kind)


def setup_inputs(seed: int = 0, part: int = 0) -> dict:
    seeds = jax.random.split(jax.random.key(seed), 7)
    part_keys = jax.random.split(jax.random.fold_in(seeds[6], part), 7)
    data = normal_values(part_keys[0], (FREQ, 2, NR, PS), 1.0, 6.0, ((2, 16),))
    wavelet = normal_values(seeds[1], (FREQ, 2), 1.0, 4.0, (), jnp.float32)
    panel_block = jax.random.randint(seeds[2], (1,), 0, N_TILES).astype(jnp.int32)
    tiles = normal_values(part_keys[3], (TILES_ALL, 2, BLOCK, BLOCK), (2 * BLOCK * N_TILES // FREQ) ** -0.5, 0.25, ((0, 16),))
    cover_rows = draw_cover_rows(jax.random.fold_in(jax.random.fold_in(seeds[6], part), 71), part)
    cover_freqs = draw_cover_freqs(jax.random.fold_in(jax.random.fold_in(seeds[6], part), 71), part)
    return dict(data=data, wavelet=wavelet, panel_block=panel_block, tiles=tiles, cover_rows=cover_rows, cover_freqs=cover_freqs)


def complex_product(left, right):
    left = left.astype(jnp.float32)
    right = right.astype(jnp.float32)

    def product(first, second):
        return jnp.einsum("sab,sbp->sap", first, second)

    real_part = product(left[:, 0], right[:, 0]) - product(left[:, 1], right[:, 1])
    imag_part = product(left[:, 0], right[:, 1]) + product(left[:, 1], right[:, 0])
    return jnp.stack([real_part, imag_part], axis=1)


def shot_gradient(rows_res, rows_src):
    rows_res = rows_res.astype(jnp.float32)
    rows_src = rows_src.astype(jnp.float32)
    scale = 1.0 / PS

    def outer(first, second):
        return jnp.einsum("kap,kbp->kab", first, second)

    real_part = -(outer(rows_res[:, 0], rows_src[:, 0]) + outer(rows_res[:, 1], rows_src[:, 1])) * scale
    imag_part = -(outer(rows_res[:, 1], rows_src[:, 0]) - outer(rows_res[:, 0], rows_src[:, 1])) * scale
    return jnp.stack([real_part, imag_part], axis=1).astype(jnp.bfloat16)


def reference(data, wavelet, panel_block, tiles, cover_rows, cover_freqs):
    row_ids = jnp.arange(BLOCK * N_TILES, dtype=jnp.int32)[:, None]
    col_ids = jnp.arange(PS, dtype=jnp.int32)[None, :]
    identity = (row_ids - panel_block[0] * BLOCK == col_ids).astype(jnp.float32)
    source_re = -data[:, 0].astype(jnp.float32) + wavelet[:, 0, None, None] * identity
    source_im = -data[:, 1].astype(jnp.float32) + wavelet[:, 1, None, None] * identity
    source = jnp.stack([source_re, source_im], axis=1).astype(jnp.bfloat16)
    source_cols = source.reshape(FREQ, 2, N_TILES, BLOCK, PS).transpose(2, 0, 1, 3, 4)
    tile_cols = tiles.reshape(N_TILES, SLOTS, 2, BLOCK, BLOCK)
    row_cols = cover_rows.reshape(N_TILES, SLOTS)
    freq_cols = cover_freqs.reshape(N_TILES, SLOTS)

    def forward(total, column):
        tile_set, rows, freqs, column_src = column
        parts = complex_product(tile_set, column_src[freqs]).astype(jnp.bfloat16)
        return total.at[freqs, rows].add(parts.astype(jnp.float32)), None

    start = jnp.zeros((FREQ, N_TILES, 2, BLOCK, PS), jnp.float32)
    total, _ = lax.scan(forward, start, (tile_cols, row_cols, freq_cols, source_cols))
    predicted = total.transpose(0, 2, 1, 3, 4).reshape(FREQ, 2, N_TILES * BLOCK, PS)
    residual = data.astype(jnp.float32) - predicted
    res_blocks = residual.astype(jnp.bfloat16).reshape(FREQ, 2, N_TILES, BLOCK, PS).transpose(0, 2, 1, 3, 4)

    def backward(carry, column):
        rows, freqs, column_src = column
        return carry, shot_gradient(res_blocks[freqs, rows], column_src[freqs])

    _, grads = lax.scan(backward, jnp.zeros((), jnp.float32), (row_cols, freq_cols, source_cols))
    return residual, grads.reshape(N_TILES * SLOTS, 2, BLOCK, BLOCK)
```

```python
import functools

import jax
import jax.numpy as jnp
from jax import lax
from jax.experimental import pallas as pl
from jax.experimental.pallas import tpu as pltpu
from jax.sharding import PartitionSpec as P

GROUP = 8
CHUNKS = 2
BF16 = jnp.bfloat16
F32 = jnp.float32
VMEM = pl.BlockSpec(memory_space=pltpu.VMEM)
SMEM = pl.BlockSpec(memory_space=pltpu.SMEM)


def call(kernel, name, out_shape, scratch=(), specs=None, flops=0, moved=1 << 20):
    return pl.pallas_call(
        kernel,
        name=name,
        out_shape=out_shape,
        in_specs=specs,
        out_specs=jax.tree.map(lambda _: VMEM, out_shape),
        scratch_shapes=list(scratch),
        cost_estimate=pl.CostEstimate(flops=flops, bytes_accessed=moved, transcendentals=0),
        compiler_params=pltpu.CompilerParams(vmem_limit_bytes=40 * 1024 * 1024),
    )


def local_index():
    return lax.rem(lax.axis_index("tiles"), GROUP)


def group_index():
    return lax.div(lax.axis_index("tiles"), GROUP)


def pack(real, imag):
    return jnp.concatenate([real, imag], axis=0).astype(BF16)


def slices_kernel(data, rows, freqs, *outs):
    outs, wide = outs[:-1], outs[-1]
    wide[...] = data[...].astype(F32)
    local = local_index()
    freq_count, _, block, shots = data.shape
    chunk = block // CHUNKS
    piece = chunk // GROUP
    slots = rows.shape[0]
    for k in range(GROUP):
        start = (local ^ k) * piece
        for c in range(CHUNKS):
            at = pl.ds(pl.multiple_of(c * chunk + start, piece), piece)
            for f in range(freq_count):
                outs[k][c * freq_count + f] = pack(wide[f, 0, at, :], wide[f, 1, at, :])
    lists = jnp.zeros((2 * slots, shots), F32)
    line = lax.broadcasted_iota(jnp.int32, (2 * slots, shots), 0)

    def put(t, lists):
        lists = jnp.where(line == t, rows[t].astype(F32), lists)
        return jnp.where(line == slots + t, freqs[t].astype(F32), lists)

    lists = lax.fori_loop(0, slots, put, lists)
    height = 2 * piece
    for b in range(2 * slots // height):
        for k in range(GROUP):
            outs[k][CHUNKS * freq_count + b] = lists[b * height : (b + 1) * height].astype(BF16)


def parts_kernel(data, wavelet, panel, tiles, freqs, source, *outs_scratch):
    outs, product = outs_scratch[:-1], outs_scratch[-1]
    local = local_index()
    freq_count, _, block, shots = data.shape
    chunk = block // CHUNKS
    piece = chunk // GROUP
    at_panel = (lax.axis_index("tiles") == panel[0]).astype(F32)
    identity = (
        lax.broadcasted_iota(jnp.int32, (block, shots), 0)
        == lax.broadcasted_iota(jnp.int32, (block, shots), 1)
    ).astype(F32) * at_panel
    for f in range(freq_count):
        real = -data[f, 0].astype(F32) + wavelet[f, 0] * identity
        imag = -data[f, 1].astype(F32) + wavelet[f, 1] * identity
        source[f, :block, :shots] = real.astype(BF16)
        source[f, :block, shots:] = imag.astype(BF16)
        source[f, block:, :shots] = (-imag).astype(BF16)
        source[f, block:, shots:] = real.astype(BF16)

    def one(t, carry):
        left = jnp.concatenate([tiles[t, 0], tiles[t, 1]], axis=1)
        product[...] = jnp.dot(left, source[freqs[t]], preferred_element_type=F32)
        for c in range(CHUNKS):
            for k in range(GROUP):
                at = pl.ds(pl.multiple_of(c * chunk + (local ^ k) * piece, piece), piece)
                outs[c * GROUP + k][t] = pack(product[at, :shots], product[at, shots:])
        return carry

    lax.fori_loop(0, tiles.shape[0], one, 0)


def combine_kernel(freq_count, index, *refs):
    parts, own, sends, total = refs[:GROUP], refs[GROUP], refs[GROUP + 1 : -1], refs[-1]
    slots = parts[0].shape[0]
    group = group_index()
    span = GROUP * freq_count

    total[...] = jnp.zeros_like(total)
    for k in range(GROUP):

        def add(t, carry, k=k):
            at = index[k, t]
            total[at] += parts[k][t].astype(F32)
            return carry

        lax.fori_loop(0, slots, add, 0, unroll=4)
    own[...] = total[pl.ds(group * span, span)]
    for q, send in enumerate(sends, 1):
        send[...] = total[pl.ds((group ^ q) * span, span)].astype(BF16)


def residual_kernel(freq_count, at_chunk, own, *refs):
    count = len(refs) - 2 * GROUP - 1
    got, data = refs[:count], refs[count : count + GROUP]
    rounded, back = refs[count + GROUP], refs[count + GROUP + 1 :]
    local = local_index()
    for k in range(GROUP):
        at = pl.ds((local ^ k) * freq_count, freq_count)
        predicted = own[at]
        for ref in got:
            predicted += ref[at].astype(F32)
        values = data[k][at_chunk * freq_count : (at_chunk + 1) * freq_count].astype(F32)
        rounded[at] = (values - predicted).astype(BF16)
        back[k][...] = predicted.astype(BF16)


def spread_kernel(freq_count, index, *refs):
    outs, table = refs[-GROUP - 1 : -1], refs[-1]
    have = refs[: -GROUP - 1]
    group = group_index()
    span = GROUP * freq_count
    for q, ref in enumerate(have):
        table[pl.ds((group ^ q) * span, span)] = ref[...]
    for k in range(GROUP):

        def take(t, carry, k=k):
            outs[k][t] = table[index[k, t]]
            return carry

        lax.fori_loop(0, outs[0].shape[0], take, 0, unroll=4)


def gradient_kernel(data, source, freqs, *refs):
    slices, back = refs[: CHUNKS * GROUP], refs[CHUNKS * GROUP : 2 * CHUNKS * GROUP]
    residual, gradient, left = refs[2 * CHUNKS * GROUP :]
    local = local_index()
    freq_count, _, block, shots = data.shape
    chunk = block // CHUNKS
    piece = chunk // GROUP
    scale = 1.0 / shots
    residual[...] = data[...].astype(F32)
    for c in range(CHUNKS):
        for k in range(GROUP):
            at = pl.ds(pl.multiple_of(c * chunk + (local ^ k) * piece, piece), piece)
            for f in range(freq_count):
                predicted = back[c * GROUP + k][f].astype(F32)
                residual[f, 0, at, :] -= predicted[:piece]
                residual[f, 1, at, :] -= predicted[piece:]

    def one(t, carry):
        for c in range(CHUNKS):
            for k in range(GROUP):
                at = pl.ds(pl.multiple_of(c * chunk + (local ^ k) * piece, piece), piece)
                values = slices[c * GROUP + k][t].astype(F32)
                left[at, :shots] = values[:piece]
                left[at, shots:] = values[piece:]
        total = lax.dot_general(
            left[...].astype(BF16),
            source[freqs[t]],
            (((1,), (1,)), ((), ())),
            preferred_element_type=F32,
        )
        total = (-total * scale).astype(BF16)
        gradient[t, 0] = total[:, :block]
        gradient[t, 1] = total[:, block:]
        return carry

    lax.fori_loop(0, gradient.shape[0], one, 0)


def per_device(data, wavelet, panel_block, tiles, cover_rows, cover_freqs):
    freq_count, _, block, shots = data.shape
    slots = tiles.shape[0]
    peers = lax.axis_size("tiles")
    groups = peers // GROUP
    height = 2 * block // (CHUNKS * GROUP)
    span = GROUP * freq_count

    def shape(count, kind=BF16):
        return jax.ShapeDtypeStruct((count, height, shots), kind)

    def swap(value, distance):
        pairs = [(i, i ^ distance) for i in range(peers)]
        return lax.ppermute(value, "tiles", pairs)

    def exchange(values):
        got = {k: swap(values[k], k) for k in (6, 4, 7, 5, 2, 3, 1)}
        got[0] = values[0]
        return [got[k] for k in range(GROUP)]

    def across(values):
        return [swap(value, (q + 1) * GROUP) for q, value in enumerate(values)]

    lists = 2 * slots // height
    data_out = call(
        slices_kernel,
        "data_slices",
        [shape(CHUNKS * freq_count + lists)] * GROUP,
        scratch=[pltpu.VMEM(data.shape, F32)],
        specs=[VMEM, SMEM, SMEM],
    )(data, cover_rows, cover_freqs)
    data_in = exchange(data_out)

    source, *parts = call(
        parts_kernel,
        "parts",
        [jax.ShapeDtypeStruct((freq_count, 2 * block, 2 * shots), BF16)]
        + [shape(slots)] * (CHUNKS * GROUP),
        scratch=[pltpu.VMEM((block, 2 * shots), F32)],
        specs=[VMEM, SMEM, SMEM, VMEM, SMEM],
    )(data, wavelet, panel_block, tiles, cover_freqs)

    cover = jnp.stack([x[CHUNKS * freq_count :, :, 0].reshape(2, slots) for x in data_in])
    cover = cover.astype(jnp.int32)
    index = cover[:, 0] * freq_count + cover[:, 1]

    arrived = [exchange(parts[c * GROUP : (c + 1) * GROUP]) for c in range(CHUNKS)]
    sums = []
    for c in range(CHUNKS):
        own, *sends = call(
            functools.partial(combine_kernel, freq_count),
            "combine",
            [shape(span, F32)] + [shape(span)] * (groups - 1),
            scratch=[pltpu.VMEM((peers * freq_count, height, shots), F32)],
            specs=[SMEM] + [VMEM] * GROUP,
        )(index, *arrived[c])
        sums.append((own, across(sends)))
    rounded, back = [], []
    for c in range(CHUNKS):
        own, got = sums[c]
        mine, *predicted = call(
            functools.partial(residual_kernel, freq_count, c),
            "residual_slices",
            [shape(span)] + [shape(freq_count)] * GROUP,
            specs=[VMEM] * (1 + len(got) + GROUP),
        )(own, *got, *data_in)
        rounded.append([mine] + across([mine] * (groups - 1)))
        back.append(predicted)
    slices = []
    for c in range(CHUNKS):
        out = call(
            functools.partial(spread_kernel, freq_count),
            "spread",
            [shape(slots)] * GROUP,
            scratch=[pltpu.VMEM((peers * freq_count, height, shots), BF16)],
            specs=[SMEM] + [VMEM] * groups,
        )(index, *rounded[c])
        slices += exchange(out)
    returned = []
    for c in range(CHUNKS):
        returned += exchange(back[c])
    return call(
        gradient_kernel,
        "gradient",
        [
            jax.ShapeDtypeStruct(data.shape, F32),
            jax.ShapeDtypeStruct(tiles.shape, BF16),
        ],
        scratch=[pltpu.VMEM((block, 2 * shots), F32)],
        specs=[VMEM, VMEM, SMEM] + [VMEM] * (2 * CHUNKS * GROUP),
    )(data, source, cover_freqs, *slices, *returned)


def solution(mesh):
    in_specs = (
        P("windows", None, "tiles", None),
        P(),
        P(),
        P(("windows", "tiles"), None, None, None),
        P(("windows", "tiles")),
        P(("windows", "tiles")),
    )
    out_specs = (P("windows", None, "tiles", None), P(("windows", "tiles"), None, None, None))
    return jax.shard_map(
        lambda *args: tuple(per_device(*args)),
        mesh=mesh,
        in_specs=in_specs,
        out_specs=out_specs,
        check_vma=False,
    )
```

```python
import functools

import jax
import jax.numpy as jnp
from jax import lax
from jax.experimental import pallas as pl
from jax.experimental.pallas import tpu as pltpu
from jax.sharding import PartitionSpec as P

GROUP = 16
BF16 = jnp.bfloat16
F32 = jnp.float32
VMEM = pl.BlockSpec(memory_space=pltpu.VMEM)
SMEM = pl.BlockSpec(memory_space=pltpu.SMEM)
HBM = pl.BlockSpec(memory_space=pltpu.HBM)


def call(kernel, name, out_shape, in_specs, scratch=(), out_specs=None):
    return pl.pallas_call(
        kernel,
        name=name,
        out_shape=out_shape,
        in_specs=in_specs,
        out_specs=out_specs or jax.tree.map(lambda _: VMEM, out_shape),
        scratch_shapes=list(scratch),
        cost_estimate=pl.CostEstimate(flops=0, bytes_accessed=1 << 20, transcendentals=0),
        compiler_params=pltpu.CompilerParams(vmem_limit_bytes=48 * 1024 * 1024),
    )


def pack(real, imag):
    return jnp.concatenate([real, imag], axis=0).astype(BF16)


def parts_kernel(
    data_hbm, wavelet_hbm, panel_hbm, tiles_hbm, rows_hbm, freqs_hbm,
    source, out, data, wavelet, panel, tiles, rows, freqs, sems,
):
    freq_count, _, block, shots = data.shape
    slots = tiles.shape[0]
    height = out.shape[2]
    piece = height // 2
    pairs = (
        (data_hbm, data),
        (tiles_hbm, tiles),
        (wavelet_hbm, wavelet),
        (panel_hbm, panel),
        (freqs_hbm, freqs),
        (rows_hbm, rows),
    )
    copies = [pltpu.make_async_copy(*pair, sems.at[i]) for i, pair in enumerate(pairs)]
    for copy in copies:
        copy.start()
    diagonal = (
        lax.broadcasted_iota(jnp.int32, (block, shots), 0)
        == lax.broadcasted_iota(jnp.int32, (block, shots), 1)
    ).astype(F32)
    for i in (2, 3, 4, 5, 0):
        copies[i].wait()
    identity = diagonal * (lax.axis_index("tiles") == panel[0]).astype(F32)
    lists = slots // height
    for f in range(freq_count):
        real, imag = data[f, 0].astype(F32), data[f, 1].astype(F32)
        source[f, 0] = (wavelet[0, f] * identity - real).astype(BF16)
        source[f, 1] = (wavelet[1, f] * identity - imag).astype(BF16)
        for j in range(GROUP):
            at = slice(j * piece, (j + 1) * piece)
            out[j, slots + lists + f] = pack(real[at], imag[at])
    line = lax.broadcasted_iota(jnp.int32, (height, shots), 0)
    lane = lax.broadcasted_iota(jnp.int32, (height, shots), 1)
    for b in range(lists):
        values = jnp.zeros((height, shots), F32)
        for r in range(height):
            t = b * height + r
            pair = jnp.where(lane < shots // 2, rows[t].astype(F32), freqs[t].astype(F32))
            values = jnp.where(line == r, pair, values)
        for j in range(GROUP):
            out[j, slots + b] = values.astype(BF16)
    copies[1].wait()

    def one(t, carry):
        f = freqs[t]
        left = tiles[t].reshape(2 * block, block)
        right = jnp.concatenate([source[f, 0], source[f, 1]], axis=1)
        product = jnp.dot(left, right, preferred_element_type=F32)
        real = product[:block, :shots] - product[block:, shots:]
        imag = product[:block, shots:] + product[block:, :shots]
        for j in range(GROUP):
            at = slice(j * piece, (j + 1) * piece)
            out[j, t] = pack(real[at], imag[at])
        return carry

    lax.fori_loop(0, slots, one, 0, unroll=4)


def add_parts(freq_count, slots, index, parts, total):
    total[...] = jnp.zeros_like(total)
    for j in range(GROUP):

        def add(t, carry, j=j):
            total[index[j, t]] += parts[j, t].astype(F32)
            return carry

        lax.fori_loop(0, slots, add, 0, unroll=8)


def own_rows(freq_count, slots, got, own, parts, rounded, out):
    first = parts.shape[1] - freq_count
    for j in range(GROUP):
        at = slice(j * freq_count, (j + 1) * freq_count)
        predicted = own[at]
        for ref in got:
            predicted += ref[at].astype(F32)
        rounded[at] = (parts[j, first:].astype(F32) - predicted).astype(BF16)
        out[j, slots:] = predicted.astype(BF16)


def take_rows(slots, index, table, out):
    for j in range(GROUP):

        def take(t, carry, j=j):
            out[j, t] = table[index[j, t]]
            return carry

        lax.fori_loop(0, slots, take, 0, unroll=8)


def whole_kernel(freq_count, slots, index, parts, out, total, table):
    add_parts(freq_count, slots, index, parts, total)
    own_rows(freq_count, slots, (), total, parts, table, out)
    take_rows(slots, index, table, out)


def sum_kernel(freq_count, slots, index, parts, own, *refs):
    sends, total = refs[:-1], refs[-1]
    group = lax.div(lax.axis_index("tiles"), GROUP)
    span = GROUP * freq_count
    add_parts(freq_count, slots, index, parts, total)
    own[...] = total[pl.ds(group * span, span)]
    for q, send in enumerate(sends, 1):
        send[...] = total[pl.ds((group ^ q) * span, span)].astype(BF16)


def residual_kernel(freq_count, slots, own, parts, *refs):
    got, (rounded, back) = refs[:-2], refs[-2:]
    own_rows(freq_count, 0, got, own, parts, rounded, back)


def spread_kernel(freq_count, slots, index, back, *refs):
    have, (out, table) = refs[:-2], refs[-2:]
    group = lax.div(lax.axis_index("tiles"), GROUP)
    span = GROUP * freq_count
    for q, ref in enumerate(have):
        table[pl.ds((group ^ q) * span, span)] = ref[...]
    out[:, slots:] = back[...]
    take_rows(slots, index, table, out)


def gradient_kernel(
    data, source, freqs, arrived, residual_hbm, gradient_hbm, residual, gradient, sems
):
    freq_count, _, block, shots = data.shape
    slots, height = gradient.shape[0], arrived.shape[2]
    piece = height // 2
    scale = 1.0 / shots
    for f in range(freq_count):
        real, imag = data[f, 0].astype(F32), data[f, 1].astype(F32)
        for j in range(GROUP):
            at = slice(j * piece, (j + 1) * piece)
            predicted = arrived[j, slots + f].astype(F32)
            residual[f, 0, at, :] = real[at] - predicted[:piece]
            residual[f, 1, at, :] = imag[at] - predicted[piece:]
    copies = [pltpu.make_async_copy(residual, residual_hbm, sems.at[0])]
    copies[0].start()
    parts = 4
    step = slots // parts

    def one(t, carry):
        left = arrived[:, t].reshape(GROUP * height, shots)
        right = source[freqs[t]].reshape(2 * block, shots)
        total = -scale * lax.dot_general(
            left, right, (((1,), (1,)), ((), ())), preferred_element_type=F32
        )
        real, imag = [], []
        for j in range(GROUP):
            upper = total[j * height : j * height + piece]
            lower = total[j * height + piece : (j + 1) * height]
            real.append(upper[:, :block] + lower[:, block:])
            imag.append(lower[:, :block] - upper[:, block:])
        gradient[t, 0] = jnp.concatenate(real, axis=0).astype(BF16)
        gradient[t, 1] = jnp.concatenate(imag, axis=0).astype(BF16)
        return carry

    for i in range(parts):
        lax.fori_loop(i * step, (i + 1) * step, one, 0, unroll=4)
        at = pl.ds(i * step, step)
        copies.append(
            pltpu.make_async_copy(gradient.at[at], gradient_hbm.at[at], sems.at[i + 1])
        )
        copies[-1].start()
    for copy in copies:
        copy.wait()


def per_device(data, wavelet, panel_block, tiles, cover_rows, cover_freqs):
    freq_count, _, block, shots = data.shape
    slots = tiles.shape[0]
    peers = lax.axis_size("tiles")
    groups = peers // GROUP
    height = 2 * block // GROUP
    span = GROUP * freq_count
    sizes = (freq_count, slots)
    members = [list(range(g * GROUP, (g + 1) * GROUP)) for g in range(groups)]

    def shape(count, kind=BF16):
        return jax.ShapeDtypeStruct((count, height, shots), kind)

    def payload(count):
        return jax.ShapeDtypeStruct((GROUP, count, height, shots), BF16)

    def exchange(value):
        return lax.all_to_all(
            value, "tiles", split_axis=0, concat_axis=0, tiled=True, axis_index_groups=members
        )

    def across(values):
        return [
            lax.ppermute(value, "tiles", [(i, i ^ (q * GROUP)) for i in range(peers)])
            for q, value in enumerate(values, 1)
        ]

    source, sent = call(
        parts_kernel,
        "parts",
        [
            jax.ShapeDtypeStruct(data.shape, BF16),
            payload(slots + slots // height + freq_count),
        ],
        [HBM] * 6,
        scratch=[
            pltpu.VMEM(data.shape, BF16),
            pltpu.SMEM((2, freq_count), F32),
            pltpu.SMEM((1,), jnp.int32),
            pltpu.VMEM(tiles.shape, BF16),
            pltpu.SMEM((slots,), jnp.int32),
            pltpu.SMEM((slots,), jnp.int32),
            pltpu.SemaphoreType.DMA((6,)),
        ],
    )(data, wavelet.T, panel_block, tiles, cover_rows, cover_freqs)
    parts = exchange(sent)
    lists = parts[:, slots:-freq_count].reshape(GROUP, slots, shots).astype(jnp.int32)
    index = lists[:, :, 0] * freq_count + lists[:, :, shots // 2]
    total = pltpu.VMEM((peers * freq_count, height, shots), F32)
    table = pltpu.VMEM((peers * freq_count, height, shots), BF16)
    if groups == 1:
        returns = call(
            functools.partial(whole_kernel, *sizes),
            "residual_slices",
            payload(slots + freq_count),
            [SMEM, VMEM],
            scratch=[total, table],
        )(index, parts)
    else:
        own, *sends = call(
            functools.partial(sum_kernel, *sizes),
            "sums",
            [shape(span, F32)] + [shape(span)] * (groups - 1),
            [SMEM, VMEM],
            scratch=[total],
        )(index, parts)
        mine, back = call(
            functools.partial(residual_kernel, *sizes),
            "residual_slices",
            [shape(span), payload(freq_count)],
            [VMEM] * (1 + groups),
        )(own, parts, *across(sends))
        returns = call(
            functools.partial(spread_kernel, *sizes),
            "spread",
            payload(slots + freq_count),
            [SMEM] + [VMEM] * (1 + groups),
            scratch=[table],
        )(index, back, mine, *across([mine] * (groups - 1)))
    return call(
        gradient_kernel,
        "gradient",
        (jax.ShapeDtypeStruct(data.shape, F32), jax.ShapeDtypeStruct(tiles.shape, BF16)),
        [VMEM, VMEM, SMEM, VMEM],
        out_specs=(HBM, HBM),
        scratch=[
            pltpu.VMEM(data.shape, F32),
            pltpu.VMEM(tiles.shape, BF16),
            pltpu.SemaphoreType.DMA((5,)),
        ],
    )(data, source, cover_freqs, exchange(returns))


def solution(mesh):
    in_specs = (
        P("windows", None, "tiles", None),
        P(),
        P(),
        P(("windows", "tiles"), None, None, None),
        P(("windows", "tiles")),
        P(("windows", "tiles")),
    )
    out_specs = (P("windows", None, "tiles", None), P(("windows", "tiles"), None, None, None))
    return jax.shard_map(
        per_device, mesh=mesh, in_specs=in_specs, out_specs=out_specs, check_vma=False
    )
```

```python
import functools

import jax
import jax.numpy as jnp
from jax import lax
from jax.experimental import pallas as pl
from jax.experimental.pallas import tpu as pltpu
from jax.sharding import PartitionSpec as P

GROUP = 16
BF16 = jnp.bfloat16
F32 = jnp.float32
VMEM = pl.BlockSpec(memory_space=pltpu.VMEM)
SMEM = pl.BlockSpec(memory_space=pltpu.SMEM)
HBM = pl.BlockSpec(memory_space=pltpu.HBM)


def call(kernel, name, out_shape, in_specs, scratch=(), out_specs=None, mib=48):
    return pl.pallas_call(
        kernel,
        name=name,
        out_shape=out_shape,
        in_specs=in_specs,
        out_specs=out_specs or jax.tree.map(lambda _: VMEM, out_shape),
        scratch_shapes=list(scratch),
        cost_estimate=pl.CostEstimate(flops=0, bytes_accessed=1 << 20, transcendentals=0),
        compiler_params=pltpu.CompilerParams(vmem_limit_bytes=mib * 1024 * 1024),
    )


def pack(real, imag):
    return jnp.concatenate([real, imag], axis=0).astype(BF16)


def parts_kernel(
    data_hbm, wavelet_hbm, panel_hbm, tiles_hbm, rows_hbm, freqs_hbm,
    source, out, data, wavelet, panel, tiles, rows, freqs, sems,
):
    freq_count, _, block, shots = data.shape
    slots = tiles.shape[0]
    height = out.shape[2]
    piece = height // 2
    pairs = (
        (data_hbm, data),
        (tiles_hbm, tiles),
        (wavelet_hbm, wavelet),
        (panel_hbm, panel),
        (freqs_hbm, freqs),
        (rows_hbm, rows),
    )
    copies = [pltpu.make_async_copy(*pair, sems.at[i]) for i, pair in enumerate(pairs)]
    for copy in copies:
        copy.start()
    diagonal = (
        lax.broadcasted_iota(jnp.int32, (block, shots), 0)
        == lax.broadcasted_iota(jnp.int32, (block, shots), 1)
    ).astype(F32)
    for i in (2, 3, 4, 5, 0):
        copies[i].wait()
    identity = diagonal * (lax.axis_index("tiles") == panel[0]).astype(F32)
    lists = slots // height
    for f in range(freq_count):
        real, imag = data[f, 0].astype(F32), data[f, 1].astype(F32)
        source[f, 0] = (wavelet[0, f] * identity - real).astype(BF16)
        source[f, 1] = (wavelet[1, f] * identity - imag).astype(BF16)
        for j in range(GROUP):
            at = slice(j * piece, (j + 1) * piece)
            out[j, slots + lists + f] = pack(real[at], imag[at])
    line = lax.broadcasted_iota(jnp.int32, (height, shots), 0)
    lane = lax.broadcasted_iota(jnp.int32, (height, shots), 1)
    for b in range(lists):
        values = jnp.zeros((height, shots), F32)
        for r in range(height):
            t = b * height + r
            pair = jnp.where(lane < shots // 2, rows[t].astype(F32), freqs[t].astype(F32))
            values = jnp.where(line == r, pair, values)
        for j in range(GROUP):
            out[j, slots + b] = values.astype(BF16)
    copies[1].wait()

    def one(t, carry):
        f = freqs[t]
        left = tiles[t].reshape(2 * block, block)
        right = jnp.concatenate([source[f, 0], source[f, 1]], axis=1)
        product = jnp.dot(left, right, preferred_element_type=F32)
        real = product[:block, :shots] - product[block:, shots:]
        imag = product[:block, shots:] + product[block:, :shots]
        for j in range(GROUP):
            at = slice(j * piece, (j + 1) * piece)
            out[j, t] = pack(real[at], imag[at])
        return carry

    lax.fori_loop(0, slots, one, 0, unroll=4)


def add_parts(freq_count, slots, index, parts, total):
    total[...] = jnp.zeros_like(total)
    for j in range(GROUP):

        def add(t, carry, j=j):
            total[index[j, t]] += parts[j, t].astype(F32)
            return carry

        lax.fori_loop(0, slots, add, 0, unroll=8)


def own_rows(freq_count, slots, got, own, parts, rounded, out):
    first = parts.shape[1] - freq_count
    for j in range(GROUP):
        at = slice(j * freq_count, (j + 1) * freq_count)
        predicted = own[at]
        for ref in got:
            predicted += ref[at].astype(F32)
        rounded[at] = (parts[j, first:].astype(F32) - predicted).astype(BF16)
        out[j, slots:] = predicted.astype(BF16)


def take_rows(slots, index, table, out):
    for j in range(GROUP):

        def take(t, carry, j=j):
            out[j, t] = table[index[j, t]]
            return carry

        lax.fori_loop(0, slots, take, 0, unroll=8)


def whole_kernel(freq_count, slots, index, parts, out, total, table):
    add_parts(freq_count, slots, index, parts, total)
    own_rows(freq_count, slots, (), total, parts, table, out)
    take_rows(slots, index, table, out)


def sum_kernel(freq_count, slots, index, parts, own, *refs):
    sends, total = refs[:-1], refs[-1]
    group = lax.div(lax.axis_index("tiles"), GROUP)
    span = GROUP * freq_count
    add_parts(freq_count, slots, index, parts, total)
    own[...] = total[pl.ds(group * span, span)]
    for q, send in enumerate(sends, 1):
        send[...] = total[pl.ds((group ^ q) * span, span)].astype(BF16)


def residual_kernel(freq_count, slots, own, parts, *refs):
    got, (rounded, back) = refs[:-2], refs[-2:]
    own_rows(freq_count, 0, got, own, parts, rounded, back)


def spread_kernel(freq_count, slots, index, back, *refs):
    have, (out, table) = refs[:-2], refs[-2:]
    group = lax.div(lax.axis_index("tiles"), GROUP)
    span = GROUP * freq_count
    for q, ref in enumerate(have):
        table[pl.ds((group ^ q) * span, span)] = ref[...]
    out[:, slots:] = back[...]
    take_rows(slots, index, table, out)


def gradient_kernel(
    data, source, freqs, arrived, residual_hbm, gradient_hbm, residual, gradient, sems
):
    freq_count, _, block, shots = data.shape
    slots, height = gradient.shape[0], arrived.shape[2]
    piece = height // 2
    scale = 1.0 / shots
    for f in range(freq_count):
        real, imag = data[f, 0].astype(F32), data[f, 1].astype(F32)
        for j in range(GROUP):
            at = slice(j * piece, (j + 1) * piece)
            predicted = arrived[j, slots + f].astype(F32)
            residual[f, 0, at, :] = real[at] - predicted[:piece]
            residual[f, 1, at, :] = imag[at] - predicted[piece:]
    copies = [pltpu.make_async_copy(residual, residual_hbm, sems.at[0])]
    copies[0].start()
    parts = 4
    step = slots // parts

    def one(t, carry):
        left = arrived[:, t].reshape(GROUP * height, shots)
        right = source[freqs[t]].reshape(2 * block, shots)
        total = -scale * lax.dot_general(
            left, right, (((1,), (1,)), ((), ())), preferred_element_type=F32
        )
        real, imag = [], []
        for j in range(GROUP):
            upper = total[j * height : j * height + piece]
            lower = total[j * height + piece : (j + 1) * height]
            real.append(upper[:, :block] + lower[:, block:])
            imag.append(lower[:, :block] - upper[:, block:])
        gradient[t, 0] = jnp.concatenate(real, axis=0).astype(BF16)
        gradient[t, 1] = jnp.concatenate(imag, axis=0).astype(BF16)
        return carry

    for i in range(parts):
        lax.fori_loop(i * step, (i + 1) * step, one, 0, unroll=4)
        at = pl.ds(i * step, step)
        copies.append(
            pltpu.make_async_copy(gradient.at[at], gradient_hbm.at[at], sems.at[i + 1])
        )
        copies[-1].start()
    for copy in copies:
        copy.wait()


def per_device(data, wavelet, panel_block, tiles, cover_rows, cover_freqs):
    freq_count, _, block, shots = data.shape
    slots = tiles.shape[0]
    peers = lax.axis_size("tiles")
    groups = peers // GROUP
    height = 2 * block // GROUP
    span = GROUP * freq_count
    sizes = (freq_count, slots)
    members = [list(range(g * GROUP, (g + 1) * GROUP)) for g in range(groups)]

    def shape(count, kind=BF16):
        return jax.ShapeDtypeStruct((count, height, shots), kind)

    def payload(count):
        return jax.ShapeDtypeStruct((GROUP, count, height, shots), BF16)

    def exchange(value):
        return lax.all_to_all(
            value, "tiles", split_axis=0, concat_axis=0, tiled=True, axis_index_groups=members
        )

    def across(values):
        return [
            lax.ppermute(value, "tiles", [(i, i ^ (q * GROUP)) for i in range(peers)])
            for q, value in enumerate(values, 1)
        ]

    source, sent = call(
        parts_kernel,
        "parts",
        [
            jax.ShapeDtypeStruct(data.shape, BF16),
            payload(slots + slots // height + freq_count),
        ],
        [HBM] * 6,
        scratch=[
            pltpu.VMEM(data.shape, BF16),
            pltpu.SMEM((2, freq_count), F32),
            pltpu.SMEM((1,), jnp.int32),
            pltpu.VMEM(tiles.shape, BF16),
            pltpu.SMEM((slots,), jnp.int32),
            pltpu.SMEM((slots,), jnp.int32),
            pltpu.SemaphoreType.DMA((6,)),
        ],
        mib=60,
    )(data, wavelet.T, panel_block, tiles, cover_rows, cover_freqs)
    parts = exchange(sent)
    lists = parts[:, slots:-freq_count].reshape(GROUP, slots, shots).astype(jnp.int32)
    index = lists[:, :, 0] * freq_count + lists[:, :, shots // 2]
    total = pltpu.VMEM((peers * freq_count, height, shots), F32)
    table = pltpu.VMEM((peers * freq_count, height, shots), BF16)
    if groups == 1:
        returns = call(
            functools.partial(whole_kernel, *sizes),
            "residual_slices",
            payload(slots + freq_count),
            [SMEM, VMEM],
            scratch=[total, table],
        )(index, parts)
    else:
        own, *sends = call(
            functools.partial(sum_kernel, *sizes),
            "sums",
            [shape(span, F32)] + [shape(span)] * (groups - 1),
            [SMEM, VMEM],
            scratch=[total],
        )(index, parts)
        mine, back = call(
            functools.partial(residual_kernel, *sizes),
            "residual_slices",
            [shape(span), payload(freq_count)],
            [VMEM] * (1 + groups),
        )(own, parts, *across(sends))
        returns = call(
            functools.partial(spread_kernel, *sizes),
            "spread",
            payload(slots + freq_count),
            [SMEM] + [VMEM] * (1 + groups),
            scratch=[table],
        )(index, back, mine, *across([mine] * (groups - 1)))
    return call(
        gradient_kernel,
        "gradient",
        (jax.ShapeDtypeStruct(data.shape, F32), jax.ShapeDtypeStruct(tiles.shape, BF16)),
        [VMEM, VMEM, SMEM, VMEM],
        out_specs=(HBM, HBM),
        scratch=[
            pltpu.VMEM(data.shape, F32),
            pltpu.VMEM(tiles.shape, BF16),
            pltpu.SemaphoreType.DMA((5,)),
        ],
    )(data, source, cover_freqs, exchange(returns))


def solution(mesh):
    in_specs = (
        P("windows", None, "tiles", None),
        P(),
        P(),
        P(("windows", "tiles"), None, None, None),
        P(("windows", "tiles")),
        P(("windows", "tiles")),
    )
    out_specs = (P("windows", None, "tiles", None), P(("windows", "tiles"), None, None, None))
    return jax.shard_map(
        per_device, mesh=mesh, in_specs=in_specs, out_specs=out_specs, check_vma=False
    )
```

```python
import functools

import jax
import jax.numpy as jnp
from jax import lax
from jax.experimental import pallas as pl
from jax.experimental.pallas import tpu as pltpu
from jax.sharding import PartitionSpec as P

GROUP = 16
BF16 = jnp.bfloat16
F32 = jnp.float32
VMEM = pl.BlockSpec(memory_space=pltpu.VMEM)
SMEM = pl.BlockSpec(memory_space=pltpu.SMEM)
HBM = pl.BlockSpec(memory_space=pltpu.HBM)


def call(kernel, name, out_shape, in_specs, scratch=(), out_specs=None, mib=48):
    return pl.pallas_call(
        kernel,
        name=name,
        out_shape=out_shape,
        in_specs=in_specs,
        out_specs=out_specs or jax.tree.map(lambda _: VMEM, out_shape),
        scratch_shapes=list(scratch),
        cost_estimate=pl.CostEstimate(flops=0, bytes_accessed=1 << 20, transcendentals=0),
        compiler_params=pltpu.CompilerParams(vmem_limit_bytes=mib * 1024 * 1024),
    )


def put(buffer, slot, count, real, imag):
    piece = real.shape[0] // GROUP
    for j in range(GROUP):
        at = slice(j * piece, (j + 1) * piece)
        first = 2 * j * piece * count + slot
        buffer[pl.ds(first, piece, stride=count), :] = real[at]
        buffer[pl.ds(first + piece * count, piece, stride=count), :] = imag[at]


def get(buffer, slot, count, piece, j):
    first = 2 * j * piece * count + slot
    return (
        buffer[pl.ds(first, piece, stride=count), :],
        buffer[pl.ds(first + piece * count, piece, stride=count), :],
    )


def parts_kernel(
    data_hbm, wavelet_hbm, panel_hbm, tiles_hbm, rows_hbm, freqs_hbm,
    source, out, data, wavelet, panel, tiles, rows, freqs, sems, wide, wide_data,
):
    freq_count, _, block, shots = data.shape
    slots = tiles.shape[0]
    height = 2 * block // GROUP
    peers = lax.axis_size("tiles")
    pairs = (
        (data_hbm, data),
        (tiles_hbm, tiles),
        (wavelet_hbm, wavelet),
        (panel_hbm, panel),
        (freqs_hbm, freqs),
        (rows_hbm, rows),
    )
    copies = [pltpu.make_async_copy(*pair, sems.at[i]) for i, pair in enumerate(pairs)]
    for copy in copies:
        copy.start()
    diagonal = (
        lax.broadcasted_iota(jnp.int32, (block, shots), 0)
        == lax.broadcasted_iota(jnp.int32, (block, shots), 1)
    ).astype(F32)
    for i in (2, 3, 4, 5, 0):
        copies[i].wait()
    identity = diagonal * (lax.axis_index("tiles") == panel[0]).astype(F32)
    for f in range(freq_count):
        real, imag = data[f, 0].astype(F32), data[f, 1].astype(F32)
        source[f, 0] = (wavelet[0, f] * identity - real).astype(BF16)
        source[f, 1] = (wavelet[1, f] * identity - imag).astype(BF16)
        put(wide_data, f, freq_count, real, imag)
    line = lax.broadcasted_iota(jnp.int32, (slots, shots), 0)
    targets = jnp.zeros((slots, shots), jnp.int32)
    for t in range(slots):
        targets = jnp.where(line == t, rows[t] * freq_count + freqs[t], targets)
    targets = (targets - peers * freq_count // 2).astype(F32).astype(BF16)
    first, second = height * slots, height * (slots + freq_count)
    for j in range(GROUP):
        at = slice(j * height * freq_count, (j + 1) * height * freq_count)
        out[j, first:second] = wide_data[at].astype(BF16)
        out[j, second:] = targets
    copies[1].wait()

    def one(t, carry):
        f = freqs[t]
        left = tiles[t].reshape(2 * block, block)
        right = jnp.concatenate([source[f, 0], source[f, 1]], axis=1)
        product = jnp.dot(left, right, preferred_element_type=F32)
        real = product[:block, :shots] - product[block:, shots:]
        put(wide, t, slots, real, product[:block, shots:] + product[block:, :shots])
        return carry

    lax.fori_loop(0, slots, one, 0, unroll=4)
    for j in range(GROUP):
        out[j, :first] = wide[j * first : (j + 1) * first].astype(BF16)


def one_hot(slots, peers, freq_count, parts):
    first = parts.shape[1] - slots
    shots = parts.shape[2]
    targets = parts[:, first:].astype(F32).reshape(GROUP * slots, shots)
    count = peers * freq_count
    lane = lax.broadcasted_iota(jnp.int32, (GROUP * slots, shots), 1).astype(F32)
    hot = [
        (targets == lane + float(start - count // 2)).astype(F32).astype(BF16)
        for start in range(0, count, shots)
    ]
    return jnp.concatenate(hot, axis=1) if len(hot) > 1 else hot[0]


def row_of_slots(slots, r, parts):
    at = slice(r * slots, (r + 1) * slots)
    return parts[:, at].reshape(GROUP * slots, parts.shape[2])


def sum_row(hot, row):
    return lax.dot_general(hot, row, (((0,), (0,)), ((), ())), preferred_element_type=F32)


def row_of_data(freq_count, slots, r, height, parts):
    first = height * slots + r * freq_count
    rows = parts[:, first : first + freq_count].astype(F32)
    return rows.reshape(GROUP * freq_count, parts.shape[2])


def put_back(freq_count, first, predicted, out):
    for r in range(0, len(predicted), 2):
        for j in range(GROUP):
            at = slice(j * freq_count, (j + 1) * freq_count)
            rows = jnp.concatenate([predicted[r][at], predicted[r + 1][at]], axis=0)
            out[j, first + r * freq_count : first + (r + 2) * freq_count] = rows.astype(BF16)


def whole_kernel(sizes, parts, out):
    freq_count, slots, peers = sizes
    height = (parts.shape[1] - slots) // (slots + freq_count)
    shots = parts.shape[2]
    hot = one_hot(slots, peers, freq_count, parts)
    step = 2
    for r in range(0, height, step):
        rows = [row_of_slots(slots, r + i, parts) for i in range(step)]
        total = sum_row(hot, jnp.concatenate(rows, axis=1))
        predicted = [total[:, i * shots : (i + 1) * shots] for i in range(step)]
        data = [row_of_data(freq_count, slots, r + i, height, parts) for i in range(step)]
        rounded = jnp.concatenate(
            [(d - p).astype(BF16) for d, p in zip(data, predicted)], axis=1
        )
        picked = jnp.dot(hot, rounded, preferred_element_type=F32).astype(BF16)
        for i in range(step):
            at = slice((r + i) * slots, (r + i + 1) * slots)
            out[:, at] = picked[:, i * shots : (i + 1) * shots].reshape(GROUP, slots, shots)
        put_back(freq_count, height * slots + r * freq_count, predicted, out)


def sum_kernel(sizes, parts, own, *refs):
    freq_count, slots, peers = sizes
    sends, total = refs[:-1], refs[-1]
    span = GROUP * freq_count
    group = lax.div(lax.axis_index("tiles"), GROUP)
    hot = one_hot(slots, peers, freq_count, parts)
    for r in range(own.shape[0]):
        total[...] = sum_row(hot, row_of_slots(slots, r, parts))
        own[r] = total[pl.ds(pl.multiple_of(group * span, span), span)]
        for q, send in enumerate(sends, 1):
            there = pl.multiple_of((group ^ q) * span, span)
            send[r] = total[pl.ds(there, span)].astype(BF16)


def residual_kernel(sizes, own, parts, *refs):
    freq_count, slots, _ = sizes
    got, (rounded, back) = refs[:-2], refs[-2:]
    height = own.shape[0]
    for r in range(0, height, 2):
        predicted = []
        for i in (r, r + 1):
            values = own[i]
            for ref in got:
                values += ref[i].astype(F32)
            predicted.append(values)
            data = row_of_data(freq_count, slots, i, height, parts)
            rounded[i] = (data - values).astype(BF16)
        put_back(freq_count, r * freq_count, predicted, back)


def spread_kernel(sizes, parts, back, *refs):
    freq_count, slots, peers = sizes
    have, (out, table) = refs[:-2], refs[-2:]
    height, span, shots = have[0].shape
    group = lax.div(lax.axis_index("tiles"), GROUP)
    hot = one_hot(slots, peers, freq_count, parts)
    for r in range(height):
        for q, ref in enumerate(have):
            table[pl.ds(pl.multiple_of((group ^ q) * span, span), span)] = ref[r]
        picked = jnp.dot(hot, table[...], preferred_element_type=F32).astype(BF16)
        out[:, r * slots : (r + 1) * slots] = picked.reshape(GROUP, slots, shots)
    out[:, height * slots :] = back[...]


def gradient_kernel(
    data, source, freqs, arrived, residual_hbm, gradient_hbm, residual, gradient, sems, wide, wide_data
):
    freq_count, _, block, shots = data.shape
    slots = gradient.shape[0]
    piece = block // GROUP
    height = 2 * piece
    first = height * slots
    second = first + height * freq_count
    scale = 1.0 / shots
    for j in range(GROUP):
        at = slice(j * height * freq_count, (j + 1) * height * freq_count)
        wide_data[at] = arrived[j, first:second].astype(F32)
    for f in range(freq_count):
        real, imag = data[f, 0].astype(F32), data[f, 1].astype(F32)
        for j in range(GROUP):
            at = slice(j * piece, (j + 1) * piece)
            predicted = get(wide_data, f, freq_count, piece, j)
            residual[f, 0, at, :] = real[at] - predicted[0]
            residual[f, 1, at, :] = imag[at] - predicted[1]
    copies = [pltpu.make_async_copy(residual, residual_hbm, sems.at[0])]
    copies[0].start()
    for j in range(GROUP):
        wide[j * first : (j + 1) * first] = arrived[j, :first].astype(F32)
    parts = 4
    step = slots // parts

    def one(t, carry):
        left = wide[pl.ds(t, GROUP * height, stride=slots), :].astype(BF16)
        right = source[freqs[t]].reshape(2 * block, shots)
        total = -scale * lax.dot_general(
            left, right, (((1,), (1,)), ((), ())), preferred_element_type=F32
        )
        real, imag = [], []
        for j in range(GROUP):
            upper = total[j * height : j * height + piece]
            lower = total[j * height + piece : (j + 1) * height]
            real.append(upper[:, :block] + lower[:, block:])
            imag.append(lower[:, :block] - upper[:, block:])
        gradient[t, 0] = jnp.concatenate(real, axis=0).astype(BF16)
        gradient[t, 1] = jnp.concatenate(imag, axis=0).astype(BF16)
        return carry

    for i in range(parts):
        lax.fori_loop(i * step, (i + 1) * step, one, 0, unroll=4)
        at = pl.ds(i * step, step)
        copies.append(
            pltpu.make_async_copy(gradient.at[at], gradient_hbm.at[at], sems.at[i + 1])
        )
        copies[-1].start()
    for copy in copies:
        copy.wait()


def per_device(data, wavelet, panel_block, tiles, cover_rows, cover_freqs):
    freq_count, _, block, shots = data.shape
    slots = tiles.shape[0]
    peers = lax.axis_size("tiles")
    groups = peers // GROUP
    height = 2 * block // GROUP
    span = GROUP * freq_count
    sizes = (freq_count, slots, peers)
    members = [list(range(g * GROUP, (g + 1) * GROUP)) for g in range(groups)]
    wide = pltpu.VMEM((GROUP * height * slots, shots), F32)
    wide_data = pltpu.VMEM((GROUP * height * freq_count, shots), F32)

    def shape(kind=BF16):
        return jax.ShapeDtypeStruct((height, span, shots), kind)

    def payload(count):
        return jax.ShapeDtypeStruct((GROUP, count, shots), BF16)

    def exchange(value):
        return lax.all_to_all(
            value, "tiles", split_axis=0, concat_axis=0, tiled=True, axis_index_groups=members
        )

    def across(values):
        return [
            lax.ppermute(value, "tiles", [(i, i ^ (q * GROUP)) for i in range(peers)])
            for q, value in enumerate(values, 1)
        ]

    source, sent = call(
        parts_kernel,
        "parts",
        [
            jax.ShapeDtypeStruct(data.shape, BF16),
            payload(height * (slots + freq_count) + slots),
        ],
        [HBM] * 6,
        scratch=[
            pltpu.VMEM(data.shape, BF16),
            pltpu.SMEM((2, freq_count), F32),
            pltpu.SMEM((1,), jnp.int32),
            pltpu.VMEM(tiles.shape, BF16),
            pltpu.SMEM((slots,), jnp.int32),
            pltpu.SMEM((slots,), jnp.int32),
            pltpu.SemaphoreType.DMA((6,)),
            wide,
            wide_data,
        ],
        mib=60,
    )(data, wavelet.T, panel_block, tiles, cover_rows, cover_freqs)
    parts = exchange(sent)
    returns = payload(height * (slots + freq_count))
    if groups == 1:
        out = call(
            functools.partial(whole_kernel, sizes), "residual_slices", returns, [VMEM]
        )(parts)
    else:
        own, *sends = call(
            functools.partial(sum_kernel, sizes),
            "sums",
            [shape(F32)] + [shape()] * (groups - 1),
            [VMEM],
            scratch=[pltpu.VMEM((peers * freq_count, shots), F32)],
        )(parts)
        mine, back = call(
            functools.partial(residual_kernel, sizes),
            "residual_slices",
            [shape(), payload(height * freq_count)],
            [VMEM] * (1 + groups),
        )(own, parts, *across(sends))
        out = call(
            functools.partial(spread_kernel, sizes),
            "spread",
            returns,
            [VMEM] * (2 + groups),
            scratch=[pltpu.VMEM((peers * freq_count, shots), BF16)],
        )(parts, back, mine, *across([mine] * (groups - 1)))
    return call(
        gradient_kernel,
        "gradient",
        (jax.ShapeDtypeStruct(data.shape, F32), jax.ShapeDtypeStruct(tiles.shape, BF16)),
        [VMEM, VMEM, SMEM, VMEM],
        out_specs=(HBM, HBM),
        scratch=[
            pltpu.VMEM(data.shape, F32),
            pltpu.VMEM(tiles.shape, BF16),
            pltpu.SemaphoreType.DMA((5,)),
            wide,
            wide_data,
        ],
    )(data, source, cover_freqs, exchange(out))


def solution(mesh):
    in_specs = (
        P("windows", None, "tiles", None),
        P(),
        P(),
        P(("windows", "tiles"), None, None, None),
        P(("windows", "tiles")),
        P(("windows", "tiles")),
    )
    out_specs = (P("windows", None, "tiles", None), P(("windows", "tiles"), None, None, None))
    return jax.shard_map(
        per_device, mesh=mesh, in_specs=in_specs, out_specs=out_specs, check_vma=False
    )
```

```python
import functools

import jax
import jax.numpy as jnp
from jax import lax
from jax.experimental import pallas as pl
from jax.experimental.pallas import tpu as pltpu
from jax.sharding import PartitionSpec as P

GROUP = 16
BF16 = jnp.bfloat16
F32 = jnp.float32
VMEM = pl.BlockSpec(memory_space=pltpu.VMEM)
SMEM = pl.BlockSpec(memory_space=pltpu.SMEM)
HBM = pl.BlockSpec(memory_space=pltpu.HBM)


def call(kernel, name, out_shape, in_specs, scratch=(), out_specs=None, mib=48):
    return pl.pallas_call(
        kernel,
        name=name,
        out_shape=out_shape,
        in_specs=in_specs,
        out_specs=out_specs or jax.tree.map(lambda _: VMEM, out_shape),
        scratch_shapes=list(scratch),
        cost_estimate=pl.CostEstimate(flops=0, bytes_accessed=1 << 20, transcendentals=0),
        compiler_params=pltpu.CompilerParams(vmem_limit_bytes=mib * 1024 * 1024),
    )


def stay(array):
    return pltpu.with_memory_space_constraint(array, pltpu.HBM)


def put(buffer, slot, count, real, imag):
    piece = real.shape[0] // GROUP
    for j in range(GROUP):
        at = slice(j * piece, (j + 1) * piece)
        first = 2 * j * piece * count + slot
        buffer[pl.ds(first, piece, stride=count), :] = real[at]
        buffer[pl.ds(first + piece * count, piece, stride=count), :] = imag[at]


def get(buffer, slot, count, piece, j):
    first = 2 * j * piece * count + slot
    return (
        buffer[pl.ds(first, piece, stride=count), :],
        buffer[pl.ds(first + piece * count, piece, stride=count), :],
    )


def parts_kernel(
    data_hbm, wavelet_hbm, panel_hbm, tiles_hbm, rows_hbm, freqs_hbm,
    source, out, data, wavelet, panel, tiles, rows, freqs, sems, wide, wide_data,
):
    freq_count, _, block, shots = data.shape
    slots = tiles.shape[0]
    height = 2 * block // GROUP
    peers = lax.axis_size("tiles")
    pairs = (
        (data_hbm, data),
        (tiles_hbm, tiles),
        (wavelet_hbm, wavelet),
        (panel_hbm, panel),
        (freqs_hbm, freqs),
        (rows_hbm, rows),
    )
    copies = [pltpu.make_async_copy(*pair, sems.at[i]) for i, pair in enumerate(pairs)]
    for copy in copies:
        copy.start()
    diagonal = (
        lax.broadcasted_iota(jnp.int32, (block, shots), 0)
        == lax.broadcasted_iota(jnp.int32, (block, shots), 1)
    ).astype(F32)
    for i in (2, 3, 4, 5, 0):
        copies[i].wait()
    identity = diagonal * (lax.axis_index("tiles") == panel[0]).astype(F32)
    for f in range(freq_count):
        real, imag = data[f, 0].astype(F32), data[f, 1].astype(F32)
        source[f, 0] = (wavelet[0, f] * identity - real).astype(BF16)
        source[f, 1] = (wavelet[1, f] * identity - imag).astype(BF16)
        put(wide_data, f, freq_count, real, imag)
    line = lax.broadcasted_iota(jnp.int32, (slots, shots), 0)
    targets = jnp.zeros((slots, shots), jnp.int32)
    for t in range(slots):
        targets = jnp.where(line == t, rows[t] * freq_count + freqs[t], targets)
    targets = (targets - peers * freq_count // 2).astype(F32).astype(BF16)
    first, second = height * slots, height * (slots + freq_count)
    for j in range(GROUP):
        at = slice(j * height * freq_count, (j + 1) * height * freq_count)
        out[j, first:second] = wide_data[at].astype(BF16)
        out[j, second:] = targets
    copies[1].wait()

    def one(t, carry):
        f = freqs[t]
        left = tiles[t].reshape(2 * block, block)
        right = jnp.concatenate([source[f, 0], source[f, 1]], axis=1)
        product = jnp.dot(left, right, preferred_element_type=F32)
        real = product[:block, :shots] - product[block:, shots:]
        put(wide, t, slots, real, product[:block, shots:] + product[block:, :shots])
        return carry

    lax.fori_loop(0, slots, one, 0, unroll=16)
    for j in range(GROUP):
        out[j, :first] = wide[j * first : (j + 1) * first].astype(BF16)


def one_hot(slots, peers, freq_count, parts):
    first = parts.shape[1] - slots
    shots = parts.shape[2]
    targets = parts[:, first:].astype(F32).reshape(GROUP * slots, shots)
    count = peers * freq_count
    lane = lax.broadcasted_iota(jnp.int32, (GROUP * slots, shots), 1).astype(F32)
    hot = [
        (targets == lane + float(start - count // 2)).astype(F32).astype(BF16)
        for start in range(0, count, shots)
    ]
    return jnp.concatenate(hot, axis=1) if len(hot) > 1 else hot[0]


def row_of_slots(slots, r, parts):
    at = slice(r * slots, (r + 1) * slots)
    return parts[:, at].reshape(GROUP * slots, parts.shape[2])


def sum_row(hot, row):
    return lax.dot_general(hot, row, (((0,), (0,)), ((), ())), preferred_element_type=F32)


def row_of_data(freq_count, slots, r, height, parts):
    first = height * slots + r * freq_count
    rows = parts[:, first : first + freq_count].astype(F32)
    return rows.reshape(GROUP * freq_count, parts.shape[2])


def put_back(freq_count, first, predicted, out):
    for r in range(0, len(predicted), 2):
        for j in range(GROUP):
            at = slice(j * freq_count, (j + 1) * freq_count)
            rows = jnp.concatenate([predicted[r][at], predicted[r + 1][at]], axis=0)
            out[j, first + r * freq_count : first + (r + 2) * freq_count] = rows.astype(BF16)


def whole_kernel(sizes, parts, out):
    freq_count, slots, peers = sizes
    height = (parts.shape[1] - slots) // (slots + freq_count)
    shots = parts.shape[2]
    hot = one_hot(slots, peers, freq_count, parts)
    step = 2
    for r in range(0, height, step):
        rows = [row_of_slots(slots, r + i, parts) for i in range(step)]
        total = sum_row(hot, jnp.concatenate(rows, axis=1))
        predicted = [total[:, i * shots : (i + 1) * shots] for i in range(step)]
        data = [row_of_data(freq_count, slots, r + i, height, parts) for i in range(step)]
        rounded = jnp.concatenate(
            [(d - p).astype(BF16) for d, p in zip(data, predicted)], axis=1
        )
        picked = jnp.dot(hot, rounded, preferred_element_type=F32).astype(BF16)
        for i in range(step):
            at = slice((r + i) * slots, (r + i + 1) * slots)
            out[:, at] = picked[:, i * shots : (i + 1) * shots].reshape(GROUP, slots, shots)
        put_back(freq_count, height * slots + r * freq_count, predicted, out)


def sum_kernel(sizes, parts, own, *refs):
    freq_count, slots, peers = sizes
    sends, total = refs[:-1], refs[-1]
    span = GROUP * freq_count
    group = lax.div(lax.axis_index("tiles"), GROUP)
    hot = one_hot(slots, peers, freq_count, parts)
    for r in range(own.shape[0]):
        total[...] = sum_row(hot, row_of_slots(slots, r, parts))
        own[r] = total[pl.ds(pl.multiple_of(group * span, span), span)]
        for q, send in enumerate(sends, 1):
            there = pl.multiple_of((group ^ q) * span, span)
            send[r] = total[pl.ds(there, span)].astype(BF16)


def residual_kernel(sizes, own, parts, *refs):
    freq_count, slots, _ = sizes
    got, (rounded, back) = refs[:-2], refs[-2:]
    height = own.shape[0]
    for r in range(0, height, 2):
        predicted = []
        for i in (r, r + 1):
            values = own[i]
            for ref in got:
                values += ref[i].astype(F32)
            predicted.append(values)
            data = row_of_data(freq_count, slots, i, height, parts)
            rounded[i] = (data - values).astype(BF16)
        put_back(freq_count, r * freq_count, predicted, back)


def spread_kernel(sizes, parts, back, *refs):
    freq_count, slots, peers = sizes
    have, (out, table) = refs[:-2], refs[-2:]
    height, span, shots = have[0].shape
    group = lax.div(lax.axis_index("tiles"), GROUP)
    hot = one_hot(slots, peers, freq_count, parts)
    for r in range(height):
        for q, ref in enumerate(have):
            table[pl.ds(pl.multiple_of((group ^ q) * span, span), span)] = ref[r]
        picked = jnp.dot(hot, table[...], preferred_element_type=F32).astype(BF16)
        out[:, r * slots : (r + 1) * slots] = picked.reshape(GROUP, slots, shots)
    out[:, height * slots :] = back[...]


def gradient_kernel(
    data, source, freqs, arrived, residual_hbm, gradient_hbm, residual, gradient, sems, wide, wide_data
):
    freq_count, _, block, shots = data.shape
    slots = gradient.shape[0]
    piece = block // GROUP
    height = 2 * piece
    first = height * slots
    second = first + height * freq_count
    scale = 1.0 / shots
    for j in range(GROUP):
        at = slice(j * height * freq_count, (j + 1) * height * freq_count)
        wide_data[at] = arrived[j, first:second].astype(F32)
    for f in range(freq_count):
        real, imag = data[f, 0].astype(F32), data[f, 1].astype(F32)
        for j in range(GROUP):
            at = slice(j * piece, (j + 1) * piece)
            predicted = get(wide_data, f, freq_count, piece, j)
            residual[f, 0, at, :] = real[at] - predicted[0]
            residual[f, 1, at, :] = imag[at] - predicted[1]
    copies = [pltpu.make_async_copy(residual, residual_hbm, sems.at[0])]
    copies[0].start()
    for j in range(GROUP):
        wide[j * first : (j + 1) * first] = arrived[j, :first].astype(F32)
    parts = 4
    step = slots // parts

    def one(t, carry):
        left = wide[pl.ds(t, GROUP * height, stride=slots), :].astype(BF16)
        right = source[freqs[t]].reshape(2 * block, shots)
        total = -scale * lax.dot_general(
            left, right, (((1,), (1,)), ((), ())), preferred_element_type=F32
        )
        real, imag = [], []
        for j in range(GROUP):
            upper = total[j * height : j * height + piece]
            lower = total[j * height + piece : (j + 1) * height]
            real.append(upper[:, :block] + lower[:, block:])
            imag.append(lower[:, :block] - upper[:, block:])
        gradient[t, 0] = jnp.concatenate(real, axis=0).astype(BF16)
        gradient[t, 1] = jnp.concatenate(imag, axis=0).astype(BF16)
        return carry

    for i in range(parts):
        lax.fori_loop(i * step, (i + 1) * step, one, 0, unroll=4)
        at = pl.ds(i * step, step)
        copies.append(
            pltpu.make_async_copy(gradient.at[at], gradient_hbm.at[at], sems.at[i + 1])
        )
        copies[-1].start()
    for copy in copies:
        copy.wait()


def per_device(data, wavelet, panel_block, tiles, cover_rows, cover_freqs):
    freq_count, _, block, shots = data.shape
    slots = tiles.shape[0]
    peers = lax.axis_size("tiles")
    groups = peers // GROUP
    height = 2 * block // GROUP
    span = GROUP * freq_count
    sizes = (freq_count, slots, peers)
    members = [list(range(g * GROUP, (g + 1) * GROUP)) for g in range(groups)]
    wide = pltpu.VMEM((GROUP * height * slots, shots), F32)
    wide_data = pltpu.VMEM((GROUP * height * freq_count, shots), F32)

    def shape(kind=BF16):
        return jax.ShapeDtypeStruct((height, span, shots), kind)

    def payload(count):
        return jax.ShapeDtypeStruct((GROUP, count, shots), BF16)

    def exchange(value):
        return lax.all_to_all(
            value, "tiles", split_axis=0, concat_axis=0, tiled=True, axis_index_groups=members
        )

    def across(values):
        return [
            lax.ppermute(value, "tiles", [(i, i ^ (q * GROUP)) for i in range(peers)])
            for q, value in enumerate(values, 1)
        ]

    source, sent = call(
        parts_kernel,
        "parts",
        [
            jax.ShapeDtypeStruct(data.shape, BF16),
            payload(height * (slots + freq_count) + slots),
        ],
        [HBM] * 6,
        scratch=[
            pltpu.VMEM(data.shape, BF16),
            pltpu.SMEM((2, freq_count), F32),
            pltpu.SMEM((1,), jnp.int32),
            pltpu.VMEM(tiles.shape, BF16),
            pltpu.SMEM((slots,), jnp.int32),
            pltpu.SMEM((slots,), jnp.int32),
            pltpu.SemaphoreType.DMA((6,)),
            wide,
            wide_data,
        ],
    )(stay(data), stay(wavelet.T), panel_block, *map(stay, (tiles, cover_rows, cover_freqs)))
    parts = exchange(sent)
    returns = payload(height * (slots + freq_count))
    if groups == 1:
        out = call(
            functools.partial(whole_kernel, sizes), "residual_slices", returns, [VMEM]
        )(parts)
    else:
        own, *sends = call(
            functools.partial(sum_kernel, sizes),
            "sums",
            [shape(F32)] + [shape()] * (groups - 1),
            [VMEM],
            scratch=[pltpu.VMEM((peers * freq_count, shots), F32)],
        )(parts)
        mine, back = call(
            functools.partial(residual_kernel, sizes),
            "residual_slices",
            [shape(), payload(height * freq_count)],
            [VMEM] * (1 + groups),
        )(own, parts, *across(sends))
        out = call(
            functools.partial(spread_kernel, sizes),
            "spread",
            returns,
            [VMEM] * (2 + groups),
            scratch=[pltpu.VMEM((peers * freq_count, shots), BF16)],
        )(parts, back, mine, *across([mine] * (groups - 1)))
    return call(
        gradient_kernel,
        "gradient",
        (jax.ShapeDtypeStruct(data.shape, F32), jax.ShapeDtypeStruct(tiles.shape, BF16)),
        [VMEM, VMEM, SMEM, VMEM],
        out_specs=(HBM, HBM),
        scratch=[
            pltpu.VMEM(data.shape, F32),
            pltpu.VMEM(tiles.shape, BF16),
            pltpu.SemaphoreType.DMA((5,)),
            wide,
            wide_data,
        ],
    )(data, source, cover_freqs, exchange(out))


def solution(mesh):
    in_specs = (
        P("windows", None, "tiles", None),
        P(),
        P(),
        P(("windows", "tiles"), None, None, None),
        P(("windows", "tiles")),
        P(("windows", "tiles")),
    )
    out_specs = (P("windows", None, "tiles", None), P(("windows", "tiles"), None, None, None))
    return jax.shard_map(
        per_device, mesh=mesh, in_specs=in_specs, out_specs=out_specs, check_vma=False
    )
```

```python
import functools

import jax
import jax.numpy as jnp
from jax import lax
from jax.experimental import pallas as pl
from jax.experimental.pallas import tpu as pltpu
from jax.sharding import PartitionSpec as P

GROUP = 8
CHIPS = (2, 4, 6)
BF16 = jnp.bfloat16
F32 = jnp.float32
VMEM = pl.BlockSpec(memory_space=pltpu.VMEM)
SMEM = pl.BlockSpec(memory_space=pltpu.SMEM)
HBM = pl.BlockSpec(memory_space=pltpu.HBM)
ANY = pl.BlockSpec(memory_space=pl.ANY)


def call(kernel, name, out_shape, in_specs, scratch=(), out_specs=None, mib=24):
    return pl.pallas_call(
        kernel,
        name=name,
        out_shape=out_shape,
        in_specs=in_specs,
        out_specs=out_specs or jax.tree.map(lambda _: VMEM, out_shape),
        scratch_shapes=list(scratch),
        cost_estimate=pl.CostEstimate(flops=0, bytes_accessed=1 << 20, transcendentals=0),
        compiler_params=pltpu.CompilerParams(vmem_limit_bytes=mib * 1024 * 1024),
    )


def stay(array):
    return pltpu.with_memory_space_constraint(array, pltpu.HBM)


def local_index():
    return lax.rem(lax.axis_index("tiles"), GROUP)


def group_index():
    return lax.div(lax.axis_index("tiles"), GROUP)


def put(buffer, slot, count, real, imag):
    piece = real.shape[0] // GROUP
    for j in range(GROUP):
        at = slice(j * piece, (j + 1) * piece)
        first = 2 * j * piece * count + slot
        buffer[pl.ds(first, piece, stride=count), :] = real[at]
        buffer[pl.ds(first + piece * count, piece, stride=count), :] = imag[at]


def transposed_dot(left, right):
    return lax.dot_general(left, right, (((0,), (0,)), ((), ())), preferred_element_type=F32)


def member_rows(k, count):
    return pl.ds(pl.multiple_of((local_index() ^ k) * count, count), count)


def parts_kernel(data_hbm, wavelet_hbm, panel_hbm, tiles_hbm, rows_hbm, freqs_hbm, *refs):
    source, outs = refs[0], refs[1 : 1 + GROUP]
    data, wavelet, panel, tiles, rows, freqs, sems, wide = refs[1 + GROUP :]
    freq_count, _, block, shots = data.shape
    slots = tiles.shape[0]
    size = 2 * block // GROUP * slots
    half = lax.axis_size("tiles") * freq_count // 2
    pairs = (
        (data_hbm, data),
        (tiles_hbm, tiles),
        (wavelet_hbm, wavelet),
        (panel_hbm, panel),
        (freqs_hbm, freqs),
        (rows_hbm, rows),
    )
    copies = [pltpu.make_async_copy(*pair, sems.at[i]) for i, pair in enumerate(pairs)]
    for copy in copies:
        copy.start()
    diagonal = (
        lax.broadcasted_iota(jnp.int32, (block, shots), 0)
        == lax.broadcasted_iota(jnp.int32, (block, shots), 1)
    ).astype(F32)
    for i in (2, 3, 4, 5, 0):
        copies[i].wait()
    identity = diagonal * (lax.axis_index("tiles") == panel[0]).astype(F32)
    for f in range(freq_count):
        source[f, 0] = (wavelet[0, f] * identity - data[f, 0].astype(F32)).astype(BF16)
        source[f, 1] = (wavelet[1, f] * identity - data[f, 1].astype(F32)).astype(BF16)
    line = lax.broadcasted_iota(jnp.int32, (slots, shots), 0)
    targets = jnp.zeros((slots, shots), jnp.int32)
    for t in range(slots):
        targets = jnp.where(line == t, rows[t] * freq_count + freqs[t] - half, targets)
    for k in range(GROUP):
        outs[k][size:] = targets.astype(F32).astype(BF16)
    copies[1].wait()

    def one(t, carry):
        f = freqs[t]
        left = tiles[t].reshape(2 * block, block)
        right = jnp.concatenate([source[f, 0], source[f, 1]], axis=1)
        product = jnp.dot(left, right, preferred_element_type=F32)
        real = product[:block, :shots] - product[block:, shots:]
        put(wide, t, slots, real, product[:block, shots:] + product[block:, :shots])
        return carry

    lax.fori_loop(0, slots, one, 0, unroll=16)
    for k in range(GROUP):
        outs[k][:size] = wide[member_rows(k, size)].astype(BF16)


def sums_kernel(sizes, *refs):
    slots, groups, span, cap = sizes
    parts, (hot_out, own, *sends) = refs[:GROUP], refs[GROUP:]
    height, _, shots = own.shape
    count = GROUP * slots
    group = group_index()
    targets = jnp.concatenate([part[height * slots :] for part in parts], axis=0).astype(F32)
    lane = lax.broadcasted_iota(jnp.int32, (count, shots), 1)
    hot = []
    for q in range(0, groups, shots // span):
        here = jnp.zeros((count, shots), jnp.int32)
        for i in range(shots // span):
            inside = lane - i * span + (group ^ (q + i)) * span - groups * span // 2
            here = jnp.where(lane >= i * span, inside, here)
        hot.append((targets == here.astype(F32)).astype(F32).astype(BF16))
    if groups == 2:
        other = hot[0][:, span:]
        used = (transposed_dot(other, jnp.ones((count, shots), BF16)) > 0).astype(F32)
        before = (
            lax.broadcasted_iota(jnp.int32, (span, span), 0)
            > lax.broadcasted_iota(jnp.int32, (span, span), 1)
        ).astype(F32)
        rank = jnp.dot(before.astype(BF16), used.astype(BF16), preferred_element_type=F32)
        slot = lax.broadcasted_iota(jnp.int32, (span, shots), 1).astype(F32)
        chosen = jnp.where(rank == slot, used, 0.0)
        number = jnp.sum(used, axis=0, keepdims=True)
        sends[0][height * cap :] = jnp.where(slot < span, chosen, number).astype(BF16)
        moved = jnp.dot(other, chosen[:, :span].astype(BF16), preferred_element_type=F32)
        hot = [jnp.concatenate([hot[0][:, :span], moved.astype(BF16)], axis=1)]
    hot = jnp.concatenate(hot, axis=1) if len(hot) > 1 else hot[0]
    hot_out[...] = hot
    step = 2
    for r in range(0, height, step):
        rows = [
            jnp.concatenate([part[(r + i) * slots : (r + i + 1) * slots] for part in parts], axis=0)
            for i in range(step)
        ]
        total = transposed_dot(hot, jnp.concatenate(rows, axis=1))
        for i in range(step):
            values = total[:, i * shots : (i + 1) * shots]
            own[r + i] = values[:span]
            if groups == 2:
                at = slice((r + i) * cap, (r + i + 1) * cap)
                sends[0][at] = values[span : span + cap].astype(BF16)
                sends[1][r + i] = values[span + cap :].astype(BF16)
            else:
                for q, send in enumerate(sends, 1):
                    send[r + i] = values[q * span : (q + 1) * span].astype(BF16)


def hand_out(outs, rows):
    size = outs[0].shape[0]
    outs[0][...] = rows(0)
    outs[1][...] = rows(1)
    for out, k in zip(outs[2:], CHIPS):
        out[:size] = rows(k)
        out[size:] = rows(k ^ 1)


def collect(refs, rows):
    own, *got, mate = refs
    size = own.shape[0]
    rows(0, own[...])
    rows(1, mate[:size])
    for i, k in enumerate(CHIPS):
        rows(k, got[i][:size])
        rows(k ^ 1, mate[(i + 1) * size : (i + 2) * size])


def relay_kernel(own, *refs):
    got, out = refs[:-1], refs[-1]
    size = own.shape[0]
    out[:size] = own[...]
    for i, ref in enumerate(got, 1):
        out[i * size : (i + 1) * size] = ref[size:]


def most_kernel(got_hbm, mine_hbm, *refs):
    out, got, mine, sems = refs[-4:]
    last = pl.ds(got_hbm.shape[0] - got.shape[0], got.shape[0])
    copies = [
        pltpu.make_async_copy(got_hbm.at[last], got, sems.at[0]),
        pltpu.make_async_copy(mine_hbm.at[last], mine, sems.at[1]),
    ]
    for copy in copies:
        copy.start()
    for copy in copies:
        copy.wait()
    half = got.shape[1] // 2
    most = jnp.maximum(got[:, half:].astype(F32), mine[:, half:].astype(F32))
    out[0] = jnp.max(most).astype(jnp.int32)


def slices_kernel(data, _, *refs):
    outs, wide = refs[:-1], refs[-1]
    freq_count = data.shape[0]
    for f in range(freq_count):
        put(wide, f, freq_count, data[f, 0].astype(F32), data[f, 1].astype(F32))
    for k in range(GROUP):
        outs[k][...] = wide[member_rows(k, outs[k].shape[0])].astype(BF16)


def residual_kernel(sizes, own, *refs):
    slots, groups, span, cap = sizes
    height, _, shots = own.shape
    data_in, refs = refs[:GROUP], refs[GROUP:]
    if groups == 2:
        got, got_rest, rounded, send, rest, *outs, data, back = refs
        chosen = got[height * cap :, :span]
    else:
        got, (rounded, *outs, data, back) = refs[: groups - 1], refs[groups - 1 :]
    local = local_index()
    freq_count = data.shape[1] // height
    for k in range(GROUP):
        data[local ^ k] = data_in[k][...]
    step = 8
    for r in range(0, height, step):
        rows = range(r, r + step)
        total = jnp.concatenate([own[i] for i in rows], axis=1)
        if groups == 2:
            more = []
            for i in rows:
                used = got[i * cap : (i + 1) * cap]
                more.append(jnp.concatenate([used, got_rest[i]], axis=0))
            more = jnp.concatenate(more, axis=1)
            total += jnp.dot(chosen, more, preferred_element_type=F32)
        else:
            for ref in got:
                total += jnp.concatenate([ref[i].astype(F32) for i in rows], axis=1)
        values = data[:, r * freq_count : (r + step) * freq_count].astype(F32)
        values = [
            values[:, i * freq_count : (i + 1) * freq_count].reshape(span, shots)
            for i in range(step)
        ]
        values = (jnp.concatenate(values, axis=1) - total).astype(BF16)
        for j in range(GROUP):
            at = slice(j * freq_count, (j + 1) * freq_count)
            pair = [total[at, i * shots : (i + 1) * shots] for i in range(step)]
            pair = jnp.concatenate(pair, axis=0)
            back[j, r * freq_count : (r + step) * freq_count] = pair.astype(BF16)
        picked = transposed_dot(chosen, values).astype(BF16) if groups == 2 else None
        for i in rows:
            at = slice((i - r) * shots, (i - r + 1) * shots)
            rounded[i] = values[:, at]
            if groups == 2:
                send[i] = picked[:cap, at]
                rest[i] = picked[cap:, at]
    hand_out(outs, lambda k: back[local ^ k])


def spread_kernel(slots, hot, *refs):
    have, outs = refs[:-GROUP], refs[-GROUP:]
    height, _, shots = have[0].shape
    step = 8
    for r in range(0, height, step):
        rows = [
            jnp.concatenate([ref[i] for ref in have], axis=0) for i in range(r, r + step)
        ]
        picked = jnp.dot(hot[...], jnp.concatenate(rows, axis=1), preferred_element_type=F32)
        picked = picked.astype(BF16)
        for i in range(step):
            for k in range(GROUP):
                outs[k][(r + i) * slots : (r + i + 1) * slots] = picked[
                    k * slots : (k + 1) * slots, i * shots : (i + 1) * shots
                ]


def residual_out_kernel(data, *refs):
    back, (residual, wide) = refs[:-2], refs[-2:]
    freq_count, _, block, _ = data.shape
    size = back[0].shape[0]
    piece = block // GROUP

    def keep(k, rows):
        wide[member_rows(k, size)] = rows.astype(F32)

    collect(back, keep)
    for f in range(freq_count):
        real, imag = data[f, 0].astype(F32), data[f, 1].astype(F32)
        for j in range(GROUP):
            at = slice(j * piece, (j + 1) * piece)
            first = j * size + f
            rows = pl.ds(first, piece, stride=freq_count)
            residual[f, 0, at, :] = real[at] - wide[rows, :]
            rows = pl.ds(first + piece * freq_count, piece, stride=freq_count)
            residual[f, 1, at, :] = imag[at] - wide[rows, :]


def gradient_kernel(source, freqs_hbm, *refs):
    parts, (gradient_hbm, gradient, wide, freqs, sems) = refs[:GROUP], refs[GROUP:]
    copy = pltpu.make_async_copy(freqs_hbm, freqs, sems.at[4])
    copy.start()
    slots, _, block, _ = gradient.shape
    size, shots = parts[0].shape
    height = size // slots
    piece = height // 2
    scale = 1.0 / shots
    for k in range(GROUP):
        wide[member_rows(k, size)] = parts[k][...].astype(F32)
    copy.wait()

    def one(t, carry):
        left = wide[pl.ds(t, GROUP * height, stride=slots), :].astype(BF16)
        right = source[freqs[t]].reshape(2 * block, shots)
        total = -scale * lax.dot_general(
            left, right, (((1,), (1,)), ((), ())), preferred_element_type=F32
        )
        real, imag = [], []
        for j in range(GROUP):
            upper = total[j * height : j * height + piece]
            lower = total[j * height + piece : (j + 1) * height]
            real.append(upper[:, :block] + lower[:, block:])
            imag.append(lower[:, :block] - upper[:, block:])
        gradient[t, 0] = jnp.concatenate(real, axis=0).astype(BF16)
        gradient[t, 1] = jnp.concatenate(imag, axis=0).astype(BF16)
        return carry

    copies = []
    quarters = 4
    step = slots // quarters
    for i in range(quarters):
        lax.fori_loop(i * step, (i + 1) * step, one, 0, unroll=4)
        at = pl.ds(i * step, step)
        copies.append(
            pltpu.make_async_copy(gradient.at[at], gradient_hbm.at[at], sems.at[i])
        )
        copies[-1].start()
    for copy in copies:
        copy.wait()


def per_device(data, wavelet, panel_block, tiles, cover_rows, cover_freqs):
    freq_count, _, block, shots = data.shape
    slots = tiles.shape[0]
    peers = lax.axis_size("tiles")
    groups = peers // GROUP
    height = 2 * block // GROUP
    span = GROUP * freq_count
    cap = 3 * span // 4 if groups == 2 else span
    sizes = (slots, groups, span, cap)

    def shape(*dims, kind=BF16):
        return jax.ShapeDtypeStruct((*dims, shots), kind)

    wide = pltpu.VMEM((GROUP * height * slots, shots), F32)
    wide_data = pltpu.VMEM((GROUP * height * freq_count, shots), F32)
    to_members = [jax.ShapeDtypeStruct((height * slots, shots), BF16)] * GROUP
    size = height * freq_count
    to_owners = [shape(size)] * 2 + [shape(2 * size)] * len(CHIPS)
    members = pltpu.VMEM((GROUP, height * freq_count, shots), BF16)

    def swap(value, distance):
        return lax.ppermute(value, "tiles", [(i, i ^ distance) for i in range(peers)])

    def in_group(values):
        got = {k: swap(values[k], k) for k in (6, 4, 2, 7, 5, 3, 1)}
        return [values[0]] + [got[k] for k in range(1, GROUP)]

    def hand_around(values):
        got = [swap(value, k) for value, k in zip(values[2:], CHIPS)]
        mate = call(relay_kernel, "for_mate", shape(4 * size), [VMEM] * (1 + len(CHIPS)))(
            values[1], *got
        )
        return [values[0], *got, swap(mate, 1)]

    def across(values):
        return [swap(value, q * GROUP) for q, value in enumerate(values, 1)]

    source, *sent = call(
        parts_kernel,
        "parts",
        [shape(freq_count, 2, block)] + [shape(height * slots + slots)] * GROUP,
        [HBM] * 6,
        scratch=[
            pltpu.VMEM(data.shape, BF16),
            pltpu.SMEM((2, freq_count), F32),
            pltpu.SMEM((1,), jnp.int32),
            pltpu.VMEM(tiles.shape, BF16),
            pltpu.SMEM((slots,), jnp.int32),
            pltpu.SMEM((slots,), jnp.int32),
            pltpu.SemaphoreType.DMA((6,)),
            wide,
        ],
    )(stay(data), stay(wavelet.T), panel_block, *map(stay, (tiles, cover_rows, cover_freqs)))
    rests = [shape(height, span - cap)] if groups == 2 else []
    if groups == 2:
        sends = [shape(height * cap + span)]
    else:
        sends = [shape(height, span)] * (groups - 1)
    hot, own, *out = call(
        functools.partial(sums_kernel, sizes),
        "sums",
        [
            jax.ShapeDtypeStruct((GROUP * slots, groups * span), BF16),
            shape(height, span, kind=F32),
        ]
        + sends
        + rests,
        [VMEM] * GROUP,
    )(*in_group(sent))
    got = [swap(out[0], GROUP)] if groups == 2 else across(out)
    data_in = in_group(
        call(slices_kernel, "data_slices", [shape(size)] * GROUP, [VMEM, ANY], scratch=[wide_data])(
            data, own
        )
    )
    if groups == 2:
        most = call(
            most_kernel,
            "most",
            jax.ShapeDtypeStruct((1,), jnp.int32),
            [ANY] * (2 + GROUP - 1),
            out_specs=SMEM,
            scratch=[pltpu.VMEM((16, shots), BF16)] * 2 + [pltpu.SemaphoreType.DMA((2,))],
        )(got[0], out[0], *data_in[1:])
        full = most[0] > cap

        def rest(value):
            return lax.cond(full, lambda v: swap(v, GROUP), jnp.zeros_like, value)

        got.append(rest(out[1]))
    rounded, *out = call(
        functools.partial(residual_kernel, sizes),
        "residual_slices",
        [shape(height, span)] + ([shape(height, cap)] + rests if groups == 2 else []) + to_owners,
        [VMEM] * (1 + len(data_in) + len(got)),
        scratch=[members, members],
    )(own, *data_in, *got)
    if groups == 2:
        got = [swap(out[0], GROUP), rest(out[1])]
    else:
        got = across([rounded] * (groups - 1))
    residual = call(
        residual_out_kernel,
        "residual",
        jax.ShapeDtypeStruct(data.shape, F32),
        [VMEM] * (1 + len(to_owners)),
        scratch=[wide_data],
    )(data, *hand_around(out[-len(to_owners) :]))
    out = call(
        functools.partial(spread_kernel, slots),
        "spread",
        to_members,
        [VMEM] * (2 + len(got)),
    )(hot, rounded, *got)
    gradient = call(
        gradient_kernel,
        "gradient",
        jax.ShapeDtypeStruct(tiles.shape, BF16),
        [VMEM, HBM] + [VMEM] * GROUP,
        out_specs=HBM,
        scratch=[
            pltpu.VMEM(tiles.shape, BF16),
            wide,
            pltpu.SMEM((slots,), jnp.int32),
            pltpu.SemaphoreType.DMA((5,)),
        ],
    )(source, stay(cover_freqs), *in_group(out))
    return residual, gradient


def solution(mesh):
    in_specs = (
        P("windows", None, "tiles", None),
        P(),
        P(),
        P(("windows", "tiles"), None, None, None),
        P(("windows", "tiles")),
        P(("windows", "tiles")),
    )
    out_specs = (P("windows", None, "tiles", None), P(("windows", "tiles"), None, None, None))
    return jax.shard_map(
        per_device, mesh=mesh, in_specs=in_specs, out_specs=out_specs, check_vma=False
    )
```

```python
import functools

import jax
import jax.numpy as jnp
from jax import lax
from jax.experimental import pallas as pl
from jax.experimental.pallas import tpu as pltpu
from jax.sharding import PartitionSpec as P

GROUP = 8
CHIPS = (2, 4, 6)
BF16 = jnp.bfloat16
F32 = jnp.float32
VMEM = pl.BlockSpec(memory_space=pltpu.VMEM)
SMEM = pl.BlockSpec(memory_space=pltpu.SMEM)
HBM = pl.BlockSpec(memory_space=pltpu.HBM)
ANY = pl.BlockSpec(memory_space=pl.ANY)


def call(kernel, name, out_shape, in_specs, scratch=(), out_specs=None, mib=24):
    return pl.pallas_call(
        kernel,
        name=name,
        out_shape=out_shape,
        in_specs=in_specs,
        out_specs=out_specs or jax.tree.map(lambda _: VMEM, out_shape),
        scratch_shapes=list(scratch),
        cost_estimate=pl.CostEstimate(flops=0, bytes_accessed=1 << 20, transcendentals=0),
        compiler_params=pltpu.CompilerParams(vmem_limit_bytes=mib * 1024 * 1024),
    )


def stay(array):
    return pltpu.with_memory_space_constraint(array, pltpu.HBM)


def in_hbm(shape):
    return pltpu.HBM(shape.shape, shape.dtype)


def local_index():
    return lax.rem(lax.axis_index("tiles"), GROUP)


def group_index():
    return lax.div(lax.axis_index("tiles"), GROUP)


def put(buffer, slot, count, real, imag):
    piece = real.shape[0] // GROUP
    for j in range(GROUP):
        at = slice(j * piece, (j + 1) * piece)
        first = 2 * j * piece * count + slot
        buffer[pl.ds(first, piece, stride=count), :] = real[at]
        buffer[pl.ds(first + piece * count, piece, stride=count), :] = imag[at]


def transposed_dot(left, right):
    return lax.dot_general(left, right, (((0,), (0,)), ((), ())), preferred_element_type=F32)


def member_rows(k, count):
    return pl.ds(pl.multiple_of((local_index() ^ k) * count, count), count)


def parts_kernel(data_hbm, wavelet_hbm, panel_hbm, tiles_hbm, rows_hbm, freqs_hbm, *refs):
    source, own_hbm, outs = refs[0], refs[1], refs[2 : 2 + GROUP]
    data, wavelet, panel, tiles, rows, freqs, sems, wide, own = refs[2 + GROUP :]
    freq_count, _, block, shots = data.shape
    slots = tiles.shape[0]
    size = 2 * block // GROUP * slots
    half = lax.axis_size("tiles") * freq_count // 2
    pairs = (
        (data_hbm, data),
        (tiles_hbm, tiles),
        (wavelet_hbm, wavelet),
        (panel_hbm, panel),
        (freqs_hbm, freqs),
        (rows_hbm, rows),
    )
    copies = [pltpu.make_async_copy(*pair, sems.at[i]) for i, pair in enumerate(pairs)]
    for copy in copies:
        copy.start()
    diagonal = (
        lax.broadcasted_iota(jnp.int32, (block, shots), 0)
        == lax.broadcasted_iota(jnp.int32, (block, shots), 1)
    ).astype(F32)
    for i in (2, 3, 4, 5, 0):
        copies[i].wait()
    identity = diagonal * (lax.axis_index("tiles") == panel[0]).astype(F32)
    for f in range(freq_count):
        source[f, 0] = (wavelet[0, f] * identity - data[f, 0].astype(F32)).astype(BF16)
        source[f, 1] = (wavelet[1, f] * identity - data[f, 1].astype(F32)).astype(BF16)
    piece = block // GROUP
    mine = pl.ds(pl.multiple_of(local_index() * piece, piece), piece)
    for f in range(freq_count):
        for x in range(2):
            at = pl.ds(x * piece * freq_count + f, piece, stride=freq_count)
            wide[at, :] = data[f, x, mine, :].astype(F32)
    own[...] = wide[: own.shape[0]].astype(BF16)
    own_copy = pltpu.make_async_copy(own, own_hbm, sems.at[6])
    own_copy.start()
    line = lax.broadcasted_iota(jnp.int32, (slots, shots), 0)
    targets = jnp.zeros((slots, shots), jnp.int32)
    for t in range(slots):
        targets = jnp.where(line == t, rows[t] * freq_count + freqs[t] - half, targets)
    for k in range(GROUP):
        outs[k][size:] = targets.astype(F32).astype(BF16)
    copies[1].wait()

    def one(t, carry):
        f = freqs[t]
        left = tiles[t].reshape(2 * block, block)
        right = jnp.concatenate([source[f, 0], source[f, 1]], axis=1)
        product = jnp.dot(left, right, preferred_element_type=F32)
        real = product[:block, :shots] - product[block:, shots:]
        put(wide, t, slots, real, product[:block, shots:] + product[block:, :shots])
        return carry

    lax.fori_loop(0, slots, one, 0, unroll=16)
    for k in range(GROUP):
        outs[k][:size] = wide[member_rows(k, size)].astype(BF16)
    own_copy.wait()


def sums_kernel(sizes, *refs):
    slots, groups, span, cap = sizes
    parts, (hot_hbm, own, *sends, hot_out, rest, sems) = refs[:GROUP], refs[GROUP:]
    height, _, shots = own.shape
    count = GROUP * slots
    group = group_index()
    targets = jnp.concatenate([part[height * slots :] for part in parts], axis=0).astype(F32)
    lane = lax.broadcasted_iota(jnp.int32, (count, shots), 1)
    hot = []
    for q in range(0, groups, shots // span):
        here = jnp.zeros((count, shots), jnp.int32)
        for i in range(shots // span):
            inside = lane - i * span + (group ^ (q + i)) * span - groups * span // 2
            here = jnp.where(lane >= i * span, inside, here)
        hot.append((targets == here.astype(F32)).astype(F32).astype(BF16))
    if groups == 2:
        other = hot[0][:, span:]
        used = (transposed_dot(other, jnp.ones((count, shots), BF16)) > 0).astype(F32)
        before = (
            lax.broadcasted_iota(jnp.int32, (span, span), 0)
            > lax.broadcasted_iota(jnp.int32, (span, span), 1)
        ).astype(F32)
        rank = jnp.dot(before.astype(BF16), used.astype(BF16), preferred_element_type=F32)
        slot = lax.broadcasted_iota(jnp.int32, (span, shots), 1).astype(F32)
        chosen = jnp.where(rank == slot, used, 0.0)
        number = jnp.sum(used, axis=0, keepdims=True)
        sends[0][height * cap :] = jnp.where(slot < span, chosen, number).astype(BF16)
        moved = jnp.dot(other, chosen[:, :span].astype(BF16), preferred_element_type=F32)
        hot = [jnp.concatenate([hot[0][:, :span], moved.astype(BF16)], axis=1)]
    hot = jnp.concatenate(hot, axis=1) if len(hot) > 1 else hot[0]
    hot_out[...] = hot
    copies = [pltpu.make_async_copy(hot_out, hot_hbm, sems.at[0])]
    copies[0].start()
    step = 2
    for r in range(0, height, step):
        rows = [
            jnp.concatenate([part[(r + i) * slots : (r + i + 1) * slots] for part in parts], axis=0)
            for i in range(step)
        ]
        total = transposed_dot(hot, jnp.concatenate(rows, axis=1))
        for i in range(step):
            values = total[:, i * shots : (i + 1) * shots]
            own[r + i] = values[:span]
            if groups == 2:
                at = slice((r + i) * cap, (r + i + 1) * cap)
                sends[0][at] = values[span : span + cap].astype(BF16)
                rest[r + i] = values[span + cap :].astype(BF16)
            else:
                for q, send in enumerate(sends, 1):
                    send[r + i] = values[q * span : (q + 1) * span].astype(BF16)
    if groups == 2:
        copies.append(pltpu.make_async_copy(rest, sends[1], sems.at[1]))
        copies[1].start()
    for copy in copies:
        copy.wait()


def hand_out(outs, rows):
    size = outs[0].shape[0]
    outs[0][...] = rows(0)
    outs[1][...] = rows(1)
    for out, k in zip(outs[2:], CHIPS):
        out[:size] = rows(k)
        out[size:] = rows(k ^ 1)


def collect(refs, rows):
    own, *got, mate = refs
    size = own.shape[0]
    rows(0, own[...])
    rows(1, mate[:size])
    for i, k in enumerate(CHIPS):
        rows(k, got[i][:size])
        rows(k ^ 1, mate[(i + 1) * size : (i + 2) * size])


def relay_kernel(own, *refs):
    got, out = refs[:-1], refs[-1]
    size = own.shape[0]
    out[:size] = own[...]
    for i, ref in enumerate(got, 1):
        out[i * size : (i + 1) * size] = ref[size:]


def most_kernel(got, mine, *refs):
    out = refs[-1]
    last = slice(got.shape[0] - 16, got.shape[0])
    half = got.shape[1] // 2
    most = jnp.maximum(got[last, half:].astype(F32), mine[last, half:].astype(F32))
    out[0] = jnp.max(most).astype(jnp.int32)


def slices_kernel(data, _, *refs):
    outs, wide = refs[:-1], refs[-1]
    freq_count = data.shape[0]
    for f in range(freq_count):
        put(wide, f, freq_count, data[f, 0].astype(F32), data[f, 1].astype(F32))
    for k, out in enumerate(outs, 1):
        out[...] = wide[member_rows(k, out.shape[0])].astype(BF16)


def fetch_rest(full, got_rest_any, got_rest, sem):
    @pl.when(full)
    def _():
        copy = pltpu.make_async_copy(got_rest_any, got_rest, sem)
        copy.start()
        copy.wait()

    @pl.when(jnp.logical_not(full))
    def _():
        got_rest[...] = jnp.zeros_like(got_rest)


def residual_kernel(sizes, own, *refs):
    slots, groups, span, cap = sizes
    height, _, shots = own.shape
    data_in, refs = refs[:GROUP], refs[GROUP:]
    if groups == 2:
        most, got, got_rest_any, rounded, send, rest_hbm, *outs = refs[:-6]
        data, back, total, sems, got_rest, rest = refs[-6:]
        chosen = got[height * cap :, :span]
        full = most[0] > cap
    else:
        got, (rounded, *outs, data, back, total, sems) = refs[: groups - 1], refs[groups - 1 :]
    local = local_index()
    freq_count = data.shape[1] // height
    own_copy = pltpu.make_async_copy(data_in[0], data.at[local], sems.at[0])
    own_copy.start()
    if groups == 2:

        fetch_rest(full, got_rest_any, got_rest, sems.at[1])
    for k in range(1, GROUP):
        data[local ^ k] = data_in[k][...]
    step = 8
    for r in range(0, height, step):
        rows = range(r, r + step)
        values = jnp.concatenate([own[i] for i in rows], axis=1)
        if groups == 2:
            more = []
            for i in rows:
                used = got[i * cap : (i + 1) * cap]
                more.append(jnp.concatenate([used, got_rest[i]], axis=0))
            more = jnp.concatenate(more, axis=1)
            values += jnp.dot(chosen, more, preferred_element_type=F32)
        else:
            for ref in got:
                values += jnp.concatenate([ref[i].astype(F32) for i in rows], axis=1)
        total[:, r * shots : (r + step) * shots] = values
        for j in range(GROUP):
            at = slice(j * freq_count, (j + 1) * freq_count)
            pair = [values[at, i * shots : (i + 1) * shots] for i in range(step)]
            pair = jnp.concatenate(pair, axis=0)
            back[j, r * freq_count : (r + step) * freq_count] = pair.astype(BF16)
    own_copy.wait()
    for r in range(0, height, step):
        rows = range(r, r + step)
        values = data[:, r * freq_count : (r + step) * freq_count].astype(F32)
        values = [
            values[:, i * freq_count : (i + 1) * freq_count].reshape(span, shots)
            for i in range(step)
        ]
        values = jnp.concatenate(values, axis=1) - total[:, r * shots : (r + step) * shots]
        values = values.astype(BF16)
        picked = transposed_dot(chosen, values).astype(BF16) if groups == 2 else None
        for i in rows:
            at = slice((i - r) * shots, (i - r + 1) * shots)
            rounded[i] = values[:, at]
            if groups == 2:
                send[i * cap : (i + 1) * cap] = picked[:cap, at]
                rest[i] = picked[cap:, at]
    if groups == 2:

        @pl.when(full)
        def _():
            copy = pltpu.make_async_copy(rest, rest_hbm, sems.at[1])
            copy.start()
            copy.wait()

    hand_out(outs, lambda k: back[local ^ k])


def spread_kernel(sizes, hot, rounded, *refs):
    slots, groups, span, cap = sizes
    height, _, shots = rounded.shape
    if groups == 2:
        most, got, got_rest_any, *outs, got_rest, sem = refs
        fetch_rest(most[0] > cap, got_rest_any, got_rest, sem)
    else:
        got, outs = refs[: groups - 1], refs[groups - 1 :]
    step = 8
    for r in range(0, height, step):
        rows = []
        for i in range(r, r + step):
            if groups == 2:
                row = [rounded[i], got[i * cap : (i + 1) * cap], got_rest[i]]
            else:
                row = [rounded[i]] + [ref[i] for ref in got]
            rows.append(jnp.concatenate(row, axis=0))
        picked = jnp.dot(hot[...], jnp.concatenate(rows, axis=1), preferred_element_type=F32)
        picked = picked.astype(BF16)
        for i in range(step):
            for k in range(GROUP):
                outs[k][(r + i) * slots : (r + i + 1) * slots] = picked[
                    k * slots : (k + 1) * slots, i * shots : (i + 1) * shots
                ]


def residual_out_kernel(data, *refs):
    back, (residual, wide) = refs[:-2], refs[-2:]
    freq_count, _, block, _ = data.shape
    size = back[0].shape[0]
    piece = block // GROUP

    def keep(k, rows):
        wide[member_rows(k, size)] = rows.astype(F32)

    collect(back, keep)
    for f in range(freq_count):
        real, imag = data[f, 0].astype(F32), data[f, 1].astype(F32)
        for j in range(GROUP):
            at = slice(j * piece, (j + 1) * piece)
            first = j * size + f
            rows = pl.ds(first, piece, stride=freq_count)
            residual[f, 0, at, :] = real[at] - wide[rows, :]
            rows = pl.ds(first + piece * freq_count, piece, stride=freq_count)
            residual[f, 1, at, :] = imag[at] - wide[rows, :]


def gradient_kernel(source, freqs_hbm, *refs):
    parts, (gradient_hbm, gradient, wide, freqs, sems) = refs[:GROUP], refs[GROUP:]
    copy = pltpu.make_async_copy(freqs_hbm, freqs, sems.at[4])
    copy.start()
    slots, _, block, _ = gradient.shape
    size, shots = parts[0].shape
    height = size // slots
    piece = height // 2
    scale = 1.0 / shots
    for k in range(GROUP):
        wide[member_rows(k, size)] = parts[k][...].astype(F32)
    copy.wait()

    def one(t, carry):
        left = wide[pl.ds(t, GROUP * height, stride=slots), :].astype(BF16)
        right = source[freqs[t]].reshape(2 * block, shots)
        total = -scale * lax.dot_general(
            left, right, (((1,), (1,)), ((), ())), preferred_element_type=F32
        )
        real, imag = [], []
        for j in range(GROUP):
            upper = total[j * height : j * height + piece]
            lower = total[j * height + piece : (j + 1) * height]
            real.append(upper[:, :block] + lower[:, block:])
            imag.append(lower[:, :block] - upper[:, block:])
        gradient[t, 0] = jnp.concatenate(real, axis=0).astype(BF16)
        gradient[t, 1] = jnp.concatenate(imag, axis=0).astype(BF16)
        return carry

    copies = []
    quarters = 4
    step = slots // quarters
    for i in range(quarters):
        lax.fori_loop(i * step, (i + 1) * step, one, 0, unroll=4)
        at = pl.ds(i * step, step)
        copies.append(
            pltpu.make_async_copy(gradient.at[at], gradient_hbm.at[at], sems.at[i])
        )
        copies[-1].start()
    for copy in copies:
        copy.wait()


def per_device(data, wavelet, panel_block, tiles, cover_rows, cover_freqs):
    freq_count, _, block, shots = data.shape
    slots = tiles.shape[0]
    peers = lax.axis_size("tiles")
    groups = peers // GROUP
    height = 2 * block // GROUP
    span = GROUP * freq_count
    cap = 3 * span // 4 if groups == 2 else span
    sizes = (slots, groups, span, cap)

    def shape(*dims, kind=BF16):
        return jax.ShapeDtypeStruct((*dims, shots), kind)

    wide = pltpu.VMEM((GROUP * height * slots, shots), F32)
    wide_data = pltpu.VMEM((GROUP * height * freq_count, shots), F32)
    to_members = [jax.ShapeDtypeStruct((height * slots, shots), BF16)] * GROUP
    size = height * freq_count
    to_owners = [shape(size)] * 2 + [shape(2 * size)] * len(CHIPS)
    members = pltpu.VMEM((GROUP, height * freq_count, shots), BF16)

    def swap(value, distance):
        return lax.ppermute(value, "tiles", [(i, i ^ distance) for i in range(peers)])

    def in_group(values):
        got = {k: swap(values[k], k) for k in (6, 4, 2, 7, 5, 3, 1)}
        return [values[0]] + [got[k] for k in range(1, GROUP)]

    def hand_around(values):
        got = [swap(value, k) for value, k in zip(values[2:], CHIPS)]
        mate = call(relay_kernel, "for_mate", shape(4 * size), [VMEM] * (1 + len(CHIPS)))(
            values[1], *got
        )
        return [values[0], *got, swap(mate, 1)]

    def across(values):
        return [swap(value, q * GROUP) for q, value in enumerate(values, 1)]

    source, own_data, *sent = call(
        parts_kernel,
        "parts",
        [shape(freq_count, 2, block), in_hbm(shape(size))]
        + [shape(height * slots + slots)] * GROUP,
        [HBM] * 6,
        out_specs=[VMEM, HBM] + [VMEM] * GROUP,
        scratch=[
            pltpu.VMEM(data.shape, BF16),
            pltpu.SMEM((2, freq_count), F32),
            pltpu.SMEM((1,), jnp.int32),
            pltpu.VMEM(tiles.shape, BF16),
            pltpu.SMEM((slots,), jnp.int32),
            pltpu.SMEM((slots,), jnp.int32),
            pltpu.SemaphoreType.DMA((7,)),
            wide,
            pltpu.VMEM((size, shots), BF16),
        ],
    )(stay(data), stay(wavelet.T), panel_block, *map(stay, (tiles, cover_rows, cover_freqs)))
    rests = [in_hbm(shape(height, span - cap))] if groups == 2 else []
    rest_rows = [pltpu.VMEM((height, span - cap, shots), BF16)] * len(rests)
    if groups == 2:
        sends = [shape(height * cap + span)]
    else:
        sends = [shape(height, span)] * (groups - 1)
    hot, own, *out = call(
        functools.partial(sums_kernel, sizes),
        "sums",
        [pltpu.HBM((GROUP * slots, groups * span), BF16), shape(height, span, kind=F32)]
        + sends
        + rests,
        [VMEM] * GROUP,
        out_specs=[HBM] + [VMEM] * (1 + len(sends)) + [HBM] * len(rests),
        scratch=[
            pltpu.VMEM((GROUP * slots, groups * span), BF16),
            pltpu.VMEM((height, max(span - cap, 16), shots), BF16),
            pltpu.SemaphoreType.DMA((2,)),
        ],
    )(*in_group(sent))
    got = [swap(out[0], GROUP)] if groups == 2 else across(out)
    data_out = call(
        slices_kernel, "data_slices", [shape(size)] * (GROUP - 1), [VMEM, ANY], scratch=[wide_data]
    )(data, own)
    data_in = in_group([own_data, *data_out])
    if groups == 2:
        most = call(
            most_kernel,
            "most",
            pltpu.SMEM((1,), jnp.int32),
            [VMEM] * 2 + [ANY] * (GROUP - 1),
            out_specs=SMEM,
        )(got[0], out[0], *data_in[1:])
        full = most[0] > cap

        def rest(value):
            return lax.cond(full, lambda v: swap(v, GROUP), jnp.zeros_like, value)

        got = [most, *got, rest(out[1])]
    rounded, *out = call(
        functools.partial(residual_kernel, sizes),
        "residual_slices",
        [shape(height, span)] + [shape(height * cap)] * len(rests) + rests + to_owners,
        [VMEM, HBM]
        + [VMEM] * (GROUP - 1)
        + ([SMEM, VMEM, ANY] if groups == 2 else [VMEM] * len(got)),
        out_specs=[VMEM] * (1 + len(rests)) + [HBM] * len(rests) + [VMEM] * len(to_owners),
        scratch=[
            members,
            members,
            pltpu.VMEM((span, height * shots), F32),
            pltpu.SemaphoreType.DMA((2,)),
        ]
        + rest_rows * 2,
    )(own, stay(data_in[0]), *data_in[1:], *got)
    if groups == 2:
        got = [most, swap(out[0], GROUP), rest(out[1])]
    else:
        got = across([rounded] * (groups - 1))
    residual = call(
        residual_out_kernel,
        "residual",
        jax.ShapeDtypeStruct(data.shape, F32),
        [VMEM] * (1 + len(to_owners)),
        scratch=[wide_data],
    )(data, *hand_around(out[-len(to_owners) :]))
    out = call(
        functools.partial(spread_kernel, sizes),
        "spread",
        to_members,
        [VMEM] * 2 + ([SMEM, VMEM, ANY] if groups == 2 else [VMEM] * len(got)),
        scratch=rest_rows + [pltpu.SemaphoreType.DMA] * len(rests),
    )(hot, rounded, *got)
    gradient = call(
        gradient_kernel,
        "gradient",
        jax.ShapeDtypeStruct(tiles.shape, BF16),
        [VMEM, HBM] + [VMEM] * GROUP,
        out_specs=HBM,
        scratch=[
            pltpu.VMEM(tiles.shape, BF16),
            wide,
            pltpu.SMEM((slots,), jnp.int32),
            pltpu.SemaphoreType.DMA((5,)),
        ],
    )(source, stay(cover_freqs), *in_group(out))
    return residual, gradient


def solution(mesh):
    in_specs = (
        P("windows", None, "tiles", None),
        P(),
        P(),
        P(("windows", "tiles"), None, None, None),
        P(("windows", "tiles")),
        P(("windows", "tiles")),
    )
    out_specs = (P("windows", None, "tiles", None), P(("windows", "tiles"), None, None, None))
    return jax.shard_map(
        per_device, mesh=mesh, in_specs=in_specs, out_specs=out_specs, check_vma=False
    )
```

```python
import functools

import jax
import jax.numpy as jnp
from jax import lax
from jax.experimental import pallas as pl
from jax.experimental.pallas import tpu as pltpu
from jax.sharding import PartitionSpec as P

GROUP = 8
TABLE = 16
CHIPS = (2, 4, 6)
BF16 = jnp.bfloat16
F32 = jnp.float32
VMEM = pl.BlockSpec(memory_space=pltpu.VMEM)
SMEM = pl.BlockSpec(memory_space=pltpu.SMEM)
HBM = pl.BlockSpec(memory_space=pltpu.HBM)
ANY = pl.BlockSpec(memory_space=pl.ANY)


def call(kernel, name, out_shape, in_specs, scratch=(), out_specs=None, mib=24):
    return pl.pallas_call(
        kernel,
        name=name,
        out_shape=out_shape,
        in_specs=in_specs,
        out_specs=out_specs or jax.tree.map(lambda _: VMEM, out_shape),
        scratch_shapes=list(scratch),
        cost_estimate=pl.CostEstimate(flops=0, bytes_accessed=1 << 20, transcendentals=0),
        compiler_params=pltpu.CompilerParams(vmem_limit_bytes=mib * 1024 * 1024),
    )


def stay(array):
    return pltpu.with_memory_space_constraint(array, pltpu.HBM)


def in_hbm(shape):
    return pltpu.HBM(shape.shape, shape.dtype)


def local_index():
    return lax.rem(lax.axis_index("tiles"), GROUP)


def group_index():
    return lax.div(lax.axis_index("tiles"), GROUP)


def put(buffer, slot, count, real, imag):
    piece = real.shape[0] // GROUP
    for j in range(GROUP):
        at = slice(j * piece, (j + 1) * piece)
        first = 2 * j * piece * count + slot
        buffer[pl.ds(first, piece, stride=count), :] = real[at]
        buffer[pl.ds(first + piece * count, piece, stride=count), :] = imag[at]


def transposed_dot(left, right):
    return lax.dot_general(left, right, (((0,), (0,)), ((), ())), preferred_element_type=F32)


def member_rows(k, count):
    return pl.ds(pl.multiple_of((local_index() ^ k) * count, count), count)


def parts_kernel(data_hbm, wavelet_hbm, panel_hbm, tiles_hbm, rows_hbm, freqs_hbm, *refs):
    source, own_hbm, freqs_out, outs = *refs[:3], refs[3 : 3 + GROUP]
    data, wavelet, panel, tiles, rows, freqs, sems, wide, own = refs[3 + GROUP :]
    freq_count, _, block, shots = data.shape
    slots = tiles.shape[0]
    size = 2 * block // GROUP * slots
    half = lax.axis_size("tiles") * freq_count // 2
    pairs = (
        (data_hbm, data),
        (tiles_hbm, tiles),
        (wavelet_hbm, wavelet),
        (panel_hbm, panel),
        (freqs_hbm, freqs),
        (rows_hbm, rows),
    )
    copies = [pltpu.make_async_copy(*pair, sems.at[i]) for i, pair in enumerate(pairs)]
    for copy in copies:
        copy.start()
    diagonal = (
        lax.broadcasted_iota(jnp.int32, (block, shots), 0)
        == lax.broadcasted_iota(jnp.int32, (block, shots), 1)
    ).astype(F32)
    for i in (2, 3, 4, 5, 0):
        copies[i].wait()
    identity = diagonal * (lax.axis_index("tiles") == panel[0]).astype(F32)
    for f in range(freq_count):
        source[f, 0] = (wavelet[0, f] * identity - data[f, 0].astype(F32)).astype(BF16)
        source[f, 1] = (wavelet[1, f] * identity - data[f, 1].astype(F32)).astype(BF16)
    piece = block // GROUP
    mine = pl.ds(pl.multiple_of(local_index() * piece, piece), piece)
    for f in range(freq_count):
        for x in range(2):
            at = pl.ds(x * piece * freq_count + f, piece, stride=freq_count)
            wide[at, :] = data[f, x, mine, :].astype(F32)
    own[...] = wide[: own.shape[0]].astype(BF16)
    own_copy = pltpu.make_async_copy(own, own_hbm, sems.at[6])
    own_copy.start()
    line = lax.broadcasted_iota(jnp.int32, (slots, shots), 0)
    targets = jnp.zeros((slots, shots), jnp.int32)
    for t in range(slots):
        freqs_out[t] = freqs[t]
        targets = jnp.where(line == t, rows[t] * freq_count + freqs[t] - half, targets)
    for k in range(GROUP):
        outs[k][size:] = targets.astype(F32).astype(BF16)
    copies[1].wait()

    def one(t, carry):
        f = freqs[t]
        left = tiles[t].reshape(2 * block, block)
        right = jnp.concatenate([source[f, 0], source[f, 1]], axis=1)
        product = jnp.dot(left, right, preferred_element_type=F32)
        real = product[:block, :shots] - product[block:, shots:]
        put(wide, t, slots, real, product[:block, shots:] + product[block:, :shots])
        return carry

    lax.fori_loop(0, slots, one, 0, unroll=16)
    for k in range(GROUP):
        outs[k][:size] = wide[member_rows(k, size)].astype(BF16)
    own_copy.wait()


def sums_kernel(sizes, *refs):
    slots, groups, span, cap = sizes
    parts, (hot_out, own, *sends) = refs[:GROUP], refs[GROUP:]
    height, _, shots = own.shape
    count = GROUP * slots
    group = group_index()
    targets = jnp.concatenate([part[height * slots :] for part in parts], axis=0).astype(F32)
    lane = lax.broadcasted_iota(jnp.int32, (count, shots), 1)
    hot = []
    for q in range(0, groups, shots // span):
        here = jnp.zeros((count, shots), jnp.int32)
        for i in range(shots // span):
            inside = lane - i * span + (group ^ (q + i)) * span - groups * span // 2
            here = jnp.where(lane >= i * span, inside, here)
        hot.append((targets == here.astype(F32)).astype(F32).astype(BF16))
    if groups == 2:
        other = hot[0][:, span:]
        used = (transposed_dot(other, jnp.ones((count, shots), BF16)) > 0).astype(F32)
        before = (
            lax.broadcasted_iota(jnp.int32, (span, span), 0)
            > lax.broadcasted_iota(jnp.int32, (span, span), 1)
        ).astype(F32)
        rank = jnp.dot(before.astype(BF16), used.astype(BF16), preferred_element_type=F32)
        slot = lax.broadcasted_iota(jnp.int32, (span, shots), 1).astype(F32)
        chosen = jnp.where(rank == slot, used, 0.0)
        number = jnp.sum(used, axis=0, keepdims=True)
        target = lax.broadcasted_iota(jnp.int32, (span, shots), 0).astype(F32) + 1.0
        listed = jnp.sum(chosen * target, axis=0, keepdims=True)
        listed = jnp.where(slot[:TABLE] < span, listed, number)
        sends[0][height * cap :] = listed.astype(BF16)
        moved = jnp.dot(other, chosen[:, :span].astype(BF16), preferred_element_type=F32)
        hot = [jnp.concatenate([hot[0][:, :span], moved.astype(BF16)], axis=1)]
    hot = jnp.concatenate(hot, axis=1) if len(hot) > 1 else hot[0]
    hot_out[...] = hot
    step = 4
    for r in range(0, height, step):
        rows = [
            jnp.concatenate([part[(r + i) * slots : (r + i + 1) * slots] for part in parts], axis=0)
            for i in range(step)
        ]
        total = transposed_dot(hot, jnp.concatenate(rows, axis=1))
        for i in range(step):
            values = total[:, i * shots : (i + 1) * shots]
            own[r + i] = values[:span]
            if groups == 2:
                at = slice((r + i) * cap, (r + i + 1) * cap)
                sends[0][at] = values[span : span + cap].astype(BF16)
                sends[1][r + i] = values[span + cap :].astype(BF16)
            else:
                for q, send in enumerate(sends, 1):
                    send[r + i] = values[q * span : (q + 1) * span].astype(BF16)


def hand_out(outs, rows):
    size = outs[0].shape[0]
    outs[0][...] = rows(0)
    outs[1][...] = rows(1)
    for out, k in zip(outs[2:], CHIPS):
        out[:size] = rows(k)
        out[size:] = rows(k ^ 1)


def collect(refs, rows):
    own, *got, mate = refs
    size = own.shape[0]
    rows(0, own[...])
    rows(1, mate[:size])
    for i, k in enumerate(CHIPS):
        rows(k, got[i][:size])
        rows(k ^ 1, mate[(i + 1) * size : (i + 2) * size])


def relay_kernel(own, *refs):
    got, out = refs[:-1], refs[-1]
    size = own.shape[0]
    out[:size] = own[...]
    for i, ref in enumerate(got, 1):
        out[i * size : (i + 1) * size] = ref[size:]


def most_kernel(got, mine, *refs):
    out = refs[-1]
    last = slice(got.shape[0] - TABLE, got.shape[0])
    half = got.shape[1] // 2
    most = jnp.maximum(got[last, half:].astype(F32), mine[last, half:].astype(F32))
    out[0] = jnp.max(most).astype(jnp.int32)


def slices_kernel(data, _, *refs):
    *refs, wide, sems = refs
    count = (len(refs) - GROUP + 1) // 2
    waiting, stored, outs = refs[:count], refs[count : 2 * count], refs[2 * count :]
    copies = [
        pltpu.make_async_copy(src, dst, sems.at[i])
        for i, (src, dst) in enumerate(zip(waiting, stored))
    ]
    for copy in copies:
        copy.start()
    freq_count = data.shape[0]
    for f in range(freq_count):
        put(wide, f, freq_count, data[f, 0].astype(F32), data[f, 1].astype(F32))
    for k, out in enumerate(outs, 1):
        out[...] = wide[member_rows(k, out.shape[0])].astype(BF16)
    for copy in copies:
        copy.wait()


def fetch_rest(full, got_rest_any, got_rest, sem):
    @pl.when(full)
    def _():
        copy = pltpu.make_async_copy(got_rest_any, got_rest, sem)
        copy.start()
        copy.wait()

    @pl.when(jnp.logical_not(full))
    def _():
        got_rest[...] = jnp.zeros_like(got_rest)


def residual_kernel(sizes, own, *refs):
    slots, groups, span, cap = sizes
    height, _, shots = own.shape
    data_in, refs = refs[:GROUP], refs[GROUP:]
    if groups == 2:
        most, got, got_rest_any, rounded, send, rest_hbm, *outs = refs[:-6]
        data, back, total, sems, got_rest, rest = refs[-6:]
        target = lax.broadcasted_iota(jnp.int32, (span, span), 0).astype(F32) + 1.0
        listed = got[height * cap :, :span].astype(F32)[:1]
        chosen = (listed == target).astype(F32).astype(BF16)
        full = most[0] > cap
    else:
        got, (rounded, *outs, data, back, total, sems) = refs[: groups - 1], refs[groups - 1 :]
    local = local_index()
    freq_count = data.shape[1] // height
    own_copy = pltpu.make_async_copy(data_in[0], data.at[local], sems.at[0])
    own_copy.start()
    if groups == 2:

        fetch_rest(full, got_rest_any, got_rest, sems.at[1])
    for k in range(1, GROUP):
        data[local ^ k] = data_in[k][...]
    step = 8
    for r in range(0, height, step):
        rows = range(r, r + step)
        values = jnp.concatenate([own[i] for i in rows], axis=1)
        if groups == 2:
            more = []
            for i in rows:
                used = got[i * cap : (i + 1) * cap]
                more.append(jnp.concatenate([used, got_rest[i]], axis=0))
            more = jnp.concatenate(more, axis=1)
            values += jnp.dot(chosen, more, preferred_element_type=F32)
        else:
            for ref in got:
                values += jnp.concatenate([ref[i].astype(F32) for i in rows], axis=1)
        total[:, r * shots : (r + step) * shots] = values
        for j in range(GROUP):
            at = slice(j * freq_count, (j + 1) * freq_count)
            pair = [values[at, i * shots : (i + 1) * shots] for i in range(step)]
            pair = jnp.concatenate(pair, axis=0)
            back[j, r * freq_count : (r + step) * freq_count] = pair.astype(BF16)
    own_copy.wait()
    for r in range(0, height, step):
        rows = range(r, r + step)
        values = data[:, r * freq_count : (r + step) * freq_count].astype(F32)
        values = [
            values[:, i * freq_count : (i + 1) * freq_count].reshape(span, shots)
            for i in range(step)
        ]
        values = jnp.concatenate(values, axis=1) - total[:, r * shots : (r + step) * shots]
        values = values.astype(BF16)
        picked = transposed_dot(chosen, values).astype(BF16) if groups == 2 else None
        for i in rows:
            at = slice((i - r) * shots, (i - r + 1) * shots)
            rounded[i] = values[:, at]
            if groups == 2:
                send[i * cap : (i + 1) * cap] = picked[:cap, at]
                rest[i] = picked[cap:, at]
    if groups == 2:

        @pl.when(full)
        def _():
            copy = pltpu.make_async_copy(rest, rest_hbm, sems.at[1])
            copy.start()
            copy.wait()

    hand_out(outs, lambda k: back[local ^ k])


def spread_kernel(sizes, hot, rounded, *refs):
    slots, groups, span, cap = sizes
    height, _, shots = rounded.shape
    if groups == 2:
        most, got, got_rest_any, *outs, got_rest, sem = refs
        fetch_rest(most[0] > cap, got_rest_any, got_rest, sem)
    else:
        got, outs = refs[: groups - 1], refs[groups - 1 :]
    step = 8
    for r in range(0, height, step):
        rows = []
        for i in range(r, r + step):
            if groups == 2:
                row = [rounded[i], got[i * cap : (i + 1) * cap], got_rest[i]]
            else:
                row = [rounded[i]] + [ref[i] for ref in got]
            rows.append(jnp.concatenate(row, axis=0))
        picked = jnp.dot(hot[...], jnp.concatenate(rows, axis=1), preferred_element_type=F32)
        picked = picked.astype(BF16)
        for i in range(step):
            for k in range(GROUP):
                outs[k][(r + i) * slots : (r + i + 1) * slots] = picked[
                    k * slots : (k + 1) * slots, i * shots : (i + 1) * shots
                ]


def residual_out_kernel(data, *refs):
    back, (residual, wide) = refs[:-2], refs[-2:]
    freq_count, _, block, _ = data.shape
    size = back[0].shape[0]
    piece = block // GROUP

    def keep(k, rows):
        wide[member_rows(k, size)] = rows.astype(F32)

    collect(back, keep)
    for f in range(freq_count):
        real, imag = data[f, 0].astype(F32), data[f, 1].astype(F32)
        for j in range(GROUP):
            at = slice(j * piece, (j + 1) * piece)
            first = j * size + f
            rows = pl.ds(first, piece, stride=freq_count)
            residual[f, 0, at, :] = real[at] - wide[rows, :]
            rows = pl.ds(first + piece * freq_count, piece, stride=freq_count)
            residual[f, 1, at, :] = imag[at] - wide[rows, :]


def gradient_kernel(source, freqs, *refs):
    parts, (gradient_hbm, gradient, wide, sems) = refs[:GROUP], refs[GROUP:]
    slots, _, block, _ = gradient.shape
    size, shots = parts[0].shape
    height = size // slots
    piece = height // 2
    scale = 1.0 / shots
    for k in range(GROUP):
        wide[member_rows(k, size)] = parts[k][...].astype(F32)

    def one(t, carry):
        left = wide[pl.ds(t, GROUP * height, stride=slots), :].astype(BF16)
        right = source[freqs[t]].reshape(2 * block, shots)
        total = -scale * lax.dot_general(
            left, right, (((1,), (1,)), ((), ())), preferred_element_type=F32
        )
        real, imag = [], []
        for j in range(GROUP):
            upper = total[j * height : j * height + piece]
            lower = total[j * height + piece : (j + 1) * height]
            real.append(upper[:, :block] + lower[:, block:])
            imag.append(lower[:, :block] - upper[:, block:])
        gradient[t, 0] = jnp.concatenate(real, axis=0).astype(BF16)
        gradient[t, 1] = jnp.concatenate(imag, axis=0).astype(BF16)
        return carry

    copies = []
    quarters = 4
    step = slots // quarters
    for i in range(quarters):
        lax.fori_loop(i * step, (i + 1) * step, one, 0, unroll=4)
        at = pl.ds(i * step, step)
        copies.append(
            pltpu.make_async_copy(gradient.at[at], gradient_hbm.at[at], sems.at[i])
        )
        copies[-1].start()
    for copy in copies:
        copy.wait()


def per_device(data, wavelet, panel_block, tiles, cover_rows, cover_freqs):
    freq_count, _, block, shots = data.shape
    slots = tiles.shape[0]
    peers = lax.axis_size("tiles")
    groups = peers // GROUP
    height = 2 * block // GROUP
    span = GROUP * freq_count
    cap = 3 * span // 4 if groups == 2 else span
    sizes = (slots, groups, span, cap)

    def shape(*dims, kind=BF16):
        return jax.ShapeDtypeStruct((*dims, shots), kind)

    wide = pltpu.VMEM((GROUP * height * slots, shots), F32)
    wide_data = pltpu.VMEM((GROUP * height * freq_count, shots), F32)
    to_members = [jax.ShapeDtypeStruct((height * slots, shots), BF16)] * GROUP
    size = height * freq_count
    to_owners = [shape(size)] * 2 + [shape(2 * size)] * len(CHIPS)
    members = pltpu.VMEM((GROUP, height * freq_count, shots), BF16)

    def swap(value, distance):
        return lax.ppermute(value, "tiles", [(i, i ^ distance) for i in range(peers)])

    def in_group(values):
        got = {k: swap(values[k], k) for k in (6, 4, 2, 7, 5, 3, 1)}
        return [values[0]] + [got[k] for k in range(1, GROUP)]

    def hand_around(values):
        got = [swap(value, k) for value, k in zip(values[2:], CHIPS)]
        mate = call(relay_kernel, "for_mate", shape(4 * size), [VMEM] * (1 + len(CHIPS)))(
            values[1], *got
        )
        return [values[0], *got, swap(mate, 1)]

    def across(values):
        return [swap(value, q * GROUP) for q, value in enumerate(values, 1)]

    source, own_data, freqs, *sent = call(
        parts_kernel,
        "parts",
        [shape(freq_count, 2, block), in_hbm(shape(size)), pltpu.SMEM((slots,), jnp.int32)]
        + [shape(height * slots + slots)] * GROUP,
        [HBM] * 6,
        out_specs=[VMEM, HBM, SMEM] + [VMEM] * GROUP,
        scratch=[
            pltpu.VMEM(data.shape, BF16),
            pltpu.SMEM((2, freq_count), F32),
            pltpu.SMEM((1,), jnp.int32),
            pltpu.VMEM(tiles.shape, BF16),
            pltpu.SMEM((slots,), jnp.int32),
            pltpu.SMEM((slots,), jnp.int32),
            pltpu.SemaphoreType.DMA((7,)),
            wide,
            pltpu.VMEM((size, shots), BF16),
        ],
    )(stay(data), stay(wavelet.T), panel_block, *map(stay, (tiles, cover_rows, cover_freqs)))
    rests = [in_hbm(shape(height, span - cap))] if groups == 2 else []
    rest_rows = [pltpu.VMEM((height, span - cap, shots), BF16)] * len(rests)
    if groups == 2:
        sends = [shape(height * cap + TABLE)]
    else:
        sends = [shape(height, span)] * (groups - 1)
    hot, own, *out = call(
        functools.partial(sums_kernel, sizes),
        "sums",
        [
            jax.ShapeDtypeStruct((GROUP * slots, groups * span), BF16),
            shape(height, span, kind=F32),
        ]
        + sends
        + [shape(height, span - cap)] * len(rests),
        [VMEM] * GROUP,
    )(*in_group(sent))
    got = [swap(out[0], GROUP)] if groups == 2 else across(out)
    waiting = [hot, *out[1:]] if groups == 2 else [hot]
    stored = call(
        slices_kernel,
        "data_slices",
        [in_hbm(x) for x in waiting] + [shape(size)] * (GROUP - 1),
        [VMEM, ANY] + [VMEM] * len(waiting),
        out_specs=[HBM] * len(waiting) + [VMEM] * (GROUP - 1),
        scratch=[wide_data, pltpu.SemaphoreType.DMA((2,))],
    )(data, own, *waiting)
    hot = stored[0]
    data_in = in_group([own_data, *stored[len(waiting) :]])
    if groups == 2:
        most = call(
            most_kernel,
            "most",
            pltpu.SMEM((1,), jnp.int32),
            [VMEM] * 2 + [ANY] * (GROUP - 1),
            out_specs=SMEM,
        )(got[0], out[0], *data_in[1:])
        full = most[0] > cap

        def rest(value):
            return lax.cond(full, lambda v: swap(v, GROUP), jnp.zeros_like, value)

        got = [most, *got, rest(stored[1])]
    rounded, *out = call(
        functools.partial(residual_kernel, sizes),
        "residual_slices",
        [shape(height, span)] + [shape(height * cap)] * len(rests) + rests + to_owners,
        [VMEM, HBM]
        + [VMEM] * (GROUP - 1)
        + ([SMEM, VMEM, ANY] if groups == 2 else [VMEM] * len(got)),
        out_specs=[VMEM] * (1 + len(rests)) + [HBM] * len(rests) + [VMEM] * len(to_owners),
        scratch=[
            members,
            members,
            pltpu.VMEM((span, height * shots), F32),
            pltpu.SemaphoreType.DMA((2,)),
        ]
        + rest_rows * 2,
    )(own, stay(data_in[0]), *data_in[1:], *got)
    if groups == 2:
        got = [most, swap(out[0], GROUP), rest(out[1])]
    else:
        got = across([rounded] * (groups - 1))
    residual = call(
        residual_out_kernel,
        "residual",
        jax.ShapeDtypeStruct(data.shape, F32),
        [VMEM] * (1 + len(to_owners)),
        scratch=[wide_data],
    )(data, *hand_around(out[-len(to_owners) :]))
    out = call(
        functools.partial(spread_kernel, sizes),
        "spread",
        to_members,
        [VMEM] * 2 + ([SMEM, VMEM, ANY] if groups == 2 else [VMEM] * len(got)),
        scratch=rest_rows + [pltpu.SemaphoreType.DMA] * len(rests),
    )(hot, rounded, *got)
    gradient = call(
        gradient_kernel,
        "gradient",
        jax.ShapeDtypeStruct(tiles.shape, BF16),
        [VMEM, SMEM] + [VMEM] * GROUP,
        out_specs=HBM,
        scratch=[
            pltpu.VMEM(tiles.shape, BF16),
            wide,
            pltpu.SemaphoreType.DMA((4,)),
        ],
    )(source, freqs, *in_group(out))
    return residual, gradient


def solution(mesh):
    in_specs = (
        P("windows", None, "tiles", None),
        P(),
        P(),
        P(("windows", "tiles"), None, None, None),
        P(("windows", "tiles")),
        P(("windows", "tiles")),
    )
    out_specs = (P("windows", None, "tiles", None), P(("windows", "tiles"), None, None, None))
    return jax.shard_map(
        per_device, mesh=mesh, in_specs=in_specs, out_specs=out_specs, check_vma=False
    )
```

```python
import functools

import jax
import jax.numpy as jnp
from jax import lax
from jax.experimental import pallas as pl
from jax.experimental.pallas import tpu as pltpu
from jax.sharding import PartitionSpec as P

GROUP = 8
TABLE = 16
CHIPS = (2, 4, 6)
BF16 = jnp.bfloat16
F32 = jnp.float32
VMEM = pl.BlockSpec(memory_space=pltpu.VMEM)
SMEM = pl.BlockSpec(memory_space=pltpu.SMEM)
HBM = pl.BlockSpec(memory_space=pltpu.HBM)
ANY = pl.BlockSpec(memory_space=pl.ANY)


def call(kernel, name, out_shape, in_specs, scratch=(), out_specs=None, mib=24):
    return pl.pallas_call(
        kernel,
        name=name,
        out_shape=out_shape,
        in_specs=in_specs,
        out_specs=out_specs or jax.tree.map(lambda _: VMEM, out_shape),
        scratch_shapes=list(scratch),
        cost_estimate=pl.CostEstimate(flops=0, bytes_accessed=1 << 20, transcendentals=0),
        compiler_params=pltpu.CompilerParams(vmem_limit_bytes=mib * 1024 * 1024),
    )


def stay(array):
    return pltpu.with_memory_space_constraint(array, pltpu.HBM)


def in_hbm(shape):
    return pltpu.HBM(shape.shape, shape.dtype)


def local_index():
    return lax.rem(lax.axis_index("tiles"), GROUP)


def group_index():
    return lax.div(lax.axis_index("tiles"), GROUP)


def put(buffer, slot, count, real, imag):
    piece = real.shape[0] // GROUP
    for j in range(GROUP):
        at = slice(j * piece, (j + 1) * piece)
        first = 2 * j * piece * count + slot
        buffer[pl.ds(first, piece, stride=count), :] = real[at]
        buffer[pl.ds(first + piece * count, piece, stride=count), :] = imag[at]


def transposed_dot(left, right):
    return lax.dot_general(left, right, (((0,), (0,)), ((), ())), preferred_element_type=F32)


def member_rows(k, count):
    return pl.ds(pl.multiple_of((local_index() ^ k) * count, count), count)


def parts_kernel(data_hbm, wavelet_hbm, panel_hbm, tiles_hbm, rows_hbm, freqs_hbm, *refs):
    source, own_hbm, freqs_out, outs = *refs[:3], refs[3 : 3 + GROUP]
    data, wavelet, panel, tiles, rows, freqs, sems, wide, own = refs[3 + GROUP :]
    freq_count, _, block, shots = data.shape
    slots = tiles.shape[0]
    size = 2 * block // GROUP * slots
    half = lax.axis_size("tiles") * freq_count // 2
    pairs = (
        (data_hbm, data),
        (tiles_hbm, tiles),
        (wavelet_hbm, wavelet),
        (panel_hbm, panel),
        (freqs_hbm, freqs),
        (rows_hbm, rows),
    )
    copies = [pltpu.make_async_copy(*pair, sems.at[i]) for i, pair in enumerate(pairs)]
    for copy in copies:
        copy.start()
    diagonal = (
        lax.broadcasted_iota(jnp.int32, (block, shots), 0)
        == lax.broadcasted_iota(jnp.int32, (block, shots), 1)
    ).astype(F32)
    for i in (2, 3, 4, 5, 0):
        copies[i].wait()
    identity = diagonal * (lax.axis_index("tiles") == panel[0]).astype(F32)
    for f in range(freq_count):
        source[f, 0] = (wavelet[0, f] * identity - data[f, 0].astype(F32)).astype(BF16)
        source[f, 1] = (wavelet[1, f] * identity - data[f, 1].astype(F32)).astype(BF16)
    piece = block // GROUP
    mine = pl.ds(pl.multiple_of(local_index() * piece, piece), piece)
    for f in range(freq_count):
        for x in range(2):
            at = pl.ds(x * piece * freq_count + f, piece, stride=freq_count)
            wide[at, :] = data[f, x, mine, :].astype(F32)
    own[...] = wide[: own.shape[0]].astype(BF16)
    own_copy = pltpu.make_async_copy(own, own_hbm, sems.at[6])
    own_copy.start()
    line = lax.broadcasted_iota(jnp.int32, (slots, shots), 0)
    targets = jnp.zeros((slots, shots), jnp.int32)
    for t in range(slots):
        freqs_out[t] = freqs[t]
        targets = jnp.where(line == t, rows[t] * freq_count + freqs[t] - half, targets)
    for k in range(GROUP):
        outs[k][size:] = targets.astype(F32).astype(BF16)
    copies[1].wait()

    def one(t, carry):
        f = freqs[t]
        left = tiles[t].reshape(2 * block, block)
        right = jnp.concatenate([source[f, 0], source[f, 1]], axis=1)
        product = jnp.dot(left, right, preferred_element_type=F32)
        real = product[:block, :shots] - product[block:, shots:]
        put(wide, t, slots, real, product[:block, shots:] + product[block:, :shots])
        return carry

    lax.fori_loop(0, slots, one, 0, unroll=16)
    for k in range(GROUP):
        outs[k][:size] = wide[member_rows(k, size)].astype(BF16)
    own_copy.wait()


def sums_kernel(sizes, *refs):
    slots, groups, span, cap = sizes
    parts, (hot_out, own, *sends) = refs[:GROUP], refs[GROUP:]
    height, _, shots = own.shape
    count = GROUP * slots
    group = group_index()
    targets = jnp.concatenate([part[height * slots :] for part in parts], axis=0).astype(F32)
    lane = lax.broadcasted_iota(jnp.int32, (count, shots), 1)
    hot = []
    for q in range(0, groups, shots // span):
        here = jnp.zeros((count, shots), jnp.int32)
        for i in range(shots // span):
            inside = lane - i * span + (group ^ (q + i)) * span - groups * span // 2
            here = jnp.where(lane >= i * span, inside, here)
        hot.append((targets == here.astype(F32)).astype(F32).astype(BF16))
    if groups == 2:
        other = hot[0][:, span:]
        used = (transposed_dot(other, jnp.ones((count, shots), BF16)) > 0).astype(F32)
        before = (
            lax.broadcasted_iota(jnp.int32, (span, span), 0)
            > lax.broadcasted_iota(jnp.int32, (span, span), 1)
        ).astype(F32)
        rank = jnp.dot(before.astype(BF16), used.astype(BF16), preferred_element_type=F32)
        slot = lax.broadcasted_iota(jnp.int32, (span, shots), 1).astype(F32)
        chosen = jnp.where(rank == slot, used, 0.0)
        number = jnp.sum(used, axis=0, keepdims=True)
        target = lax.broadcasted_iota(jnp.int32, (span, shots), 0).astype(F32) + 1.0
        listed = jnp.sum(chosen * target, axis=0, keepdims=True)
        listed = jnp.where(slot[:TABLE] < span, listed, number)
        sends[0][height * cap :] = listed.astype(BF16)
        moved = jnp.dot(other, chosen[:, :span].astype(BF16), preferred_element_type=F32)
        hot = [jnp.concatenate([hot[0][:, :span], moved.astype(BF16)], axis=1)]
    hot = jnp.concatenate(hot, axis=1) if len(hot) > 1 else hot[0]
    hot_out[...] = hot
    step = 4
    for r in range(0, height, step):
        rows = [
            jnp.concatenate([part[(r + i) * slots : (r + i + 1) * slots] for part in parts], axis=0)
            for i in range(step)
        ]
        total = transposed_dot(hot, jnp.concatenate(rows, axis=1))
        for i in range(step):
            values = total[:, i * shots : (i + 1) * shots]
            own[r + i] = values[:span]
            if groups == 2:
                at = slice((r + i) * cap, (r + i + 1) * cap)
                sends[0][at] = values[span : span + cap].astype(BF16)
                sends[1][r + i] = values[span + cap :].astype(BF16)
            else:
                for q, send in enumerate(sends, 1):
                    send[r + i] = values[q * span : (q + 1) * span].astype(BF16)


def hand_out(outs, rows):
    size = outs[0].shape[0]
    outs[0][...] = rows(0)
    outs[1][...] = rows(1)
    for out, k in zip(outs[2:], CHIPS):
        out[:size] = rows(k)
        out[size:] = rows(k ^ 1)


def collect(refs, rows):
    own, *got, mate = refs
    size = own.shape[0]
    rows(0, own[...])
    rows(1, mate[:size])
    for i, k in enumerate(CHIPS):
        rows(k, got[i][:size])
        rows(k ^ 1, mate[(i + 1) * size : (i + 2) * size])


def relay_kernel(own, *refs):
    got, out = refs[:-1], refs[-1]
    size = own.shape[0]
    out[:size] = own[...]
    for i, ref in enumerate(got, 1):
        out[i * size : (i + 1) * size] = ref[size:]


def most_kernel(got, mine, *refs):
    out = refs[-1]
    last = slice(got.shape[0] - TABLE, got.shape[0])
    half = got.shape[1] // 2
    most = jnp.maximum(got[last, half:].astype(F32), mine[last, half:].astype(F32))
    out[0] = jnp.max(most).astype(jnp.int32)


def slices_kernel(data, _, *refs):
    *refs, wide, sems = refs
    count = (len(refs) - GROUP + 1) // 2
    waiting, stored, outs = refs[:count], refs[count : 2 * count], refs[2 * count :]
    copies = [
        pltpu.make_async_copy(src, dst, sems.at[i])
        for i, (src, dst) in enumerate(zip(waiting, stored))
    ]
    for copy in copies:
        copy.start()
    freq_count = data.shape[0]
    for f in range(freq_count):
        put(wide, f, freq_count, data[f, 0].astype(F32), data[f, 1].astype(F32))
    for k, out in enumerate(outs, 1):
        out[...] = wide[member_rows(k, out.shape[0])].astype(BF16)
    for copy in copies:
        copy.wait()


def fetch_rest(full, got_rest_any, got_rest, sem):
    @pl.when(full)
    def _():
        copy = pltpu.make_async_copy(got_rest_any, got_rest, sem)
        copy.start()
        copy.wait()

    @pl.when(jnp.logical_not(full))
    def _():
        got_rest[...] = jnp.zeros_like(got_rest)


def residual_kernel(sizes, own, *refs):
    slots, groups, span, cap = sizes
    height, _, shots = own.shape
    data_in, refs = refs[:GROUP], refs[GROUP:]
    if groups == 2:
        most, got, got_rest_any, rounded, send_hbm, rest_hbm, *outs = refs[:-7]
        data, back, total, sems, got_rest, rest, send = refs[-7:]
        target = lax.broadcasted_iota(jnp.int32, (span, span), 0).astype(F32) + 1.0
        listed = got[height * cap :, :span].astype(F32)[:1]
        chosen = (listed == target).astype(F32).astype(BF16)
        full = most[0] > cap
    else:
        got, (rounded, *outs, data, back, total, sems) = refs[: groups - 1], refs[groups - 1 :]
    local = local_index()
    freq_count = data.shape[1] // height
    own_copy = pltpu.make_async_copy(data_in[0], data.at[local], sems.at[0])
    own_copy.start()
    if groups == 2:

        fetch_rest(full, got_rest_any, got_rest, sems.at[1])
    for k in range(1, GROUP):
        data[local ^ k] = data_in[k][...]
    step = 8
    for r in range(0, height, step):
        rows = range(r, r + step)
        values = jnp.concatenate([own[i] for i in rows], axis=1)
        if groups == 2:
            more = []
            for i in rows:
                used = got[i * cap : (i + 1) * cap]
                more.append(jnp.concatenate([used, got_rest[i]], axis=0))
            more = jnp.concatenate(more, axis=1)
            values += jnp.dot(chosen, more, preferred_element_type=F32)
        else:
            for ref in got:
                values += jnp.concatenate([ref[i].astype(F32) for i in rows], axis=1)
        total[:, r * shots : (r + step) * shots] = values
        for j in range(GROUP):
            at = slice(j * freq_count, (j + 1) * freq_count)
            pair = [values[at, i * shots : (i + 1) * shots] for i in range(step)]
            pair = jnp.concatenate(pair, axis=0)
            back[j, r * freq_count : (r + step) * freq_count] = pair.astype(BF16)
    own_copy.wait()
    copies = []
    for r in range(0, height, step):
        rows = range(r, r + step)
        values = data[:, r * freq_count : (r + step) * freq_count].astype(F32)
        values = [
            values[:, i * freq_count : (i + 1) * freq_count].reshape(span, shots)
            for i in range(step)
        ]
        values = jnp.concatenate(values, axis=1) - total[:, r * shots : (r + step) * shots]
        values = values.astype(BF16)
        picked = transposed_dot(chosen, values).astype(BF16) if groups == 2 else None
        for i in rows:
            at = slice((i - r) * shots, (i - r + 1) * shots)
            rounded[i] = values[:, at]
            if groups == 2:
                send[i * cap : (i + 1) * cap] = picked[:cap, at]
                rest[i] = picked[cap:, at]
        if groups == 2:
            at = pl.ds(r * cap, step * cap)
            sem = sems.at[2 + r // step]
            copies.append(pltpu.make_async_copy(send.at[at], send_hbm.at[at], sem))
            copies[-1].start()
    if groups == 2:

        @pl.when(full)
        def _():
            copy = pltpu.make_async_copy(rest, rest_hbm, sems.at[1])
            copy.start()
            copy.wait()

    hand_out(outs, lambda k: back[local ^ k])
    for copy in copies:
        copy.wait()


def spread_kernel(sizes, hot, rounded, *refs):
    slots, groups, span, cap = sizes
    height, _, shots = rounded.shape
    if groups == 2:
        most, got, got_rest_any, *outs, got_rest, sem = refs
        fetch_rest(most[0] > cap, got_rest_any, got_rest, sem)
    else:
        got, outs = refs[: groups - 1], refs[groups - 1 :]
    step = 8
    for r in range(0, height, step):
        rows = []
        for i in range(r, r + step):
            if groups == 2:
                row = [rounded[i], got[i * cap : (i + 1) * cap], got_rest[i]]
            else:
                row = [rounded[i]] + [ref[i] for ref in got]
            rows.append(jnp.concatenate(row, axis=0))
        picked = jnp.dot(hot[...], jnp.concatenate(rows, axis=1), preferred_element_type=F32)
        picked = picked.astype(BF16)
        for i in range(step):
            for k in range(GROUP):
                outs[k][(r + i) * slots : (r + i + 1) * slots] = picked[
                    k * slots : (k + 1) * slots, i * shots : (i + 1) * shots
                ]


def residual_out_kernel(data, *refs):
    back, (residual, wide) = refs[:-2], refs[-2:]
    freq_count, _, block, _ = data.shape
    size = back[0].shape[0]
    piece = block // GROUP

    def keep(k, rows):
        wide[member_rows(k, size)] = rows.astype(F32)

    collect(back, keep)
    for f in range(freq_count):
        real, imag = data[f, 0].astype(F32), data[f, 1].astype(F32)
        for j in range(GROUP):
            at = slice(j * piece, (j + 1) * piece)
            first = j * size + f
            rows = pl.ds(first, piece, stride=freq_count)
            residual[f, 0, at, :] = real[at] - wide[rows, :]
            rows = pl.ds(first + piece * freq_count, piece, stride=freq_count)
            residual[f, 1, at, :] = imag[at] - wide[rows, :]


def gradient_kernel(source, freqs, *refs):
    parts, (gradient_hbm, gradient, wide, sems) = refs[:GROUP], refs[GROUP:]
    slots, _, block, _ = gradient.shape
    size, shots = parts[0].shape
    height = size // slots
    piece = height // 2
    scale = 1.0 / shots
    for k in range(GROUP):
        wide[member_rows(k, size)] = parts[k][...].astype(F32)

    def one(t, carry):
        left = wide[pl.ds(t, GROUP * height, stride=slots), :].astype(BF16)
        right = source[freqs[t]].reshape(2 * block, shots)
        total = -scale * lax.dot_general(
            left, right, (((1,), (1,)), ((), ())), preferred_element_type=F32
        )
        real, imag = [], []
        for j in range(GROUP):
            upper = total[j * height : j * height + piece]
            lower = total[j * height + piece : (j + 1) * height]
            real.append(upper[:, :block] + lower[:, block:])
            imag.append(lower[:, :block] - upper[:, block:])
        gradient[t, 0] = jnp.concatenate(real, axis=0).astype(BF16)
        gradient[t, 1] = jnp.concatenate(imag, axis=0).astype(BF16)
        return carry

    copies = []
    quarters = 4
    step = slots // quarters
    for i in range(quarters):
        lax.fori_loop(i * step, (i + 1) * step, one, 0, unroll=4)
        at = pl.ds(i * step, step)
        copies.append(
            pltpu.make_async_copy(gradient.at[at], gradient_hbm.at[at], sems.at[i])
        )
        copies[-1].start()
    for copy in copies:
        copy.wait()


def per_device(data, wavelet, panel_block, tiles, cover_rows, cover_freqs):
    freq_count, _, block, shots = data.shape
    slots = tiles.shape[0]
    peers = lax.axis_size("tiles")
    groups = peers // GROUP
    height = 2 * block // GROUP
    span = GROUP * freq_count
    cap = 3 * span // 4 if groups == 2 else span
    sizes = (slots, groups, span, cap)

    def shape(*dims, kind=BF16):
        return jax.ShapeDtypeStruct((*dims, shots), kind)

    wide = pltpu.VMEM(((GROUP * height + 1) * slots, shots), F32)
    wide_data = pltpu.VMEM(((GROUP * height + 1) * freq_count, shots), F32)
    to_members = [jax.ShapeDtypeStruct((height * slots, shots), BF16)] * GROUP
    size = height * freq_count
    to_owners = [shape(size)] * 2 + [shape(2 * size)] * len(CHIPS)
    members = pltpu.VMEM((GROUP, height * freq_count, shots), BF16)

    def swap(value, distance):
        return lax.ppermute(value, "tiles", [(i, i ^ distance) for i in range(peers)])

    def in_group(values):
        got = {k: swap(values[k], k) for k in (6, 4, 2, 7, 5, 3, 1)}
        return [values[0]] + [got[k] for k in range(1, GROUP)]

    def hand_around(values):
        got = [swap(value, k) for value, k in zip(values[2:], CHIPS)]
        mate = call(relay_kernel, "for_mate", shape(4 * size), [VMEM] * (1 + len(CHIPS)))(
            values[1], *got
        )
        return [values[0], *got, swap(mate, 1)]

    def across(values):
        return [swap(value, q * GROUP) for q, value in enumerate(values, 1)]

    source, own_data, freqs, *sent = call(
        parts_kernel,
        "parts",
        [shape(freq_count, 2, block), in_hbm(shape(size)), pltpu.SMEM((slots,), jnp.int32)]
        + [shape(height * slots + slots)] * GROUP,
        [HBM] * 6,
        out_specs=[VMEM, HBM, SMEM] + [VMEM] * GROUP,
        scratch=[
            pltpu.VMEM(data.shape, BF16),
            pltpu.SMEM((2, freq_count), F32),
            pltpu.SMEM((1,), jnp.int32),
            pltpu.VMEM(tiles.shape, BF16),
            pltpu.SMEM((slots,), jnp.int32),
            pltpu.SMEM((slots,), jnp.int32),
            pltpu.SemaphoreType.DMA((7,)),
            wide,
            pltpu.VMEM((size, shots), BF16),
        ],
    )(stay(data), stay(wavelet.T), panel_block, *map(stay, (tiles, cover_rows, cover_freqs)))
    rests = [in_hbm(shape(height, span - cap))] if groups == 2 else []
    rest_rows = [pltpu.VMEM((height, span - cap, shots), BF16)] * len(rests)
    if groups == 2:
        sends = [shape(height * cap + TABLE)]
    else:
        sends = [shape(height, span)] * (groups - 1)
    hot, own, *out = call(
        functools.partial(sums_kernel, sizes),
        "sums",
        [
            jax.ShapeDtypeStruct((GROUP * slots, groups * span), BF16),
            shape(height, span, kind=F32),
        ]
        + sends
        + [shape(height, span - cap)] * len(rests),
        [VMEM] * GROUP,
    )(*in_group(sent))
    got = [swap(out[0], GROUP)] if groups == 2 else across(out)
    waiting = [hot, *out[1:]] if groups == 2 else [hot]
    stored = call(
        slices_kernel,
        "data_slices",
        [in_hbm(x) for x in waiting] + [shape(size)] * (GROUP - 1),
        [VMEM, ANY] + [VMEM] * len(waiting),
        out_specs=[HBM] * len(waiting) + [VMEM] * (GROUP - 1),
        scratch=[wide_data, pltpu.SemaphoreType.DMA((2,))],
    )(data, own, *waiting)
    hot = stored[0]
    data_in = in_group([own_data, *stored[len(waiting) :]])
    if groups == 2:
        most = call(
            most_kernel,
            "most",
            pltpu.SMEM((1,), jnp.int32),
            [VMEM] * 2 + [ANY] * (GROUP - 1),
            out_specs=SMEM,
        )(got[0], out[0], *data_in[1:])
        full = most[0] > cap

        def rest(value):
            return lax.cond(full, lambda v: swap(v, GROUP), jnp.zeros_like, value)

        got = [most, *got, rest(stored[1])]
    rounded, *out = call(
        functools.partial(residual_kernel, sizes),
        "residual_slices",
        [shape(height, span)]
        + [in_hbm(shape(height * cap))] * len(rests)
        + rests
        + to_owners,
        [VMEM, HBM]
        + [VMEM] * (GROUP - 1)
        + ([SMEM, VMEM, ANY] if groups == 2 else [VMEM] * len(got)),
        out_specs=[VMEM] + [HBM] * (2 * len(rests)) + [VMEM] * len(to_owners),
        scratch=[
            members,
            members,
            pltpu.VMEM((span, height * shots), F32),
            pltpu.SemaphoreType.DMA((2 + height // 8,)),
        ]
        + rest_rows * 2
        + [pltpu.VMEM((height * cap, shots), BF16)] * len(rests),
    )(own, stay(data_in[0]), *data_in[1:], *got)
    if groups == 2:
        got = [most, swap(out[0], GROUP), rest(out[1])]
    else:
        got = across([rounded] * (groups - 1))
    residual = call(
        residual_out_kernel,
        "residual",
        jax.ShapeDtypeStruct(data.shape, F32),
        [VMEM] * (1 + len(to_owners)),
        scratch=[wide_data],
    )(data, *hand_around(out[-len(to_owners) :]))
    out = call(
        functools.partial(spread_kernel, sizes),
        "spread",
        to_members,
        [VMEM] * 2 + ([SMEM, VMEM, ANY] if groups == 2 else [VMEM] * len(got)),
        scratch=rest_rows + [pltpu.SemaphoreType.DMA] * len(rests),
    )(hot, rounded, *got)
    gradient = call(
        gradient_kernel,
        "gradient",
        jax.ShapeDtypeStruct(tiles.shape, BF16),
        [VMEM, SMEM] + [VMEM] * GROUP,
        out_specs=HBM,
        scratch=[
            pltpu.VMEM(tiles.shape, BF16),
            wide,
            pltpu.SemaphoreType.DMA((4,)),
        ],
    )(source, freqs, *in_group(out))
    return residual, gradient


def solution(mesh):
    in_specs = (
        P("windows", None, "tiles", None),
        P(),
        P(),
        P(("windows", "tiles"), None, None, None),
        P(("windows", "tiles")),
        P(("windows", "tiles")),
    )
    out_specs = (P("windows", None, "tiles", None), P(("windows", "tiles"), None, None, None))
    return jax.shard_map(
        per_device, mesh=mesh, in_specs=in_specs, out_specs=out_specs, check_vma=False
    )
```

```python
import functools

import jax
import jax.numpy as jnp
from jax import lax
from jax.experimental import pallas as pl
from jax.experimental.pallas import tpu as pltpu
from jax.sharding import PartitionSpec as P

GROUP = 8
TABLE = 16
CHIPS = (2, 4, 6)
BF16 = jnp.bfloat16
F32 = jnp.float32
VMEM = pl.BlockSpec(memory_space=pltpu.VMEM)
SMEM = pl.BlockSpec(memory_space=pltpu.SMEM)
HBM = pl.BlockSpec(memory_space=pltpu.HBM)
ANY = pl.BlockSpec(memory_space=pl.ANY)


def call(kernel, name, out_shape, in_specs, scratch=(), out_specs=None, mib=24):
    return pl.pallas_call(
        kernel,
        name=name,
        out_shape=out_shape,
        in_specs=in_specs,
        out_specs=out_specs or jax.tree.map(lambda _: VMEM, out_shape),
        scratch_shapes=list(scratch),
        cost_estimate=pl.CostEstimate(flops=0, bytes_accessed=1 << 20, transcendentals=0),
        compiler_params=pltpu.CompilerParams(vmem_limit_bytes=mib * 1024 * 1024),
    )


def stay(array):
    return pltpu.with_memory_space_constraint(array, pltpu.HBM)


def in_hbm(shape):
    return pltpu.HBM(shape.shape, shape.dtype)


def local_index():
    return lax.rem(lax.axis_index("tiles"), GROUP)


def group_index():
    return lax.div(lax.axis_index("tiles"), GROUP)


def put(buffer, slot, count, real, imag):
    piece = real.shape[0] // GROUP
    for j in range(GROUP):
        at = slice(j * piece, (j + 1) * piece)
        first = 2 * j * piece * count + slot
        buffer[pl.ds(first, piece, stride=count), :] = real[at]
        buffer[pl.ds(first + piece * count, piece, stride=count), :] = imag[at]


def transposed_dot(left, right):
    return lax.dot_general(left, right, (((0,), (0,)), ((), ())), preferred_element_type=F32)


def member_rows(k, count):
    return pl.ds(pl.multiple_of((local_index() ^ k) * count, count), count)


def parts_kernel(data_hbm, wavelet_hbm, panel_hbm, tiles_hbm, rows_hbm, freqs_hbm, *refs):
    source_hbm, own_hbm, freqs_out, outs = *refs[:3], refs[3 : 3 + GROUP]
    data, wavelet, panel, tiles, rows, freqs, sems, wide, own, source = refs[3 + GROUP :]
    freq_count, _, block, shots = data.shape
    slots = tiles.shape[0]
    size = 2 * block // GROUP * slots
    half = lax.axis_size("tiles") * freq_count // 2
    pairs = (
        (data_hbm, data),
        (tiles_hbm, tiles),
        (wavelet_hbm, wavelet),
        (panel_hbm, panel),
        (freqs_hbm, freqs),
        (rows_hbm, rows),
    )
    copies = [pltpu.make_async_copy(*pair, sems.at[i]) for i, pair in enumerate(pairs)]
    for copy in copies:
        copy.start()
    diagonal = (
        lax.broadcasted_iota(jnp.int32, (block, shots), 0)
        == lax.broadcasted_iota(jnp.int32, (block, shots), 1)
    ).astype(F32)
    for i in (2, 3, 4, 5, 0):
        copies[i].wait()
    identity = diagonal * (lax.axis_index("tiles") == panel[0]).astype(F32)
    for f in range(freq_count):
        source[f, 0] = (wavelet[0, f] * identity - data[f, 0].astype(F32)).astype(BF16)
        source[f, 1] = (wavelet[1, f] * identity - data[f, 1].astype(F32)).astype(BF16)
    piece = block // GROUP
    mine = pl.ds(pl.multiple_of(local_index() * piece, piece), piece)
    for f in range(freq_count):
        for x in range(2):
            at = pl.ds(x * piece * freq_count + f, piece, stride=freq_count)
            wide[at, :] = data[f, x, mine, :].astype(F32)
    own[...] = wide[: own.shape[0]].astype(BF16)
    stores = [
        pltpu.make_async_copy(own, own_hbm, sems.at[6]),
        pltpu.make_async_copy(source, source_hbm, sems.at[7]),
    ]
    for store in stores:
        store.start()
    line = lax.broadcasted_iota(jnp.int32, (slots, shots), 0)
    targets = jnp.zeros((slots, shots), jnp.int32)
    for t in range(slots):
        freqs_out[t] = freqs[t]
        targets = jnp.where(line == t, rows[t] * freq_count + freqs[t] - half, targets)
    for k in range(GROUP):
        outs[k][size:] = targets.astype(F32).astype(BF16)
    copies[1].wait()

    def one(t, carry):
        f = freqs[t]
        left = tiles[t].reshape(2 * block, block)
        right = jnp.concatenate([source[f, 0], source[f, 1]], axis=1)
        product = jnp.dot(left, right, preferred_element_type=F32)
        real = product[:block, :shots] - product[block:, shots:]
        put(wide, t, slots, real, product[:block, shots:] + product[block:, :shots])
        return carry

    lax.fori_loop(0, slots, one, 0, unroll=16)
    for k in range(GROUP):
        outs[k][:size] = wide[member_rows(k, size)].astype(BF16)
    for store in stores:
        store.wait()


def sums_kernel(sizes, *refs):
    slots, groups, span, cap = sizes
    parts, (hot_out, own, *sends) = refs[:GROUP], refs[GROUP:]
    height, _, shots = own.shape
    count = GROUP * slots
    group = group_index()
    targets = jnp.concatenate([part[height * slots :] for part in parts], axis=0).astype(F32)
    lane = lax.broadcasted_iota(jnp.int32, (count, shots), 1)
    hot = []
    for q in range(0, groups, shots // span):
        here = jnp.zeros((count, shots), jnp.int32)
        for i in range(shots // span):
            inside = lane - i * span + (group ^ (q + i)) * span - groups * span // 2
            here = jnp.where(lane >= i * span, inside, here)
        hot.append((targets == here.astype(F32)).astype(F32).astype(BF16))
    if groups == 2:
        other = hot[0][:, span:]
        used = (transposed_dot(other, jnp.ones((count, shots), BF16)) > 0).astype(F32)
        before = (
            lax.broadcasted_iota(jnp.int32, (span, span), 0)
            > lax.broadcasted_iota(jnp.int32, (span, span), 1)
        ).astype(F32)
        rank = jnp.dot(before.astype(BF16), used.astype(BF16), preferred_element_type=F32)
        slot = lax.broadcasted_iota(jnp.int32, (span, shots), 1).astype(F32)
        chosen = jnp.where(rank == slot, used, 0.0)
        number = jnp.sum(used, axis=0, keepdims=True)
        target = lax.broadcasted_iota(jnp.int32, (span, shots), 0).astype(F32) + 1.0
        listed = jnp.sum(chosen * target, axis=0, keepdims=True)
        listed = jnp.where(slot[:TABLE] < span, listed, number)
        sends[0][height * cap :] = listed.astype(BF16)
        moved = jnp.dot(other, chosen[:, :span].astype(BF16), preferred_element_type=F32)
        hot = [jnp.concatenate([hot[0][:, :span], moved.astype(BF16)], axis=1)]
    hot = jnp.concatenate(hot, axis=1) if len(hot) > 1 else hot[0]
    hot_out[...] = hot
    step = 4
    for r in range(0, height, step):
        rows = [
            jnp.concatenate([part[(r + i) * slots : (r + i + 1) * slots] for part in parts], axis=0)
            for i in range(step)
        ]
        total = transposed_dot(hot, jnp.concatenate(rows, axis=1))
        for i in range(step):
            values = total[:, i * shots : (i + 1) * shots]
            own[r + i] = values[:span]
            if groups == 2:
                at = slice((r + i) * cap, (r + i + 1) * cap)
                sends[0][at] = values[span : span + cap].astype(BF16)
                sends[1][r + i] = values[span + cap :].astype(BF16)
            else:
                for q, send in enumerate(sends, 1):
                    send[r + i] = values[q * span : (q + 1) * span].astype(BF16)


def hand_out(outs, rows):
    size = outs[0].shape[0]
    outs[0][...] = rows(0)
    outs[1][...] = rows(1)
    for out, k in zip(outs[2:], CHIPS):
        out[:size] = rows(k)
        out[size:] = rows(k ^ 1)


def collect(refs, rows):
    own, *got, mate = refs
    size = own.shape[0]
    rows(0, own[...])
    rows(1, mate[:size])
    for i, k in enumerate(CHIPS):
        rows(k, got[i][:size])
        rows(k ^ 1, mate[(i + 1) * size : (i + 2) * size])


def relay_kernel(own, *refs):
    got, out = refs[:-1], refs[-1]
    size = own.shape[0]
    out[:size] = own[...]
    for i, ref in enumerate(got, 1):
        out[i * size : (i + 1) * size] = ref[size:]


def most_kernel(got, mine, *refs):
    out = refs[-1]
    last = slice(got.shape[0] - TABLE, got.shape[0])
    half = got.shape[1] // 2
    most = jnp.maximum(got[last, half:].astype(F32), mine[last, half:].astype(F32))
    out[0] = jnp.max(most).astype(jnp.int32)


def slices_kernel(data, _, *refs):
    *refs, wide, sems = refs
    count = (len(refs) - 1 - len(CHIPS)) // 2
    waiting, stored, outs = refs[:count], refs[count : 2 * count], refs[2 * count :]
    copies = [
        pltpu.make_async_copy(src, dst, sems.at[i])
        for i, (src, dst) in enumerate(zip(waiting, stored))
    ]
    for copy in copies:
        copy.start()
    freq_count = data.shape[0]
    for f in range(freq_count):
        put(wide, f, freq_count, data[f, 0].astype(F32), data[f, 1].astype(F32))
    size = outs[0].shape[0]
    outs[0][...] = wide[member_rows(1, size)].astype(BF16)
    for out, k in zip(outs[1:], CHIPS):
        out[:size] = wide[member_rows(k, size)].astype(BF16)
        out[size:] = wide[member_rows(k ^ 1, size)].astype(BF16)
    for copy in copies:
        copy.wait()


def fetch_rest(full, got_rest_any, got_rest, sem):
    @pl.when(full)
    def _():
        copy = pltpu.make_async_copy(got_rest_any, got_rest, sem)
        copy.start()
        copy.wait()

    @pl.when(jnp.logical_not(full))
    def _():
        got_rest[...] = jnp.zeros_like(got_rest)


def residual_kernel(sizes, own, *refs):
    slots, groups, span, cap = sizes
    height, _, shots = own.shape
    data_in, refs = refs[: 2 + len(CHIPS)], refs[2 + len(CHIPS) :]
    if groups == 2:
        most, got, got_rest_any, rounded, send_hbm, rest_hbm, *outs = refs[:-7]
        data, back, total, sems, got_rest, rest, send = refs[-7:]
        target = lax.broadcasted_iota(jnp.int32, (span, span), 0).astype(F32) + 1.0
        listed = got[height * cap :, :span].astype(F32)[:1]
        chosen = (listed == target).astype(F32).astype(BF16)
        full = most[0] > cap
    else:
        got, (rounded, *outs, data, back, total, sems) = refs[: groups - 1], refs[groups - 1 :]
    local = local_index()
    freq_count = data.shape[1] // height
    own_copy = pltpu.make_async_copy(data_in[0], data.at[local], sems.at[0])
    own_copy.start()
    if groups == 2:

        fetch_rest(full, got_rest_any, got_rest, sems.at[1])
    *got_data, mate = data_in[1:]
    size = mate.shape[0] // 4
    data[local ^ 1] = mate[:size]
    for i, k in enumerate(CHIPS):
        data[local ^ k] = got_data[i][:size]
        data[local ^ k ^ 1] = mate[(i + 1) * size : (i + 2) * size]
    step = 8
    for r in range(0, height, step):
        rows = range(r, r + step)
        values = jnp.concatenate([own[i] for i in rows], axis=1)
        if groups == 2:
            more = []
            for i in rows:
                used = got[i * cap : (i + 1) * cap]
                more.append(jnp.concatenate([used, got_rest[i]], axis=0))
            more = jnp.concatenate(more, axis=1)
            values += jnp.dot(chosen, more, preferred_element_type=F32)
        else:
            for ref in got:
                values += jnp.concatenate([ref[i].astype(F32) for i in rows], axis=1)
        total[:, r * shots : (r + step) * shots] = values
        for j in range(GROUP):
            at = slice(j * freq_count, (j + 1) * freq_count)
            pair = [values[at, i * shots : (i + 1) * shots] for i in range(step)]
            pair = jnp.concatenate(pair, axis=0)
            back[j, r * freq_count : (r + step) * freq_count] = pair.astype(BF16)
    own_copy.wait()
    copies = []
    for r in range(0, height, step):
        rows = range(r, r + step)
        values = data[:, r * freq_count : (r + step) * freq_count].astype(F32)
        values = [
            values[:, i * freq_count : (i + 1) * freq_count].reshape(span, shots)
            for i in range(step)
        ]
        values = jnp.concatenate(values, axis=1) - total[:, r * shots : (r + step) * shots]
        values = values.astype(BF16)
        picked = transposed_dot(chosen, values).astype(BF16) if groups == 2 else None
        for i in rows:
            at = slice((i - r) * shots, (i - r + 1) * shots)
            rounded[i] = values[:, at]
            if groups == 2:
                send[i * cap : (i + 1) * cap] = picked[:cap, at]
                rest[i] = picked[cap:, at]
        if groups == 2:
            at = pl.ds(r * cap, step * cap)
            sem = sems.at[2 + r // step]
            copies.append(pltpu.make_async_copy(send.at[at], send_hbm.at[at], sem))
            copies[-1].start()
    if groups == 2:

        @pl.when(full)
        def _():
            copy = pltpu.make_async_copy(rest, rest_hbm, sems.at[1])
            copy.start()
            copy.wait()

    hand_out(outs, lambda k: back[local ^ k])
    for copy in copies:
        copy.wait()


def spread_kernel(sizes, hot, rounded, *refs):
    slots, groups, span, cap = sizes
    height, _, shots = rounded.shape
    if groups == 2:
        most, got, got_rest_any, *outs, got_rest, sem = refs
        fetch_rest(most[0] > cap, got_rest_any, got_rest, sem)
    else:
        got, outs = refs[: groups - 1], refs[groups - 1 :]
    step = 8
    for r in range(0, height, step):
        rows = []
        for i in range(r, r + step):
            if groups == 2:
                row = [rounded[i], got[i * cap : (i + 1) * cap], got_rest[i]]
            else:
                row = [rounded[i]] + [ref[i] for ref in got]
            rows.append(jnp.concatenate(row, axis=0))
        picked = jnp.dot(hot[...], jnp.concatenate(rows, axis=1), preferred_element_type=F32)
        picked = picked.astype(BF16)
        for i in range(step):
            for k in range(GROUP):
                outs[k][(r + i) * slots : (r + i + 1) * slots] = picked[
                    k * slots : (k + 1) * slots, i * shots : (i + 1) * shots
                ]


def residual_out_kernel(data, *refs):
    back, (residual, wide) = refs[:-2], refs[-2:]
    freq_count, _, block, _ = data.shape
    size = back[0].shape[0]
    piece = block // GROUP

    def keep(k, rows):
        wide[member_rows(k, size)] = rows.astype(F32)

    collect(back, keep)
    for f in range(freq_count):
        real, imag = data[f, 0].astype(F32), data[f, 1].astype(F32)
        for j in range(GROUP):
            at = slice(j * piece, (j + 1) * piece)
            first = j * size + f
            rows = pl.ds(first, piece, stride=freq_count)
            residual[f, 0, at, :] = real[at] - wide[rows, :]
            rows = pl.ds(first + piece * freq_count, piece, stride=freq_count)
            residual[f, 1, at, :] = imag[at] - wide[rows, :]


def gradient_kernel(source, freqs, *refs):
    parts, (gradient_hbm, gradient, wide, sems) = refs[:GROUP], refs[GROUP:]
    slots, _, block, _ = gradient.shape
    size, shots = parts[0].shape
    height = size // slots
    piece = height // 2
    scale = 1.0 / shots
    for k in range(GROUP):
        wide[member_rows(k, size)] = parts[k][...].astype(F32)

    def one(t, carry):
        left = wide[pl.ds(t, GROUP * height, stride=slots), :].astype(BF16)
        right = source[freqs[t]].reshape(2 * block, shots)
        total = -scale * lax.dot_general(
            left, right, (((1,), (1,)), ((), ())), preferred_element_type=F32
        )
        real, imag = [], []
        for j in range(GROUP):
            upper = total[j * height : j * height + piece]
            lower = total[j * height + piece : (j + 1) * height]
            real.append(upper[:, :block] + lower[:, block:])
            imag.append(lower[:, :block] - upper[:, block:])
        gradient[t, 0] = jnp.concatenate(real, axis=0).astype(BF16)
        gradient[t, 1] = jnp.concatenate(imag, axis=0).astype(BF16)
        return carry

    copies = []
    quarters = 4
    step = slots // quarters
    for i in range(quarters):
        lax.fori_loop(i * step, (i + 1) * step, one, 0, unroll=4)
        at = pl.ds(i * step, step)
        copies.append(
            pltpu.make_async_copy(gradient.at[at], gradient_hbm.at[at], sems.at[i])
        )
        copies[-1].start()
    for copy in copies:
        copy.wait()


def per_device(data, wavelet, panel_block, tiles, cover_rows, cover_freqs):
    freq_count, _, block, shots = data.shape
    slots = tiles.shape[0]
    peers = lax.axis_size("tiles")
    groups = peers // GROUP
    height = 2 * block // GROUP
    span = GROUP * freq_count
    cap = 3 * span // 4 if groups == 2 else span
    sizes = (slots, groups, span, cap)

    def shape(*dims, kind=BF16):
        return jax.ShapeDtypeStruct((*dims, shots), kind)

    wide = pltpu.VMEM(((GROUP * height + 1) * slots, shots), F32)
    wide_data = pltpu.VMEM(((GROUP * height + 1) * freq_count, shots), F32)
    to_members = [jax.ShapeDtypeStruct((height * slots, shots), BF16)] * GROUP
    size = height * freq_count
    to_owners = [shape(size)] * 2 + [shape(2 * size)] * len(CHIPS)
    members = pltpu.VMEM((GROUP, height * freq_count, shots), BF16)

    def swap(value, distance):
        return lax.ppermute(value, "tiles", [(i, i ^ distance) for i in range(peers)])

    def in_group(values):
        got = {k: swap(values[k], k) for k in (6, 4, 2, 7, 5, 3, 1)}
        return [values[0]] + [got[k] for k in range(1, GROUP)]

    def hand_around(values):
        got = [swap(value, k) for value, k in zip(values[2:], CHIPS)]
        mate = call(relay_kernel, "for_mate", shape(4 * size), [VMEM] * (1 + len(CHIPS)))(
            values[1], *got
        )
        return [values[0], *got, swap(mate, 1)]

    def across(values):
        return [swap(value, q * GROUP) for q, value in enumerate(values, 1)]

    source, own_data, freqs, *sent = call(
        parts_kernel,
        "parts",
        [in_hbm(shape(freq_count, 2, block)), in_hbm(shape(size)), pltpu.SMEM((slots,), jnp.int32)]
        + [shape(height * slots + slots)] * GROUP,
        [HBM] * 6,
        out_specs=[HBM, HBM, SMEM] + [VMEM] * GROUP,
        scratch=[
            pltpu.VMEM(data.shape, BF16),
            pltpu.SMEM((2, freq_count), F32),
            pltpu.SMEM((1,), jnp.int32),
            pltpu.VMEM(tiles.shape, BF16),
            pltpu.SMEM((slots,), jnp.int32),
            pltpu.SMEM((slots,), jnp.int32),
            pltpu.SemaphoreType.DMA((8,)),
            wide,
            pltpu.VMEM((size, shots), BF16),
            pltpu.VMEM(data.shape, BF16),
        ],
    )(stay(data), stay(wavelet.T), panel_block, *map(stay, (tiles, cover_rows, cover_freqs)))
    rests = [in_hbm(shape(height, span - cap))] if groups == 2 else []
    rest_rows = [pltpu.VMEM((height, span - cap, shots), BF16)] * len(rests)
    if groups == 2:
        sends = [shape(height * cap + TABLE)]
    else:
        sends = [shape(height, span)] * (groups - 1)
    hot, own, *out = call(
        functools.partial(sums_kernel, sizes),
        "sums",
        [
            jax.ShapeDtypeStruct((GROUP * slots, groups * span), BF16),
            shape(height, span, kind=F32),
        ]
        + sends
        + [shape(height, span - cap)] * len(rests),
        [VMEM] * GROUP,
    )(*in_group(sent))
    got = [swap(out[0], GROUP)] if groups == 2 else across(out)
    waiting = [hot, *out[1:]] if groups == 2 else [hot]
    stored = call(
        slices_kernel,
        "data_slices",
        [in_hbm(x) for x in waiting] + to_owners[1:],
        [VMEM, ANY] + [VMEM] * len(waiting),
        out_specs=[HBM] * len(waiting) + [VMEM] * (len(to_owners) - 1),
        scratch=[wide_data, pltpu.SemaphoreType.DMA((2,))],
    )(data, own, *waiting)
    hot = stored[0]
    data_in = hand_around([own_data, *stored[len(waiting) :]])
    if groups == 2:
        most = call(
            most_kernel,
            "most",
            pltpu.SMEM((1,), jnp.int32),
            [VMEM] * 2 + [ANY] * (len(data_in) - 1),
            out_specs=SMEM,
        )(got[0], out[0], *data_in[1:])
        full = most[0] > cap

        def rest(value):
            return lax.cond(full, lambda v: swap(v, GROUP), jnp.zeros_like, value)

        got = [most, *got, rest(stored[1])]
    rounded, *out = call(
        functools.partial(residual_kernel, sizes),
        "residual_slices",
        [shape(height, span)]
        + [in_hbm(shape(height * cap))] * len(rests)
        + rests
        + to_owners,
        [VMEM, HBM]
        + [VMEM] * (len(data_in) - 1)
        + ([SMEM, VMEM, ANY] if groups == 2 else [VMEM] * len(got)),
        out_specs=[VMEM] + [HBM] * (2 * len(rests)) + [VMEM] * len(to_owners),
        scratch=[
            members,
            members,
            pltpu.VMEM((span, height * shots), F32),
            pltpu.SemaphoreType.DMA((2 + height // 8,)),
        ]
        + rest_rows * 2
        + [pltpu.VMEM((height * cap, shots), BF16)] * len(rests),
    )(own, stay(data_in[0]), *data_in[1:], *got)
    if groups == 2:
        got = [most, swap(out[0], GROUP), rest(out[1])]
    else:
        got = across([rounded] * (groups - 1))
    residual = call(
        residual_out_kernel,
        "residual",
        jax.ShapeDtypeStruct(data.shape, F32),
        [VMEM] * (1 + len(to_owners)),
        scratch=[wide_data],
    )(data, *hand_around(out[-len(to_owners) :]))
    out = call(
        functools.partial(spread_kernel, sizes),
        "spread",
        to_members,
        [VMEM] * 2 + ([SMEM, VMEM, ANY] if groups == 2 else [VMEM] * len(got)),
        scratch=rest_rows + [pltpu.SemaphoreType.DMA] * len(rests),
    )(hot, rounded, *got)
    gradient = call(
        gradient_kernel,
        "gradient",
        jax.ShapeDtypeStruct(tiles.shape, BF16),
        [VMEM, SMEM] + [VMEM] * GROUP,
        out_specs=HBM,
        scratch=[
            pltpu.VMEM(tiles.shape, BF16),
            wide,
            pltpu.SemaphoreType.DMA((4,)),
        ],
    )(source, freqs, *in_group(out))
    return residual, gradient


def solution(mesh):
    in_specs = (
        P("windows", None, "tiles", None),
        P(),
        P(),
        P(("windows", "tiles"), None, None, None),
        P(("windows", "tiles")),
        P(("windows", "tiles")),
    )
    out_specs = (P("windows", None, "tiles", None), P(("windows", "tiles"), None, None, None))
    return jax.shard_map(
        per_device, mesh=mesh, in_specs=in_specs, out_specs=out_specs, check_vma=False
    )
```

```python
import functools

import jax
import jax.numpy as jnp
from jax import lax
from jax.experimental import pallas as pl
from jax.experimental.pallas import tpu as pltpu
from jax.sharding import PartitionSpec as P

GROUP = 8
TABLE = 16
CHIPS = (2, 4, 6)
BF16 = jnp.bfloat16
F32 = jnp.float32
VMEM = pl.BlockSpec(memory_space=pltpu.VMEM)
SMEM = pl.BlockSpec(memory_space=pltpu.SMEM)
HBM = pl.BlockSpec(memory_space=pltpu.HBM)
ANY = pl.BlockSpec(memory_space=pl.ANY)


def call(kernel, name, out_shape, in_specs, scratch=(), out_specs=None, mib=24, aliases=None):
    return pl.pallas_call(
        kernel,
        name=name,
        out_shape=out_shape,
        in_specs=in_specs,
        out_specs=out_specs or jax.tree.map(lambda _: VMEM, out_shape),
        scratch_shapes=list(scratch),
        input_output_aliases=aliases or {},
        cost_estimate=pl.CostEstimate(flops=0, bytes_accessed=1 << 20, transcendentals=0),
        compiler_params=pltpu.CompilerParams(vmem_limit_bytes=mib * 1024 * 1024),
    )


def stay(array):
    return pltpu.with_memory_space_constraint(array, pltpu.HBM)


def in_hbm(shape):
    return pltpu.HBM(shape.shape, shape.dtype)


def local_index():
    return lax.rem(lax.axis_index("tiles"), GROUP)


def group_index():
    return lax.div(lax.axis_index("tiles"), GROUP)


def put(buffer, slot, count, real, imag):
    piece = real.shape[0] // GROUP
    for j in range(GROUP):
        at = slice(j * piece, (j + 1) * piece)
        first = 2 * j * piece * count + slot
        buffer[pl.ds(first, piece, stride=count), :] = real[at]
        buffer[pl.ds(first + piece * count, piece, stride=count), :] = imag[at]


def transposed_dot(left, right):
    return lax.dot_general(left, right, (((0,), (0,)), ((), ())), preferred_element_type=F32)


def member_rows(k, count):
    return pl.ds(pl.multiple_of((local_index() ^ k) * count, count), count)


def parts_kernel(data_hbm, wavelet_hbm, panel_hbm, tiles_hbm, rows_hbm, freqs_hbm, *refs):
    source_hbm, own_hbm, freqs_out, outs = *refs[:3], refs[3 : 3 + GROUP]
    data, wavelet, panel, tiles, rows, freqs, sems, wide, own, source = refs[3 + GROUP :]
    freq_count, _, block, shots = data.shape
    slots = tiles.shape[0]
    size = 2 * block // GROUP * slots
    half = lax.axis_size("tiles") * freq_count // 2
    pairs = (
        (data_hbm, data),
        (tiles_hbm, tiles),
        (wavelet_hbm, wavelet),
        (panel_hbm, panel),
        (freqs_hbm, freqs),
        (rows_hbm, rows),
    )
    copies = [pltpu.make_async_copy(*pair, sems.at[i]) for i, pair in enumerate(pairs)]
    for copy in copies:
        copy.start()
    diagonal = (
        lax.broadcasted_iota(jnp.int32, (block, shots), 0)
        == lax.broadcasted_iota(jnp.int32, (block, shots), 1)
    ).astype(F32)
    for i in (2, 3, 4, 5, 0):
        copies[i].wait()
    identity = diagonal * (lax.axis_index("tiles") == panel[0]).astype(F32)
    for f in range(freq_count):
        source[f, 0] = (wavelet[0, f] * identity - data[f, 0].astype(F32)).astype(BF16)
        source[f, 1] = (wavelet[1, f] * identity - data[f, 1].astype(F32)).astype(BF16)
    piece = block // GROUP
    mine = pl.ds(pl.multiple_of(local_index() * piece, piece), piece)
    for f in range(freq_count):
        for x in range(2):
            at = pl.ds(x * piece * freq_count + f, piece, stride=freq_count)
            wide[at, :] = data[f, x, mine, :].astype(F32)
    own[...] = wide[: own.shape[0]].astype(BF16)
    stores = [
        pltpu.make_async_copy(own, own_hbm, sems.at[6]),
        pltpu.make_async_copy(source, source_hbm, sems.at[7]),
    ]
    for store in stores:
        store.start()
    line = lax.broadcasted_iota(jnp.int32, (slots, shots), 0)
    targets = jnp.zeros((slots, shots), jnp.int32)
    for t in range(slots):
        freqs_out[t] = freqs[t]
        targets = jnp.where(line == t, rows[t] * freq_count + freqs[t] - half, targets)
    for k in range(GROUP):
        outs[k][size:] = targets.astype(F32).astype(BF16)
    copies[1].wait()

    def one(t, carry):
        f = freqs[t]
        left = tiles[t].reshape(2 * block, block)
        right = jnp.concatenate([source[f, 0], source[f, 1]], axis=1)
        product = jnp.dot(left, right, preferred_element_type=F32)
        real = product[:block, :shots] - product[block:, shots:]
        put(wide, t, slots, real, product[:block, shots:] + product[block:, :shots])
        return carry

    lax.fori_loop(0, slots, one, 0, unroll=16)
    for k in range(GROUP):
        outs[k][:size] = wide[member_rows(k, size)].astype(BF16)
    for store in stores:
        store.wait()


def sums_kernel(sizes, *refs):
    slots, groups, span, cap = sizes
    parts, (hot_out, own, *sends) = refs[:GROUP], refs[GROUP:]
    height, _, shots = own.shape
    count = GROUP * slots
    group = group_index()
    targets = jnp.concatenate([part[height * slots :] for part in parts], axis=0).astype(F32)
    lane = lax.broadcasted_iota(jnp.int32, (count, shots), 1)
    hot = []
    for q in range(0, groups, shots // span):
        here = jnp.zeros((count, shots), jnp.int32)
        for i in range(shots // span):
            inside = lane - i * span + (group ^ (q + i)) * span - groups * span // 2
            here = jnp.where(lane >= i * span, inside, here)
        hot.append((targets == here.astype(F32)).astype(F32).astype(BF16))
    if groups == 2:
        other = hot[0][:, span:]
        used = (transposed_dot(other, jnp.ones((count, shots), BF16)) > 0).astype(F32)
        before = (
            lax.broadcasted_iota(jnp.int32, (span, span), 0)
            > lax.broadcasted_iota(jnp.int32, (span, span), 1)
        ).astype(F32)
        rank = jnp.dot(before.astype(BF16), used.astype(BF16), preferred_element_type=F32)
        slot = lax.broadcasted_iota(jnp.int32, (span, shots), 1).astype(F32)
        chosen = jnp.where(rank == slot, used, 0.0)
        number = jnp.sum(used, axis=0, keepdims=True)
        target = lax.broadcasted_iota(jnp.int32, (span, shots), 0).astype(F32) + 1.0
        listed = jnp.sum(chosen * target, axis=0, keepdims=True)
        listed = jnp.where(slot[:TABLE] < span, listed, number)
        sends[0][height * cap :] = listed.astype(BF16)
        moved = jnp.dot(other, chosen[:, :span].astype(BF16), preferred_element_type=F32)
        hot = [jnp.concatenate([hot[0][:, :span], moved.astype(BF16)], axis=1)]
    hot = jnp.concatenate(hot, axis=1) if len(hot) > 1 else hot[0]
    hot_out[...] = hot
    step = 4
    for r in range(0, height, step):
        rows = [
            jnp.concatenate([part[(r + i) * slots : (r + i + 1) * slots] for part in parts], axis=0)
            for i in range(step)
        ]
        total = transposed_dot(hot, jnp.concatenate(rows, axis=1))
        for i in range(step):
            values = total[:, i * shots : (i + 1) * shots]
            own[r + i] = values[:span]
            if groups == 2:
                at = slice((r + i) * cap, (r + i + 1) * cap)
                sends[0][at] = values[span : span + cap].astype(BF16)
                sends[1][r + i] = values[span + cap :].astype(BF16)
            else:
                for q, send in enumerate(sends, 1):
                    send[r + i] = values[q * span : (q + 1) * span].astype(BF16)


def hand_out(outs, rows):
    size = outs[0].shape[0]
    outs[0][...] = rows(0)
    outs[1][...] = rows(1)
    for out, k in zip(outs[2:], CHIPS):
        out[:size] = rows(k)
        out[size:] = rows(k ^ 1)


def collect(refs, rows):
    own, *got, mate = refs
    size = own.shape[0]
    rows(0, own[...])
    rows(1, mate[:size])
    for i, k in enumerate(CHIPS):
        rows(k, got[i][:size])
        rows(k ^ 1, mate[(i + 1) * size : (i + 2) * size])


def relay_kernel(own, *refs):
    got, out = refs[:-1], refs[-1]
    size = own.shape[0]
    out[:size] = own[...]
    for i, ref in enumerate(got, 1):
        out[i * size : (i + 1) * size] = ref[size:]


def most_kernel(got, mine, *refs):
    out = refs[-1]
    last = slice(got.shape[0] - TABLE, got.shape[0])
    half = got.shape[1] // 2
    most = jnp.maximum(got[last, half:].astype(F32), mine[last, half:].astype(F32))
    out[0] = jnp.max(most).astype(jnp.int32)


def slices_kernel(data, _, *refs):
    *refs, wide, sems = refs
    count = (len(refs) - 1 - len(CHIPS)) // 2
    waiting, stored, outs = refs[:count], refs[count : 2 * count], refs[2 * count :]
    copies = [
        pltpu.make_async_copy(src, dst, sems.at[i])
        for i, (src, dst) in enumerate(zip(waiting, stored))
    ]
    for copy in copies:
        copy.start()
    freq_count = data.shape[0]
    for f in range(freq_count):
        put(wide, f, freq_count, data[f, 0].astype(F32), data[f, 1].astype(F32))
    size = outs[0].shape[0]
    outs[0][...] = wide[member_rows(1, size)].astype(BF16)
    for out, k in zip(outs[1:], CHIPS):
        out[:size] = wide[member_rows(k, size)].astype(BF16)
        out[size:] = wide[member_rows(k ^ 1, size)].astype(BF16)
    for copy in copies:
        copy.wait()


def fetch_rest(full, got_rest_any, got_rest, sem):
    @pl.when(full)
    def _():
        copy = pltpu.make_async_copy(got_rest_any, got_rest, sem)
        copy.start()
        copy.wait()

    @pl.when(jnp.logical_not(full))
    def _():
        got_rest[...] = jnp.zeros_like(got_rest)


def residual_kernel(sizes, own, *refs):
    slots, groups, span, cap = sizes
    height, _, shots = own.shape
    data_in, refs = refs[: 2 + len(CHIPS)], refs[2 + len(CHIPS) :]
    if groups == 2:
        most, got, got_rest_any, rounded, send_hbm, rest_hbm, *outs = refs[:-7]
        data, back, total, sems, got_rest, rest, send = refs[-7:]
        target = lax.broadcasted_iota(jnp.int32, (span, span), 0).astype(F32) + 1.0
        listed = got[height * cap :, :span].astype(F32)[:1]
        chosen = (listed == target).astype(F32).astype(BF16)
        full = most[0] > cap
    else:
        got, (rounded, *outs, data, back, total, sems) = refs[: groups - 1], refs[groups - 1 :]
    local = local_index()
    freq_count = data.shape[1] // height
    own_copy = pltpu.make_async_copy(data_in[0], data.at[local], sems.at[0])
    own_copy.start()
    if groups == 2:

        fetch_rest(full, got_rest_any, got_rest, sems.at[1])
    *got_data, mate = data_in[1:]
    size = mate.shape[0] // 4
    data[local ^ 1] = mate[:size]
    for i, k in enumerate(CHIPS):
        data[local ^ k] = got_data[i][:size]
        data[local ^ k ^ 1] = mate[(i + 1) * size : (i + 2) * size]
    step = 8
    for r in range(0, height, step):
        rows = range(r, r + step)
        values = jnp.concatenate([own[i] for i in rows], axis=1)
        if groups == 2:
            more = []
            for i in rows:
                used = got[i * cap : (i + 1) * cap]
                more.append(jnp.concatenate([used, got_rest[i]], axis=0))
            more = jnp.concatenate(more, axis=1)
            values += jnp.dot(chosen, more, preferred_element_type=F32)
        else:
            for ref in got:
                values += jnp.concatenate([ref[i].astype(F32) for i in rows], axis=1)
        total[:, r * shots : (r + step) * shots] = values
        for j in range(GROUP):
            at = slice(j * freq_count, (j + 1) * freq_count)
            pair = [values[at, i * shots : (i + 1) * shots] for i in range(step)]
            pair = jnp.concatenate(pair, axis=0)
            back[j, r * freq_count : (r + step) * freq_count] = pair.astype(BF16)
    own_copy.wait()
    copies = []
    for r in range(0, height, step):
        rows = range(r, r + step)
        values = data[:, r * freq_count : (r + step) * freq_count].astype(F32)
        values = [
            values[:, i * freq_count : (i + 1) * freq_count].reshape(span, shots)
            for i in range(step)
        ]
        values = jnp.concatenate(values, axis=1) - total[:, r * shots : (r + step) * shots]
        values = values.astype(BF16)
        picked = transposed_dot(chosen, values).astype(BF16) if groups == 2 else None
        for i in rows:
            at = slice((i - r) * shots, (i - r + 1) * shots)
            rounded[i] = values[:, at]
            if groups == 2:
                send[i * cap : (i + 1) * cap] = picked[:cap, at]
                rest[i] = picked[cap:, at]
        if groups == 2:
            at = pl.ds(r * cap, step * cap)
            sem = sems.at[2 + r // step]
            copies.append(pltpu.make_async_copy(send.at[at], send_hbm.at[at], sem))
            copies[-1].start()
    if groups == 2:

        @pl.when(full)
        def _():
            copy = pltpu.make_async_copy(rest, rest_hbm, sems.at[1])
            copy.start()
            copy.wait()

    hand_out(outs, lambda k: back[local ^ k])
    for copy in copies:
        copy.wait()


def spread_kernel(sizes, hot, rounded, *refs):
    slots, groups, span, cap = sizes
    height, _, shots = rounded.shape
    if groups == 2:
        most, got, got_rest_any, *outs, got_rest, sem = refs
        fetch_rest(most[0] > cap, got_rest_any, got_rest, sem)
    else:
        got, outs = refs[: groups - 1], refs[groups - 1 :]
    step = 8
    for r in range(0, height, step):
        rows = []
        for i in range(r, r + step):
            if groups == 2:
                row = [rounded[i], got[i * cap : (i + 1) * cap], got_rest[i]]
            else:
                row = [rounded[i]] + [ref[i] for ref in got]
            rows.append(jnp.concatenate(row, axis=0))
        picked = jnp.dot(hot[...], jnp.concatenate(rows, axis=1), preferred_element_type=F32)
        picked = picked.astype(BF16)
        for i in range(step):
            for k in range(GROUP):
                outs[k][(r + i) * slots : (r + i + 1) * slots] = picked[
                    k * slots : (k + 1) * slots, i * shots : (i + 1) * shots
                ]


def residual_out_kernel(data, *refs):
    back, (residual, wide) = refs[:-2], refs[-2:]
    freq_count, _, block, _ = data.shape
    size = back[0].shape[0]
    piece = block // GROUP

    def keep(k, rows):
        wide[member_rows(k, size)] = rows.astype(F32)

    collect(back, keep)
    for f in range(freq_count):
        real, imag = data[f, 0].astype(F32), data[f, 1].astype(F32)
        for j in range(GROUP):
            at = slice(j * piece, (j + 1) * piece)
            first = j * size + f
            rows = pl.ds(first, piece, stride=freq_count)
            residual[f, 0, at, :] = real[at] - wide[rows, :]
            rows = pl.ds(first + piece * freq_count, piece, stride=freq_count)
            residual[f, 1, at, :] = imag[at] - wide[rows, :]


def gradient_kernel(members, source, freqs, *refs):
    parts, (gradient_hbm, gradient, wide, sems) = refs[: len(members)], refs[-4:]
    slots, _, _, block = gradient.shape
    size, shots = parts[0].shape
    height = size // slots
    piece = height // 2
    scale = 1.0 / shots
    local = local_index()
    for i, part in enumerate(parts):
        wide[i * size : (i + 1) * size] = part[...].astype(F32)

    def one(t, carry):
        left = wide[pl.ds(t, len(members) * height, stride=slots), :].astype(BF16)
        right = source[freqs[t]].reshape(2 * block, shots)
        total = -scale * lax.dot_general(
            left, right, (((1,), (1,)), ((), ())), preferred_element_type=F32
        )
        real, imag = [], []
        for i in range(len(members)):
            upper = total[i * height : i * height + piece]
            lower = total[i * height + piece : (i + 1) * height]
            real.append(upper[:, :block] + lower[:, block:])
            imag.append(lower[:, :block] - upper[:, block:])
        gradient[t, 0] = jnp.concatenate(real, axis=0).astype(BF16)
        gradient[t, 1] = jnp.concatenate(imag, axis=0).astype(BF16)
        return carry

    copies = []
    quarters = 4
    step = slots // quarters
    for quarter in range(quarters):
        lax.fori_loop(quarter * step, (quarter + 1) * step, one, 0, unroll=4)
        at = pl.ds(quarter * step, step)
        for i, k in enumerate(members):
            rows = pl.ds(pl.multiple_of((local ^ k) * piece, piece), piece)
            copies.append(
                pltpu.make_async_copy(
                    gradient.at[at, :, pl.ds(i * piece, piece), :],
                    gradient_hbm.at[at, :, rows, :],
                    sems.at[quarter * len(members) + i],
                )
            )
            copies[-1].start()
    for copy in copies:
        copy.wait()


def per_device(data, wavelet, panel_block, tiles, cover_rows, cover_freqs):
    freq_count, _, block, shots = data.shape
    slots = tiles.shape[0]
    peers = lax.axis_size("tiles")
    groups = peers // GROUP
    height = 2 * block // GROUP
    span = GROUP * freq_count
    cap = 3 * span // 4 if groups == 2 else span
    sizes = (slots, groups, span, cap)

    def shape(*dims, kind=BF16):
        return jax.ShapeDtypeStruct((*dims, shots), kind)

    wide = pltpu.VMEM(((GROUP * height + 1) * slots, shots), F32)
    wide_data = pltpu.VMEM(((GROUP * height + 1) * freq_count, shots), F32)
    to_members = [jax.ShapeDtypeStruct((height * slots, shots), BF16)] * GROUP
    size = height * freq_count
    to_owners = [shape(size)] * 2 + [shape(2 * size)] * len(CHIPS)
    members = pltpu.VMEM((GROUP, height * freq_count, shots), BF16)

    def swap(value, distance):
        return lax.ppermute(value, "tiles", [(i, i ^ distance) for i in range(peers)])

    def in_group(values):
        got = {k: swap(values[k], k) for k in (6, 4, 2, 7, 5, 3, 1)}
        return [values[0]] + [got[k] for k in range(1, GROUP)]

    def hand_around(values):
        got = [swap(value, k) for value, k in zip(values[2:], CHIPS)]
        mate = call(relay_kernel, "for_mate", shape(4 * size), [VMEM] * (1 + len(CHIPS)))(
            values[1], *got
        )
        return [values[0], *got, swap(mate, 1)]

    def across(values):
        return [swap(value, q * GROUP) for q, value in enumerate(values, 1)]

    source, own_data, freqs, *sent = call(
        parts_kernel,
        "parts",
        [in_hbm(shape(freq_count, 2, block)), in_hbm(shape(size)), pltpu.SMEM((slots,), jnp.int32)]
        + [shape(height * slots + slots)] * GROUP,
        [HBM] * 6,
        out_specs=[HBM, HBM, SMEM] + [VMEM] * GROUP,
        scratch=[
            pltpu.VMEM(data.shape, BF16),
            pltpu.SMEM((2, freq_count), F32),
            pltpu.SMEM((1,), jnp.int32),
            pltpu.VMEM(tiles.shape, BF16),
            pltpu.SMEM((slots,), jnp.int32),
            pltpu.SMEM((slots,), jnp.int32),
            pltpu.SemaphoreType.DMA((8,)),
            wide,
            pltpu.VMEM((size, shots), BF16),
            pltpu.VMEM(data.shape, BF16),
        ],
    )(stay(data), stay(wavelet.T), panel_block, *map(stay, (tiles, cover_rows, cover_freqs)))
    rests = [in_hbm(shape(height, span - cap))] if groups == 2 else []
    rest_rows = [pltpu.VMEM((height, span - cap, shots), BF16)] * len(rests)
    if groups == 2:
        sends = [shape(height * cap + TABLE)]
    else:
        sends = [shape(height, span)] * (groups - 1)
    hot, own, *out = call(
        functools.partial(sums_kernel, sizes),
        "sums",
        [
            jax.ShapeDtypeStruct((GROUP * slots, groups * span), BF16),
            shape(height, span, kind=F32),
        ]
        + sends
        + [shape(height, span - cap)] * len(rests),
        [VMEM] * GROUP,
    )(*in_group(sent))
    got = [swap(out[0], GROUP)] if groups == 2 else across(out)
    waiting = [hot, *out[1:]] if groups == 2 else [hot]
    stored = call(
        slices_kernel,
        "data_slices",
        [in_hbm(x) for x in waiting] + to_owners[1:],
        [VMEM, ANY] + [VMEM] * len(waiting),
        out_specs=[HBM] * len(waiting) + [VMEM] * (len(to_owners) - 1),
        scratch=[wide_data, pltpu.SemaphoreType.DMA((2,))],
    )(data, own, *waiting)
    hot = stored[0]
    data_in = hand_around([own_data, *stored[len(waiting) :]])
    if groups == 2:
        most = call(
            most_kernel,
            "most",
            pltpu.SMEM((1,), jnp.int32),
            [VMEM] * 2 + [ANY] * (len(data_in) - 1),
            out_specs=SMEM,
        )(got[0], out[0], *data_in[1:])
        full = most[0] > cap

        def rest(value):
            return lax.cond(full, lambda v: swap(v, GROUP), jnp.zeros_like, value)

        got = [most, *got, rest(stored[1])]
    rounded, *out = call(
        functools.partial(residual_kernel, sizes),
        "residual_slices",
        [shape(height, span)]
        + [in_hbm(shape(height * cap))] * len(rests)
        + rests
        + to_owners,
        [VMEM, HBM]
        + [VMEM] * (len(data_in) - 1)
        + ([SMEM, VMEM, ANY] if groups == 2 else [VMEM] * len(got)),
        out_specs=[VMEM] + [HBM] * (2 * len(rests)) + [VMEM] * len(to_owners),
        scratch=[
            members,
            members,
            pltpu.VMEM((span, height * shots), F32),
            pltpu.SemaphoreType.DMA((2 + height // 8,)),
        ]
        + rest_rows * 2
        + [pltpu.VMEM((height * cap, shots), BF16)] * len(rests),
    )(own, stay(data_in[0]), *data_in[1:], *got)
    if groups == 2:
        got = [most, swap(out[0], GROUP), rest(out[1])]
    else:
        got = across([rounded] * (groups - 1))
    residual = call(
        residual_out_kernel,
        "residual",
        jax.ShapeDtypeStruct(data.shape, F32),
        [VMEM] * (1 + len(to_owners)),
        scratch=[wide_data],
    )(data, *hand_around(out[-len(to_owners) :]))
    out = call(
        functools.partial(spread_kernel, sizes),
        "spread",
        to_members,
        [VMEM] * 2 + ([SMEM, VMEM, ANY] if groups == 2 else [VMEM] * len(got)),
        scratch=rest_rows + [pltpu.SemaphoreType.DMA] * len(rests),
    )(hot, rounded, *got)
    got = in_group(out)
    gradient = []
    for members in (range(GROUP - 2), range(GROUP - 2, GROUP)):
        rows = len(members) * block // GROUP
        gradient = [
            call(
                functools.partial(gradient_kernel, members),
                "gradient",
                in_hbm(tiles),
                [VMEM, SMEM] + [VMEM] * len(members) + [ANY] * len(gradient),
                out_specs=HBM,
                scratch=[
                    pltpu.VMEM((slots, 2, rows, block), BF16),
                    pltpu.VMEM(((len(members) * height + 1) * slots, shots), F32),
                    pltpu.SemaphoreType.DMA((4 * len(members),)),
                ],
                aliases={2 + len(members): 0} if gradient else None,
            )(source, freqs, *[got[k] for k in members], *gradient)
        ]
    gradient = gradient[0]
    return residual, gradient


def solution(mesh):
    in_specs = (
        P("windows", None, "tiles", None),
        P(),
        P(),
        P(("windows", "tiles"), None, None, None),
        P(("windows", "tiles")),
        P(("windows", "tiles")),
    )
    out_specs = (P("windows", None, "tiles", None), P(("windows", "tiles"), None, None, None))
    return jax.shard_map(
        per_device, mesh=mesh, in_specs=in_specs, out_specs=out_specs, check_vma=False
    )
```

```python
import functools

import jax
import jax.numpy as jnp
from jax import lax
from jax.experimental import pallas as pl
from jax.experimental.pallas import tpu as pltpu
from jax.sharding import PartitionSpec as P

GROUP = 8
TABLE = 16
CHIPS = (2, 4, 6)
BF16 = jnp.bfloat16
F32 = jnp.float32
VMEM = pl.BlockSpec(memory_space=pltpu.VMEM)
SMEM = pl.BlockSpec(memory_space=pltpu.SMEM)
HBM = pl.BlockSpec(memory_space=pltpu.HBM)
ANY = pl.BlockSpec(memory_space=pl.ANY)


def call(kernel, name, out_shape, in_specs, scratch=(), out_specs=None, mib=24, aliases=None):
    return pl.pallas_call(
        kernel,
        name=name,
        out_shape=out_shape,
        in_specs=in_specs,
        out_specs=out_specs or jax.tree.map(lambda _: VMEM, out_shape),
        scratch_shapes=list(scratch),
        input_output_aliases=aliases or {},
        cost_estimate=pl.CostEstimate(flops=0, bytes_accessed=1 << 20, transcendentals=0),
        compiler_params=pltpu.CompilerParams(vmem_limit_bytes=mib * 1024 * 1024),
    )


def stay(array):
    return pltpu.with_memory_space_constraint(array, pltpu.HBM)


def in_hbm(shape):
    return pltpu.HBM(shape.shape, shape.dtype)


def local_index():
    return lax.rem(lax.axis_index("tiles"), GROUP)


def group_index():
    return lax.div(lax.axis_index("tiles"), GROUP)


def put(buffer, slot, count, real, imag):
    piece = real.shape[0] // GROUP
    for j in range(GROUP):
        at = slice(j * piece, (j + 1) * piece)
        first = 2 * j * piece * count + slot
        buffer[pl.ds(first, piece, stride=count), :] = real[at]
        buffer[pl.ds(first + piece * count, piece, stride=count), :] = imag[at]


def transposed_dot(left, right):
    return lax.dot_general(left, right, (((0,), (0,)), ((), ())), preferred_element_type=F32)


def member_rows(k, count):
    return pl.ds(pl.multiple_of((local_index() ^ k) * count, count), count)


def parts_kernel(data_hbm, wavelet_hbm, panel_hbm, tiles_hbm, rows_hbm, freqs_hbm, *refs):
    source_hbm, own_hbm, freqs_out, outs = *refs[:3], refs[3 : 3 + GROUP]
    data, wavelet, panel, tiles, rows, freqs, sems, wide, own, source = refs[3 + GROUP :]
    freq_count, _, block, shots = data.shape
    slots = tiles.shape[0]
    size = 2 * block // GROUP * slots
    half = lax.axis_size("tiles") * freq_count // 2
    pairs = (
        (data_hbm, data),
        (tiles_hbm, tiles),
        (wavelet_hbm, wavelet),
        (panel_hbm, panel),
        (freqs_hbm, freqs),
        (rows_hbm, rows),
    )
    copies = [pltpu.make_async_copy(*pair, sems.at[i]) for i, pair in enumerate(pairs)]
    for copy in copies:
        copy.start()
    diagonal = (
        lax.broadcasted_iota(jnp.int32, (block, shots), 0)
        == lax.broadcasted_iota(jnp.int32, (block, shots), 1)
    ).astype(F32)
    for i in (2, 3, 4, 5, 0):
        copies[i].wait()
    identity = diagonal * (lax.axis_index("tiles") == panel[0]).astype(F32)
    for f in range(freq_count):
        source[f, 0] = (wavelet[0, f] * identity - data[f, 0].astype(F32)).astype(BF16)
        source[f, 1] = (wavelet[1, f] * identity - data[f, 1].astype(F32)).astype(BF16)
    piece = block // GROUP
    mine = pl.ds(pl.multiple_of(local_index() * piece, piece), piece)
    for f in range(freq_count):
        for x in range(2):
            at = pl.ds(x * piece * freq_count + f, piece, stride=freq_count)
            wide[at, :] = data[f, x, mine, :].astype(F32)
    own[...] = wide[: own.shape[0]].astype(BF16)
    stores = [
        pltpu.make_async_copy(own, own_hbm, sems.at[6]),
        pltpu.make_async_copy(source, source_hbm, sems.at[7]),
    ]
    for store in stores:
        store.start()
    line = lax.broadcasted_iota(jnp.int32, (slots, shots), 0)
    targets = jnp.zeros((slots, shots), jnp.int32)
    for t in range(slots):
        freqs_out[t] = freqs[t]
        targets = jnp.where(line == t, rows[t] * freq_count + freqs[t] - half, targets)
    for k in range(GROUP):
        outs[k][size:] = targets.astype(F32).astype(BF16)
    copies[1].wait()

    def one(t, carry):
        f = freqs[t]
        left = tiles[t].reshape(2 * block, block)
        right = jnp.concatenate([source[f, 0], source[f, 1]], axis=1)
        product = jnp.dot(left, right, preferred_element_type=F32)
        real = product[:block, :shots] - product[block:, shots:]
        put(wide, t, slots, real, product[:block, shots:] + product[block:, :shots])
        return carry

    lax.fori_loop(0, slots, one, 0, unroll=16)
    for k in range(GROUP):
        outs[k][:size] = wide[member_rows(k, size)].astype(BF16)
    for store in stores:
        store.wait()


def sums_kernel(sizes, *refs):
    slots, groups, span, cap = sizes
    parts, (hot_out, own, *sends) = refs[:GROUP], refs[GROUP:]
    height, _, shots = own.shape
    count = GROUP * slots
    group = group_index()
    targets = jnp.concatenate([part[height * slots :] for part in parts], axis=0).astype(F32)
    lane = lax.broadcasted_iota(jnp.int32, (count, shots), 1)
    hot = []
    for q in range(0, groups, shots // span):
        here = jnp.zeros((count, shots), jnp.int32)
        for i in range(shots // span):
            inside = lane - i * span + (group ^ (q + i)) * span - groups * span // 2
            here = jnp.where(lane >= i * span, inside, here)
        hot.append((targets == here.astype(F32)).astype(F32).astype(BF16))
    if groups == 2:
        other = hot[0][:, span:]
        used = (transposed_dot(other, jnp.ones((count, shots), BF16)) > 0).astype(F32)
        before = (
            lax.broadcasted_iota(jnp.int32, (span, span), 0)
            > lax.broadcasted_iota(jnp.int32, (span, span), 1)
        ).astype(F32)
        rank = jnp.dot(before.astype(BF16), used.astype(BF16), preferred_element_type=F32)
        slot = lax.broadcasted_iota(jnp.int32, (span, shots), 1).astype(F32)
        chosen = jnp.where(rank == slot, used, 0.0)
        number = jnp.sum(used, axis=0, keepdims=True)
        target = lax.broadcasted_iota(jnp.int32, (span, shots), 0).astype(F32) + 1.0
        listed = jnp.sum(chosen * target, axis=0, keepdims=True)
        listed = jnp.where(slot[:TABLE] < span, listed, number)
        sends[0][height * cap :] = listed.astype(BF16)
        moved = jnp.dot(other, chosen[:, :span].astype(BF16), preferred_element_type=F32)
        hot = [jnp.concatenate([hot[0][:, :span], moved.astype(BF16)], axis=1)]
    hot = jnp.concatenate(hot, axis=1) if len(hot) > 1 else hot[0]
    hot_out[...] = hot
    step = 4
    for r in range(0, height, step):
        rows = [
            jnp.concatenate([part[(r + i) * slots : (r + i + 1) * slots] for part in parts], axis=0)
            for i in range(step)
        ]
        total = transposed_dot(hot, jnp.concatenate(rows, axis=1))
        for i in range(step):
            values = total[:, i * shots : (i + 1) * shots]
            own[r + i] = values[:span]
            if groups == 2:
                at = slice((r + i) * cap, (r + i + 1) * cap)
                sends[0][at] = values[span : span + cap].astype(BF16)
                sends[1][r + i] = values[span + cap :].astype(BF16)
            else:
                for q, send in enumerate(sends, 1):
                    send[r + i] = values[q * span : (q + 1) * span].astype(BF16)


def hand_out(outs, rows):
    size = outs[0].shape[0]
    outs[0][...] = rows(0)
    outs[1][...] = rows(1)
    for out, k in zip(outs[2:], CHIPS):
        out[:size] = rows(k)
        out[size:] = rows(k ^ 1)


def collect(refs, rows):
    own, *got, mate = refs
    size = own.shape[0]
    rows(0, own[...])
    rows(1, mate[:size])
    for i, k in enumerate(CHIPS):
        rows(k, got[i][:size])
        rows(k ^ 1, mate[(i + 1) * size : (i + 2) * size])


def relay_kernel(own, *refs):
    got, out = refs[:-1], refs[-1]
    size = own.shape[0]
    out[:size] = own[...]
    for i, ref in enumerate(got, 1):
        out[i * size : (i + 1) * size] = ref[size:]


def most_kernel(got, mine, *refs):
    out = refs[-1]
    last = slice(got.shape[0] - TABLE, got.shape[0])
    half = got.shape[1] // 2
    most = jnp.maximum(got[last, half:].astype(F32), mine[last, half:].astype(F32))
    out[0] = jnp.max(most).astype(jnp.int32)


def slices_kernel(data, _, *refs):
    *refs, wide, sems = refs
    count = (len(refs) - 1 - len(CHIPS)) // 2
    waiting, stored, outs = refs[:count], refs[count : 2 * count], refs[2 * count :]
    copies = [
        pltpu.make_async_copy(src, dst, sems.at[i])
        for i, (src, dst) in enumerate(zip(waiting, stored))
    ]
    for copy in copies:
        copy.start()
    freq_count = data.shape[0]
    for f in range(freq_count):
        put(wide, f, freq_count, data[f, 0].astype(F32), data[f, 1].astype(F32))
    size = outs[0].shape[0]
    outs[0][...] = wide[member_rows(1, size)].astype(BF16)
    for out, k in zip(outs[1:], CHIPS):
        out[:size] = wide[member_rows(k, size)].astype(BF16)
        out[size:] = wide[member_rows(k ^ 1, size)].astype(BF16)
    for copy in copies:
        copy.wait()


def fetch_rest(full, got_rest_any, got_rest, sem):
    @pl.when(full)
    def _():
        copy = pltpu.make_async_copy(got_rest_any, got_rest, sem)
        copy.start()
        copy.wait()

    @pl.when(jnp.logical_not(full))
    def _():
        got_rest[...] = jnp.zeros_like(got_rest)


def residual_kernel(sizes, own, *refs):
    slots, groups, span, cap = sizes
    height, _, shots = own.shape
    data_in, refs = refs[: 2 + len(CHIPS)], refs[2 + len(CHIPS) :]
    if groups == 2:
        most, got, got_rest_any, rounded, send_hbm, rest_hbm, *outs = refs[:-7]
        data, back, total, sems, got_rest, rest, send = refs[-7:]
        target = lax.broadcasted_iota(jnp.int32, (span, span), 0).astype(F32) + 1.0
        listed = got[height * cap :, :span].astype(F32)[:1]
        chosen = (listed == target).astype(F32).astype(BF16)
        full = most[0] > cap
    else:
        got, (rounded, *outs, data, back, total, sems) = refs[: groups - 1], refs[groups - 1 :]
    local = local_index()
    freq_count = data.shape[1] // height
    own_copy = pltpu.make_async_copy(data_in[0], data.at[local], sems.at[0])
    own_copy.start()
    if groups == 2:

        fetch_rest(full, got_rest_any, got_rest, sems.at[1])
    *got_data, mate = data_in[1:]
    size = mate.shape[0] // 4
    data[local ^ 1] = mate[:size]
    for i, k in enumerate(CHIPS):
        data[local ^ k] = got_data[i][:size]
        data[local ^ k ^ 1] = mate[(i + 1) * size : (i + 2) * size]
    step = 8
    for r in range(0, height, step):
        rows = range(r, r + step)
        values = jnp.concatenate([own[i] for i in rows], axis=1)
        if groups == 2:
            more = []
            for i in rows:
                used = got[i * cap : (i + 1) * cap]
                more.append(jnp.concatenate([used, got_rest[i]], axis=0))
            more = jnp.concatenate(more, axis=1)
            values += jnp.dot(chosen, more, preferred_element_type=F32)
        else:
            for ref in got:
                values += jnp.concatenate([ref[i].astype(F32) for i in rows], axis=1)
        total[:, r * shots : (r + step) * shots] = values
        for j in range(GROUP):
            at = slice(j * freq_count, (j + 1) * freq_count)
            pair = [values[at, i * shots : (i + 1) * shots] for i in range(step)]
            pair = jnp.concatenate(pair, axis=0)
            back[j, r * freq_count : (r + step) * freq_count] = pair.astype(BF16)
    own_copy.wait()
    copies = []
    for r in range(0, height, step):
        rows = range(r, r + step)
        values = data[:, r * freq_count : (r + step) * freq_count].astype(F32)
        values = [
            values[:, i * freq_count : (i + 1) * freq_count].reshape(span, shots)
            for i in range(step)
        ]
        values = jnp.concatenate(values, axis=1) - total[:, r * shots : (r + step) * shots]
        values = values.astype(BF16)
        picked = transposed_dot(chosen, values).astype(BF16) if groups == 2 else None
        for i in rows:
            at = slice((i - r) * shots, (i - r + 1) * shots)
            rounded[i] = values[:, at]
            if groups == 2:
                send[i * cap : (i + 1) * cap] = picked[:cap, at]
                rest[i] = picked[cap:, at]
        if groups == 2:
            at = pl.ds(r * cap, step * cap)
            sem = sems.at[2 + r // step]
            copies.append(pltpu.make_async_copy(send.at[at], send_hbm.at[at], sem))
            copies[-1].start()
    if groups == 2:

        @pl.when(full)
        def _():
            copy = pltpu.make_async_copy(rest, rest_hbm, sems.at[1])
            copy.start()
            copy.wait()

    hand_out(outs, lambda k: back[local ^ k])
    for copy in copies:
        copy.wait()


def spread_kernel(sizes, hot, rounded, *refs):
    slots, groups, span, cap = sizes
    height, _, shots = rounded.shape
    if groups == 2:
        most, got, got_rest_any, *outs, got_rest, sem = refs
        fetch_rest(most[0] > cap, got_rest_any, got_rest, sem)
    else:
        got, outs = refs[: groups - 1], refs[groups - 1 :]
    step = 8
    for r in range(0, height, step):
        rows = []
        for i in range(r, r + step):
            if groups == 2:
                row = [rounded[i], got[i * cap : (i + 1) * cap], got_rest[i]]
            else:
                row = [rounded[i]] + [ref[i] for ref in got]
            rows.append(jnp.concatenate(row, axis=0))
        picked = jnp.dot(hot[...], jnp.concatenate(rows, axis=1), preferred_element_type=F32)
        picked = picked.astype(BF16)
        for i in range(step):
            for k in range(GROUP):
                outs[k][(r + i) * slots : (r + i + 1) * slots] = picked[
                    k * slots : (k + 1) * slots, i * shots : (i + 1) * shots
                ]


def residual_out_kernel(data, *refs):
    back, (residual, wide) = refs[:-2], refs[-2:]
    freq_count, _, block, _ = data.shape
    size = back[0].shape[0]
    piece = block // GROUP

    def keep(k, rows):
        wide[member_rows(k, size)] = rows.astype(F32)

    collect(back, keep)
    for f in range(freq_count):
        real, imag = data[f, 0].astype(F32), data[f, 1].astype(F32)
        for j in range(GROUP):
            at = slice(j * piece, (j + 1) * piece)
            first = j * size + f
            rows = pl.ds(first, piece, stride=freq_count)
            residual[f, 0, at, :] = real[at] - wide[rows, :]
            rows = pl.ds(first + piece * freq_count, piece, stride=freq_count)
            residual[f, 1, at, :] = imag[at] - wide[rows, :]


def gradient_kernel(members, source, freqs, *refs):
    parts, (gradient_hbm, gradient, wide, sems) = refs[: len(members)], refs[-4:]
    slots, _, _, block = gradient.shape
    size, shots = parts[0].shape
    height = size // slots
    piece = height // 2
    scale = 1.0 / shots
    local = local_index()
    for i, part in enumerate(parts):
        wide[i * size : (i + 1) * size] = part[...].astype(F32)

    def one(t, carry):
        left = wide[pl.ds(t, len(members) * height, stride=slots), :].astype(BF16)
        right = source[freqs[t]].reshape(2 * block, shots)
        total = -scale * lax.dot_general(
            left, right, (((1,), (1,)), ((), ())), preferred_element_type=F32
        )
        real, imag = [], []
        for i in range(len(members)):
            upper = total[i * height : i * height + piece]
            lower = total[i * height + piece : (i + 1) * height]
            real.append(upper[:, :block] + lower[:, block:])
            imag.append(lower[:, :block] - upper[:, block:])
        gradient[t, 0] = jnp.concatenate(real, axis=0).astype(BF16)
        gradient[t, 1] = jnp.concatenate(imag, axis=0).astype(BF16)
        return carry

    copies = []
    quarters = 4
    step = slots // quarters
    for quarter in range(quarters):
        lax.fori_loop(quarter * step, (quarter + 1) * step, one, 0, unroll=4)
        at = pl.ds(quarter * step, step)
        for i, k in enumerate(members):
            rows = pl.ds(pl.multiple_of((local ^ k) * piece, piece), piece)
            copies.append(
                pltpu.make_async_copy(
                    gradient.at[at, :, pl.ds(i * piece, piece), :],
                    gradient_hbm.at[at, :, rows, :],
                    sems.at[quarter * len(members) + i],
                )
            )
            copies[-1].start()
    for copy in copies:
        copy.wait()


def per_device(data, wavelet, panel_block, tiles, cover_rows, cover_freqs):
    freq_count, _, block, shots = data.shape
    slots = tiles.shape[0]
    peers = lax.axis_size("tiles")
    groups = peers // GROUP
    height = 2 * block // GROUP
    span = GROUP * freq_count
    cap = 3 * span // 4 if groups == 2 else span
    sizes = (slots, groups, span, cap)

    def shape(*dims, kind=BF16):
        return jax.ShapeDtypeStruct((*dims, shots), kind)

    wide = pltpu.VMEM(((GROUP * height + 1) * slots, shots), F32)
    wide_data = pltpu.VMEM(((GROUP * height + 1) * freq_count, shots), F32)
    to_members = [jax.ShapeDtypeStruct((height * slots, shots), BF16)] * GROUP
    size = height * freq_count
    to_owners = [shape(size)] * 2 + [shape(2 * size)] * len(CHIPS)
    members = pltpu.VMEM((GROUP, height * freq_count, shots), BF16)

    def swap(value, distance):
        return lax.ppermute(value, "tiles", [(i, i ^ distance) for i in range(peers)])

    def in_group(values):
        got = {k: swap(values[k], k) for k in (6, 4, 2, 7, 5, 3, 1)}
        return [values[0]] + [got[k] for k in range(1, GROUP)]

    def hand_around(values):
        got = [swap(value, k) for value, k in zip(values[2:], CHIPS)]
        mate = call(relay_kernel, "for_mate", shape(4 * size), [VMEM] * (1 + len(CHIPS)))(
            values[1], *got
        )
        return [values[0], *got, swap(mate, 1)]

    def across(values):
        return [swap(value, q * GROUP) for q, value in enumerate(values, 1)]

    source, own_data, freqs, *sent = call(
        parts_kernel,
        "parts",
        [in_hbm(shape(freq_count, 2, block)), in_hbm(shape(size)), pltpu.SMEM((slots,), jnp.int32)]
        + [shape(height * slots + slots)] * GROUP,
        [HBM] * 6,
        out_specs=[HBM, HBM, SMEM] + [VMEM] * GROUP,
        scratch=[
            pltpu.VMEM(data.shape, BF16),
            pltpu.SMEM((2, freq_count), F32),
            pltpu.SMEM((1,), jnp.int32),
            pltpu.VMEM(tiles.shape, BF16),
            pltpu.SMEM((slots,), jnp.int32),
            pltpu.SMEM((slots,), jnp.int32),
            pltpu.SemaphoreType.DMA((8,)),
            wide,
            pltpu.VMEM((size, shots), BF16),
            pltpu.VMEM(data.shape, BF16),
        ],
    )(stay(data), stay(wavelet.T), panel_block, *map(stay, (tiles, cover_rows, cover_freqs)))
    rests = [in_hbm(shape(height, span - cap))] if groups == 2 else []
    rest_rows = [pltpu.VMEM((height, span - cap, shots), BF16)] * len(rests)
    if groups == 2:
        sends = [shape(height * cap + TABLE)]
    else:
        sends = [shape(height, span)] * (groups - 1)
    hot, own, *out = call(
        functools.partial(sums_kernel, sizes),
        "sums",
        [
            jax.ShapeDtypeStruct((GROUP * slots, groups * span), BF16),
            shape(height, span, kind=F32),
        ]
        + sends
        + [shape(height, span - cap)] * len(rests),
        [VMEM] * GROUP,
    )(*in_group(sent))
    got = [swap(out[0], GROUP)] if groups == 2 else across(out)
    waiting = [hot, *out[1:]] if groups == 2 else [hot]
    stored = call(
        slices_kernel,
        "data_slices",
        [in_hbm(x) for x in waiting] + to_owners[1:],
        [VMEM, ANY] + [VMEM] * len(waiting),
        out_specs=[HBM] * len(waiting) + [VMEM] * (len(to_owners) - 1),
        scratch=[wide_data, pltpu.SemaphoreType.DMA((2,))],
    )(data, own, *waiting)
    hot = stored[0]
    data_in = hand_around([own_data, *stored[len(waiting) :]])
    if groups == 2:
        most = call(
            most_kernel,
            "most",
            pltpu.SMEM((1,), jnp.int32),
            [VMEM] * 2 + [ANY] * (len(data_in) - 1),
            out_specs=SMEM,
        )(got[0], out[0], *data_in[1:])
        full = most[0] > cap

        def rest(value):
            return lax.cond(full, lambda v: swap(v, GROUP), jnp.zeros_like, value)

        got = [most, *got, rest(stored[1])]
    rounded, *out = call(
        functools.partial(residual_kernel, sizes),
        "residual_slices",
        [shape(height, span)]
        + [in_hbm(shape(height * cap))] * len(rests)
        + rests
        + to_owners,
        [VMEM, HBM]
        + [VMEM] * (len(data_in) - 1)
        + ([SMEM, VMEM, ANY] if groups == 2 else [VMEM] * len(got)),
        out_specs=[VMEM] + [HBM] * (2 * len(rests)) + [VMEM] * len(to_owners),
        scratch=[
            members,
            members,
            pltpu.VMEM((span, height * shots), F32),
            pltpu.SemaphoreType.DMA((2 + height // 8,)),
        ]
        + rest_rows * 2
        + [pltpu.VMEM((height * cap, shots), BF16)] * len(rests),
    )(own, stay(data_in[0]), *data_in[1:], *got)
    if groups == 2:
        got = [most, swap(out[0], GROUP), rest(out[1])]
    else:
        got = across([rounded] * (groups - 1))
    residual = call(
        residual_out_kernel,
        "residual",
        jax.ShapeDtypeStruct(data.shape, F32),
        [VMEM] * (1 + len(to_owners)),
        scratch=[wide_data],
    )(data, *hand_around(out[-len(to_owners) :]))
    out = call(
        functools.partial(spread_kernel, sizes),
        "spread",
        to_members,
        [VMEM] * 2 + ([SMEM, VMEM, ANY] if groups == 2 else [VMEM] * len(got)),
        scratch=rest_rows + [pltpu.SemaphoreType.DMA] * len(rests),
    )(hot, rounded, *got)
    got = in_group(out)
    gradient = []
    for members in (range(GROUP - 2), range(GROUP - 2, GROUP - 1), range(GROUP - 1, GROUP)):
        rows = len(members) * block // GROUP
        gradient = [
            call(
                functools.partial(gradient_kernel, members),
                "gradient",
                in_hbm(tiles),
                [VMEM, SMEM] + [VMEM] * len(members) + [ANY] * len(gradient),
                out_specs=HBM,
                scratch=[
                    pltpu.VMEM((slots, 2, rows, block), BF16),
                    pltpu.VMEM(((len(members) * height + 1) * slots, shots), F32),
                    pltpu.SemaphoreType.DMA((4 * len(members),)),
                ],
                aliases={2 + len(members): 0} if gradient else None,
            )(source, freqs, *[got[k] for k in members], *gradient)
        ]
    gradient = gradient[0]
    return residual, gradient


def solution(mesh):
    in_specs = (
        P("windows", None, "tiles", None),
        P(),
        P(),
        P(("windows", "tiles"), None, None, None),
        P(("windows", "tiles")),
        P(("windows", "tiles")),
    )
    out_specs = (P("windows", None, "tiles", None), P(("windows", "tiles"), None, None, None))
    return jax.shard_map(
        per_device, mesh=mesh, in_specs=in_specs, out_specs=out_specs, check_vma=False
    )
```
